32 devices in a mesh: dp: 8 (over z, core), mp: 4 (over y, x).
Axes of the slice: x: 2, y: 2, z: 4, core: 2. Of those that a mesh axis runs over, the one named last changes fastest.
Arguments:
- tokens: bfloat16 [37632, 512], P(('dp', 'mp')), may hold values from -6 to 6
- cotangent: bfloat16 [37632, 512], P(('dp', 'mp')), may hold values from -6 to 6
- w_in: float32 [512, 2, 1536], P(None, None, 'mp'), may hold values from -0.31819805 to 0.31819805
- w_out: float32 [1536, 512], P('mp'), may hold values from -0.15625 to 0.15625
- spatial: float32 [196, 196], replicated, may hold values from -0.4375 to 0.4375
- model_vectors: float32 [3, 512], replicated, may hold values from 0.1 to 1.9
- gate_vectors: float32 [4, 1536], P(None, 'mp'), may hold values from 0.1 to 1.9
- patch_bias: float32 [196], replicated, may hold values from -3 to 3
- moment_in: float32 [512, 2, 1536], P(None, None, 'mp'), may hold values from -448 to 448
- moment_out: float32 [1536, 512], P('mp'), may hold values from -640 to 640
- moment_mix: float32 [196, 196], replicated, may hold values from -1024 to 1024
- first_model: float32 [3, 512], replicated, may hold values from -112 to 112
- second_model: float32 [3, 512], replicated, may hold values from 1881.6 to 7526.4
- first_gate: float32 [4, 1536], P(None, 'mp'), may hold values from -48 to 48
- second_gate: float32 [4, 1536], P(None, 'mp'), may hold values from 301.056 to 1204.224
- first_patch: float32 [196], replicated, may hold values from -112 to 112
- second_patch: float32 [196], replicated, may hold values from 1769.472 to 7372.8
Outputs:
- output: bfloat16 [37632, 512], P(('dp', 'mp'))
- grad_tokens: bfloat16 [37632, 512], P(('dp', 'mp'))
- grad_w_in: float32 [512, 2, 1536], P(None, None, 'mp')
- grad_w_out: float32 [1536, 512], P('mp')
- grad_spatial: float32 [196, 196], replicated
- grad_model: float32 [3, 512], replicated
- grad_gate: float32 [4, 1536], P(None, 'mp')
- grad_patch: float32 [196], replicated
- new_moment_in: float32 [512, 2, 1536], P(None, None, 'mp')
- new_moment_out: float32 [1536, 512], P('mp')
- new_moment_mix: float32 [196, 196], replicated
- new_second_model: float32 [3, 512], replicated
- new_second_gate: float32 [4, 1536], P(None, 'mp')
- new_second_patch: float32 [196], replicated
- new_w_in: float32 [512, 2, 1536], P(None, None, 'mp')
- new_w_out: float32 [1536, 512], P('mp')
- new_spatial: float32 [196, 196], replicated
- new_model: float32 [3, 512], replicated
- new_gate: float32 [4, 1536], P(None, 'mp')
- new_patch: float32 [196], replicated
The draws below stay inside these ranges and needn't reach their ends.
All inputs are finite; a program needn't handle non-finite values.
Results may differ from the reference program's by a relative error of at most 0.0096.
The reference program's roundings to bfloat16 on the way count: a program that leaves them out, or rounds other values in their place, can miss the bound.
Values may be sent and summed in bfloat16 or wider, within the bound.
No kernel may reach another device: no remote copies, remote signals or barrier semaphores. Data moves between devices by JAX's collectives and lax.ppermute only.
A program may use at most 256 MiB of HBM per device.

```python
import math
import jax
import jax.numpy as jnp
from jax import lax

D = 512
G = 1536
P_SIZE = 196
STEP = 10
IMAGES = 192
TOKENS = 37632


def draw_w_in(key, part):
    key = jax.random.fold_in(key, 7)
    column_ramp = jnp.arange(G, dtype=jnp.float32) / max(G - 1, 1)
    entries = jnp.clip(jax.random.normal(key, (D, 2, G), jnp.float32), -4.0, 4.0)
    growth = 0.6 * 3.0 ** column_ramp
    return entries * growth / math.sqrt(D)


def block_levels(stream_key, dims, shards, low, largest):
    def one(dim, parts):
        steps = jax.random.uniform(jax.random.fold_in(jax.random.fold_in(stream_key, 6), dim), (parts,), jnp.float32, low / len(shards), largest / len(shards))
        return jnp.repeat(jnp.exp(steps), dims[dim] // parts).reshape((-1,) + (1,) * (len(dims) - dim - 1))

    factor_of = one(*shards[0])
    for cut in shards[1:]:
        factor_of = factor_of * one(*cut)
    return factor_of


def gaussian(rng, shape, deviation, bound, pieces=(), kind=jnp.bfloat16):
    level = block_levels(rng, shape, pieces, -0.22, 0.18) if pieces else 1.0
    array = jax.random.normal(rng, shape, jnp.float32) * deviation * level
    return jnp.minimum(jnp.maximum(array, -bound), bound).astype(kind)


def setup_inputs(seed: int = 0) -> dict:
    key_list = jax.random.split(jax.random.key(seed), 18)
    return {
        "tokens": gaussian(key_list[0], (TOKENS, D), 1.0, 6.0, ((0, 32),)),
        "cotangent": gaussian(key_list[1], (TOKENS, D), 1.0, 6.0, ((0, 32),)),
        "w_in": draw_w_in(jax.random.fold_in(key_list[17], 71), 0),
        "w_out": gaussian(key_list[3], (G, D), G ** -0.5, 0.15625, ((0, 4),), jnp.float32),
        "spatial": gaussian(key_list[4], (P_SIZE, P_SIZE), P_SIZE ** -0.5, 0.4375, (), jnp.float32),
        "model_vectors": jnp.clip(1.0 + 0.18 * jax.random.normal(key_list[5], (3, D), jnp.float32), 0.1, 1.9),
        "gate_vectors": jnp.clip(1.0 + 0.18 * jax.random.normal(key_list[6], (4, G), jnp.float32), 0.1, 1.9),
        "patch_bias": gaussian(key_list[7], (P_SIZE,), 0.5, 3.0, (), jnp.float32),
        "moment_in": gaussian(key_list[8], (D, 2, G), (0.4 * TOKENS ** 0.5), 448.0, ((2, 4),), jnp.float32),
        "moment_out": gaussian(key_list[9], (G, D), (0.6 * TOKENS ** 0.5), 640.0, ((0, 4),), jnp.float32),
        "moment_mix": gaussian(key_list[10], (P_SIZE, P_SIZE), (0.35 * (IMAGES * G) ** 0.5), 1024.0, (), jnp.float32),
        "first_model": gaussian(key_list[11], (3, D), (0.1 * TOKENS ** 0.5), 112.0, (), jnp.float32),
        "second_model": jnp.clip(jnp.exp(jax.random.uniform(key_list[12], (3, D), jnp.float32, math.log(1881.6), math.log(7526.4))), 1881.6, 7526.4),
        "first_gate": gaussian(key_list[13], (4, G), (0.04 * TOKENS ** 0.5), 48.0, ((1, 4),), jnp.float32),
        "second_gate": jnp.clip(jnp.exp(math.log(1204.224) - 1.3862944 * jax.random.uniform(key_list[14], (4, G), jnp.float32) ** block_levels(key_list[14], (4, G), ((1, 4),), -0.2, 0.2)), 301.056, 1204.224),
        "first_patch": gaussian(key_list[15], (P_SIZE,), (0.035 * (IMAGES * G) ** 0.5), 112.0, (), jnp.float32),
        "second_patch": jnp.clip(jnp.exp(jax.random.uniform(key_list[16], (P_SIZE,), jnp.float32, math.log(1769.472), math.log(7372.8))), 1769.472, 7372.8),
    }


@jax.custom_vjp
def low(v):
    return lax.optimization_barrier(v.astype(jnp.bfloat16)).astype(jnp.float32)

@jax.custom_vjp
def low_back(v):
    return v

def low_keep(v):
    return (low(v), None)

def low_pass(kept, grad):
    return (grad,)

def back_keep(v):
    return (v, None)

def back_low(kept, grad):
    return (low(grad),)
low.defvjp(low_keep, low_pass)
low_back.defvjp(back_keep, back_low)
EPSILON = 1e-05
HIGHEST = lax.Precision.HIGHEST
COEF_FIRST = 3.4445
COEF_SECOND = -4.775
COEF_THIRD = 2.0315
MOMENTUM = 0.95
MUON_RATE = 0.2
ADAM_RATE = 0.3
DECAY_RATE = 0.01
BETA_FIRST = 0.9
BETA_SECOND = 0.95

def row_norm(rows, gain, shift):
    row_mean = lax.optimization_barrier(jnp.mean(rows, axis=-1, keepdims=True))
    centred = rows - row_mean
    row_var = lax.optimization_barrier(jnp.mean(centred * centred, axis=-1, keepdims=True))
    return centred * lax.rsqrt(row_var + EPSILON) * gain + shift

def forward(rows_in, w_in, w_out, spatial, model_vectors, gate_vectors, patch_bias):
    normed = low(row_norm(rows_in, model_vectors[0], model_vectors[1]))
    weight_cat = low(w_in).reshape(D, 2 * G)
    hidden = low_back(jnp.dot(normed, weight_cat, precision=HIGHEST) + gate_vectors[0:2].reshape(2 * G))
    activated = jax.nn.gelu(hidden)
    value_half = activated[:, :G]
    gate_half = activated[:, G:]
    gate_normed = low(row_norm(gate_half, gate_vectors[2], gate_vectors[3]))
    images = gate_normed.reshape(-1, P_SIZE, G)
    mixed_rows = jnp.einsum('pq,bqc->bpc', low(spatial), images, precision=HIGHEST) + patch_bias[None, :, None]
    mixed_rows = low_back(mixed_rows.reshape(-1, G))
    gated_vals = low(value_half * mixed_rows)
    return rows_in + jnp.dot(gated_vals, low(w_out), precision=HIGHEST) + model_vectors[2]

def newton_step(ortho, gram):
    polynomial = COEF_SECOND * gram + COEF_THIRD * jnp.dot(gram, gram, precision=HIGHEST)
    return COEF_FIRST * ortho + jnp.dot(polynomial, ortho, precision=HIGHEST)

def orthogonal(moment):
    ortho = moment / (jnp.sqrt(jnp.sum(moment * moment)) + 1e-07)
    for sweep in range(5):
        ortho = newton_step(ortho, jnp.dot(ortho, ortho.T, precision=HIGHEST))
    return ortho

def adam_update(param_now, grad_now, first_old, second_old):
    first_new = BETA_FIRST * first_old + (1.0 - BETA_FIRST) * grad_now
    second_new = BETA_SECOND * second_old + (1.0 - BETA_SECOND) * grad_now * grad_now
    first_hat = first_new / (1.0 - BETA_FIRST ** STEP)
    second_hat = second_new / (1.0 - BETA_SECOND ** STEP)
    updated = param_now * (1.0 - ADAM_RATE * DECAY_RATE) - ADAM_RATE * first_hat / (jnp.sqrt(second_hat) + 1e-08)
    return (second_new, updated)

def reference(tokens, cotangent, w_in, w_out, spatial, model_vectors, gate_vectors, patch_bias, moment_in, moment_out, moment_mix, first_model, second_model, first_gate, second_gate, first_patch, second_patch):
    params = (w_in, w_out, spatial, model_vectors, gate_vectors, patch_bias)
    pair_count = tokens.shape[0] // (2 * P_SIZE)
    inputs = tokens.astype(jnp.float32).reshape(pair_count, 2 * P_SIZE, D)
    cotans = cotangent.astype(jnp.float32).reshape(pair_count, 2 * P_SIZE, D)

    def one_pair(totals, token_pair):
        rows_in, rows_cot = token_pair
        result, pull_back = jax.vjp(forward, rows_in, *params)
        gradients = pull_back(rows_cot)
        totals = tuple((total + grad_now for total, grad_now in zip(totals, gradients[1:])))
        return (totals, (result.astype(jnp.bfloat16), gradients[0].astype(jnp.bfloat16)))
    zero_sums = tuple((jnp.zeros(item.shape, jnp.float32) for item in params))
    gradients, (output, grad_tokens) = lax.scan(one_pair, zero_sums, (inputs, cotans))
    grad_w_in, grad_w_out, grad_spatial, grad_model, grad_gate, grad_patch = gradients
    output = output.reshape(-1, D)
    grad_tokens = grad_tokens.reshape(-1, D)
    new_moment_in = MOMENTUM * moment_in + grad_w_in
    new_moment_out = MOMENTUM * moment_out + grad_w_out
    new_moment_mix = MOMENTUM * moment_mix + grad_spatial
    shrink_by = 1.0 - MUON_RATE * DECAY_RATE
    ortho_in = orthogonal(new_moment_in.reshape(D, 2 * G)).reshape(D, 2, G)
    ortho_out = orthogonal(new_moment_out.T).T
    ortho_mix = orthogonal(new_moment_mix)
    new_w_in = w_in * shrink_by - MUON_RATE * 0.2 * math.sqrt(max(D, 2 * G)) * ortho_in
    new_w_out = w_out * shrink_by - MUON_RATE * 0.2 * math.sqrt(max(D, G)) * ortho_out
    new_spatial = spatial * shrink_by - MUON_RATE * 0.2 * math.sqrt(P_SIZE) * ortho_mix
    new_second_model, new_model = adam_update(model_vectors, grad_model, first_model, second_model)
    new_second_gate, new_gate = adam_update(gate_vectors, grad_gate, first_gate, second_gate)
    new_second_patch, new_patch = adam_update(patch_bias, grad_patch, first_patch, second_patch)
    return (output, grad_tokens, grad_w_in, grad_w_out, grad_spatial, grad_model, grad_gate, grad_patch, new_moment_in, new_moment_out, new_moment_mix, new_second_model, new_second_gate, new_second_patch, new_w_in, new_w_out, new_spatial, new_model, new_gate, new_patch)
```

```python
import functools
import math

import jax
import jax.numpy as jnp
from jax import lax
from jax.experimental import pallas as pl
from jax.experimental.pallas import tpu as pltpu
from jax.sharding import PartitionSpec as P

STEP = 10
EPSILON = 1e-05
HIGHEST = lax.Precision.HIGHEST
COEF_FIRST = 3.4445
COEF_SECOND = -4.775
COEF_THIRD = 2.0315
MOMENTUM = 0.95
MUON_RATE = 0.2
ADAM_RATE = 0.3
DECAY_RATE = 0.01
BETA_FIRST = 0.9
BETA_SECOND = 0.95
LOW = jnp.bfloat16
F32 = jnp.float32


ROW_TILE = 16
CUBIC = 0.044715
SLOPE = math.sqrt(2.0 / math.pi)


def compiler(megabytes):
    return pltpu.CompilerParams(vmem_limit_bytes=megabytes << 20)


def dot_nn(a, b):
    return jnp.dot(a, b, preferred_element_type=F32)


def dot_nt(a, b):
    return lax.dot_general(a, b, (((1,), (1,)), ((), ())), preferred_element_type=F32)


def gelu_pair(hidden):
    square = hidden * hidden
    half = 0.5 + 0.5 * jnp.tanh(hidden * (SLOPE + (SLOPE * CUBIC) * square))
    active = hidden * half
    slope = half + (active - active * half) * (2.0 * SLOPE + (6.0 * SLOPE * CUBIC) * square)
    return active, slope


def lanes(v):
    total = v[:, :128]
    for at in range(128, v.shape[1], 128):
        total = total + v[:, at : at + 128]
    return total


def eights(v):
    total = v[:8]
    for at in range(8, v.shape[0], 8):
        total = total + v[at : at + 8]
    return total


def tiles(count, body, carry=None):
    def step(i, kept):
        return body(pl.ds(pl.multiple_of(i * ROW_TILE, ROW_TILE), ROW_TILE), kept)

    return lax.fori_loop(0, count // ROW_TILE, step, carry, unroll=False)


def gate_kernel(chunk, normed, weight, vec, normal, unit, slope, scale, active):
    rows, full = active.shape
    starts = range(0, full, chunk)
    for at in starts:
        active[:, at : at + chunk] = dot_nn(normed[...], weight[:, at : at + chunk])

    def act(here, _):
        total = jnp.zeros((ROW_TILE, 128), F32)
        for at in starts:
            cols = slice(at, at + chunk)
            value, grad = gelu_pair(active[here, cols] + vec[1:2, cols])
            active[here, cols] = value
            slope[here, cols] = grad.astype(LOW)
            total = total + lanes(value)
        scale[here, :] = total

    tiles(rows, act)
    mean = jnp.sum(scale[...], axis=1, keepdims=True) * (1.0 / full)
    scale[...] = jnp.broadcast_to(mean, scale.shape)

    def spread(here, _):
        total = jnp.zeros((ROW_TILE, 128), F32)
        mean_here = scale[here, :][:, :1]
        for at in starts:
            cols = slice(at, at + chunk)
            centred = active[here, cols] - mean_here
            active[here, cols] = centred
            total = total + lanes(centred * centred)
        scale[here, :] = total

    tiles(rows, spread)
    var = jnp.sum(scale[...], axis=1, keepdims=True) * (1.0 / full)
    scale[...] = jnp.broadcast_to(lax.rsqrt(var + EPSILON), scale.shape)

    def finish(here, _):
        inv = scale[here, :][:, :1]
        for at in starts:
            cols = slice(at, at + chunk)
            unit_here = active[here, cols] * inv
            unit[here, cols] = unit_here.astype(LOW)
            normal[here, cols] = (unit_here * vec[2:3, cols] + vec[3:4, cols]).astype(LOW)

    tiles(rows, finish)


def gate_forward(normed, weight, vec, images, pad):
    width, full = weight.shape
    chunk = 512 if full % 512 == 0 else full
    total = images * pad
    whole = lambda shape: pl.BlockSpec(shape, lambda i: (0, 0))
    rows = lambda n: pl.BlockSpec((pad, n), lambda i: (i, 0))
    return pl.pallas_call(
        functools.partial(gate_kernel, chunk),
        grid=(images,),
        in_specs=[rows(width), whole((width, full)), whole(vec.shape)],
        out_specs=[rows(full), rows(full), rows(full), rows(128)],
        out_shape=[jax.ShapeDtypeStruct((total, full), LOW)] * 3
        + [jax.ShapeDtypeStruct((total, 128), F32)],
        scratch_shapes=[pltpu.VMEM((pad, full), F32)],
        compiler_params=compiler(48),
        cost_estimate=pl.CostEstimate(
            flops=2 * total * width * full, bytes_accessed=8 * total * full, transcendentals=total * full
        ),
        name="gate_forward",
    )(normed, weight, vec)


def value_kernel(
    pad,
    images,
    core,
    normed,
    cot,
    normed_t,
    cot_t,
    normal,
    unit,
    w_value,
    w_back,
    mix,
    mix_t,
    bias,
    vec,
    gated,
    low_value,
    grad_unit,
    mine_value,
    theirs_value,
    mine_out,
    theirs_out,
    sum_one,
    sum_two,
    grad_mix,
    grad_bias,
    columns,
    hidden,
    back,
    mixed,
    low_mixed,
    low_pad,
    gated_pad,
):
    total, chunk = hidden.shape
    half = mine_value.shape[0]
    step = pl.program_id(0)

    @pl.when(step == 0)
    def _():
        sum_one[...] = jnp.zeros_like(sum_one)
        sum_two[...] = jnp.zeros_like(sum_two)
        grad_mix[...] = jnp.zeros_like(grad_mix)
        grad_bias[...] = jnp.zeros_like(grad_bias)
        low_pad[total:, :] = jnp.zeros_like(low_pad[total:, :])
        gated_pad[total:, :] = jnp.zeros_like(gated_pad[total:, :])

    hidden[...] = dot_nn(normed[...], w_value[...])
    back[...] = dot_nn(cot[...], w_back[...])
    for image in range(images):
        here = slice(image * pad, (image + 1) * pad)
        mixed[here, :] = dot_nn(mix[...], normal[here, :])

    def forward(i, sums):
        here = pl.ds(pl.multiple_of(i * ROW_TILE, ROW_TILE), ROW_TILE)
        row = pl.ds(pl.multiple_of(lax.rem(i, pad // ROW_TILE) * ROW_TILE, ROW_TILE), ROW_TILE)
        value, slope = gelu_pair(hidden[here, :] + vec[0:1, :])
        mixed_here = mixed[here, :] + bias[row, :][:, :1]
        back_here = back[here, :]
        gated_here = (value * mixed_here).astype(LOW)
        gated[here, :] = gated_here
        gated_pad[here, :] = gated_here
        grad_here = (back_here * value).astype(LOW)
        low_mixed[here, :] = grad_here
        grad_bias[row, :] += lanes(grad_here.astype(F32))
        low_here = (back_here * mixed_here * slope).astype(LOW)
        low_value[here, :] = low_here
        low_pad[here, :] = low_here
        return sums + eights(low_here.astype(F32))

    bias_sum = lax.fori_loop(0, total // ROW_TILE, forward, jnp.zeros((8, chunk), F32))

    for image in range(images):
        here = slice(image * pad, (image + 1) * pad)
        mixed[here, :] = dot_nn(mix_t[...], low_mixed[here, :])
        grad_mix[...] += dot_nt(low_mixed[here, :], normal[here, :])

    first = pl.multiple_of(core[0] * half, half)
    other = pl.multiple_of((1 - core[0]) * half, half)
    mine_value[...] = dot_nn(normed_t[pl.ds(first, half), :], low_pad[...])
    theirs_value[...] = dot_nn(normed_t[pl.ds(other, half), :], low_pad[...]).astype(LOW)
    mine_out[...] = dot_nn(cot_t[pl.ds(first, half), :], gated_pad[...])
    theirs_out[...] = dot_nn(cot_t[pl.ds(other, half), :], gated_pad[...]).astype(LOW)

    def backward(i, sums):
        here = pl.ds(pl.multiple_of(i * ROW_TILE, ROW_TILE), ROW_TILE)
        grad = mixed[here, :]
        unit_here = unit[here, :].astype(F32)
        gain = vec[2:3, :]
        both = grad * unit_here
        du = grad * gain
        grad_unit[here, :] = du.astype(LOW)
        sum_one[here, :] += lanes(du)
        sum_two[here, :] += lanes(both * gain)
        return sums[0] + eights(both), sums[1] + eights(grad)

    zero = jnp.zeros((8, chunk), F32)
    gain_sum, shift_sum = lax.fori_loop(0, total // ROW_TILE, backward, (zero, zero))
    columns[0:8, :] = bias_sum
    columns[8:16, :] = gain_sum
    columns[16:24, :] = shift_sum


def value_both(core, normed, cot, normed_t, cot_t, normal, unit, w_value, w_back, mix, mix_t, bias, vec, images, pad):
    width, full = w_value.shape
    total = images * pad
    deep = normed_t.shape[1]
    chunk = 512 if full % 512 == 0 else full
    half = width // 2
    once = pl.Buffered(1)
    whole = lambda a: pl.BlockSpec(a.shape, lambda i, c: (0, 0), pipeline_mode=once)
    cols = lambda n: pl.BlockSpec((n, chunk), lambda i, c: (0, i))
    fixed = lambda *s: pl.BlockSpec(s, lambda i, c: (0, 0))
    shape = jax.ShapeDtypeStruct
    return pl.pallas_call(
        functools.partial(value_kernel, pad, images),
        grid_spec=pltpu.PrefetchScalarGridSpec(
            num_scalar_prefetch=1,
            grid=(full // chunk,),
            in_specs=[whole(normed), whole(cot), whole(normed_t), whole(cot_t)]
            + [cols(total), cols(total), cols(width), cols(width)]
            + [whole(mix), whole(mix_t), whole(bias), cols(4)],
            out_specs=[cols(total), cols(total), cols(total)]
            + [cols(half)] * 4
            + [fixed(total, 128), fixed(total, 128), fixed(pad, pad), fixed(pad, 128), cols(24)],
            scratch_shapes=[pltpu.VMEM((total, chunk), F32)] * 3
            + [pltpu.VMEM((total, chunk), LOW)]
            + [pltpu.VMEM((deep, chunk), LOW)] * 2,
        ),
        out_shape=[shape((total, full), LOW)] * 3
        + [shape((half, full), F32), shape((half, full), LOW)] * 2
        + [shape((total, 128), F32)] * 2
        + [shape((pad, pad), F32), shape((pad, 128), F32), shape((24, full), F32)],
        compiler_params=compiler(60),
        cost_estimate=pl.CostEstimate(
            flops=12 * total * width * full, bytes_accessed=20 * total * full, transcendentals=total * full
        ),
        name="value_both",
    )(core, normed, cot, normed_t, cot_t, normal, unit, w_value, w_back, mix, mix_t, bias, vec)


def gate_back_kernel(
    full, core, normed_t, grad_unit, unit, slope, scale, sum_one, sum_two, low_gate, mine, theirs, columns, means, low_pad
):
    total, chunk = low_gate.shape
    half = mine.shape[0]

    @pl.when(pl.program_id(0) == 0)
    def _():
        first = jnp.sum(sum_one[...], axis=1, keepdims=True) * (1.0 / full)
        means[0] = jnp.broadcast_to(first, (total, 128))
        second = jnp.sum(sum_two[...], axis=1, keepdims=True) * (1.0 / full)
        means[1] = jnp.broadcast_to(second, (total, 128))
        low_pad[total:, :] = jnp.zeros_like(low_pad[total:, :])

    def back(i, sums):
        here = pl.ds(pl.multiple_of(i * ROW_TILE, ROW_TILE), ROW_TILE)
        one = means[0, here, :][:, :1]
        two = means[1, here, :][:, :1]
        inv = scale[here, :][:, :1]
        grad = inv * (grad_unit[here, :].astype(F32) - one - unit[here, :].astype(F32) * two)
        low = (grad * slope[here, :].astype(F32)).astype(LOW)
        low_gate[here, :] = low
        low_pad[here, :] = low
        return sums + eights(low.astype(F32))

    columns[...] = lax.fori_loop(0, total // ROW_TILE, back, jnp.zeros((8, chunk), F32))
    first = pl.multiple_of(core[0] * half, half)
    other = pl.multiple_of((1 - core[0]) * half, half)
    mine[...] = dot_nn(normed_t[pl.ds(first, half), :], low_pad[...])
    theirs[...] = dot_nn(normed_t[pl.ds(other, half), :], low_pad[...]).astype(LOW)


def gate_back(core, normed_t, grad_unit, unit, slope, scale, sum_one, sum_two):
    total, full = unit.shape
    width, deep = normed_t.shape
    chunk = 512 if full % 512 == 0 else full
    half = width // 2
    whole = lambda a: pl.BlockSpec(a.shape, lambda i, c: (0, 0), pipeline_mode=pl.Buffered(1))
    cols = lambda n: pl.BlockSpec((n, chunk), lambda i, c: (0, i))
    shape = jax.ShapeDtypeStruct
    return pl.pallas_call(
        functools.partial(gate_back_kernel, full),
        grid_spec=pltpu.PrefetchScalarGridSpec(
            num_scalar_prefetch=1,
            grid=(full // chunk,),
            in_specs=[whole(normed_t), cols(total), cols(total), cols(total)]
            + [whole(scale), whole(sum_one), whole(sum_two)],
            out_specs=[cols(total), cols(half), cols(half), cols(8)],
            scratch_shapes=[pltpu.VMEM((2, total, 128), F32), pltpu.VMEM((deep, chunk), LOW)],
        ),
        out_shape=[
            shape((total, full), LOW),
            shape((half, full), F32),
            shape((half, full), LOW),
            shape((8, full), F32),
        ],
        compiler_params=compiler(48),
        cost_estimate=pl.CostEstimate(
            flops=2 * total * width * full, bytes_accessed=10 * total * full, transcendentals=0
        ),
        name="gate_back",
    )(core, normed_t, grad_unit, unit, slope, scale, sum_one, sum_two)


def token_kernel(tokens, cot, gated, low_value, low_gate, w_value, w_gate, w_back, model, output, grad_tokens, sums):
    @pl.when(pl.program_id(0) == 0)
    def _():
        sums[...] = jnp.zeros_like(sums)

    rows = tokens[...].astype(F32)
    width = rows.shape[1]
    branch = dot_nt(gated[...], w_back[...])
    output[...] = (rows + branch + model[2:3, :]).astype(LOW)
    grad = dot_nt(low_value[...], w_value[...]) + dot_nt(low_gate[...], w_gate[...])
    mean = jnp.sum(rows, axis=1, keepdims=True) * (1.0 / width)
    centred = rows - mean
    var = jnp.sum(centred * centred, axis=1, keepdims=True) * (1.0 / width)
    inv = lax.rsqrt(var + EPSILON)
    unit = centred * inv
    both = grad * unit
    du = grad * model[0:1, :]
    first = jnp.sum(du, axis=1, keepdims=True) * (1.0 / width)
    second = jnp.sum(both * model[0:1, :], axis=1, keepdims=True) * (1.0 / width)
    cot_here = cot[...].astype(F32)
    grad_tokens[...] = (cot_here + inv * (du - first - unit * second)).astype(LOW)
    sums[0:8, :] += eights(both)
    sums[8:16, :] += eights(grad)
    sums[16:24, :] += eights(cot_here)


def token_back(tokens, cot, gated, low_value, low_gate, w_value, w_gate, w_back, model, images, pad):
    width, full = w_value.shape
    total = images * pad
    rows = lambda n: pl.BlockSpec((pad, n), lambda i: (i, 0))
    whole = lambda a: pl.BlockSpec(a.shape, lambda i: (0, 0), pipeline_mode=pl.Buffered(1))
    shape = jax.ShapeDtypeStruct
    return pl.pallas_call(
        token_kernel,
        grid=(images,),
        in_specs=[rows(width), rows(width), rows(full), rows(full), rows(full)]
        + [whole(w_value), whole(w_gate), whole(w_back), whole(model)],
        out_specs=[rows(width), rows(width), pl.BlockSpec((24, width), lambda i: (0, 0))],
        out_shape=[shape((total, width), LOW), shape((total, width), LOW), shape((24, width), F32)],
        compiler_params=compiler(48),
        cost_estimate=pl.CostEstimate(
            flops=6 * total * width * full, bytes_accessed=8 * total * full, transcendentals=0
        ),
        name="token_back",
    )(tokens, cot, gated, low_value, low_gate, w_value, w_gate, w_back, model)


def split_two(v):
    high = v.astype(LOW)
    return high, (v - high.astype(F32)).astype(LOW)


def dot3(a, b):
    return dot_nn(a[0], b[0]) + (dot_nn(a[0], b[1]) + dot_nn(a[1], b[0]))


def muon_kernel(moments, mine, ortho, gram_now, total):
    size = gram_now.shape[0]
    gram = dot_nt(moments[...], moments[...])
    row = lax.broadcasted_iota(jnp.int32, (size, size), 0)
    col = lax.broadcasted_iota(jnp.int32, (size, size), 1)
    same = row == col
    norm = jnp.sqrt(jnp.sum(jnp.where(same, gram, 0.0), keepdims=True)) + 1e-07
    inv = 1.0 / norm
    gram_now[...] = gram * (inv * inv)
    for sweep in range(5):
        now = gram_now[...]
        now_two = split_two(now)
        extra = COEF_SECOND * now + COEF_THIRD * dot3(now_two, now_two)
        extra_two = split_two(extra)
        if sweep == 0:
            total[...] = jnp.where(same, COEF_FIRST + extra, extra)
        else:
            total[...] = COEF_FIRST * total[...] + dot3(extra_two, split_two(total[...]))
        if sweep < 4:
            half = COEF_FIRST * now + dot3(extra_two, now_two)
            gram_now[...] = COEF_FIRST * half + dot3(extra_two, split_two(half))
    ortho[...] = dot3(split_two(total[...]), split_two(mine[...])) * inv


def muon(moments, mine):
    size, full = moments.shape
    return pl.pallas_call(
        muon_kernel,
        out_shape=jax.ShapeDtypeStruct(mine.shape, F32),
        scratch_shapes=[pltpu.VMEM((size, size), F32)] * 2,
        compiler_params=compiler(48),
        cost_estimate=pl.CostEstimate(
            flops=2 * size * size * (51 * size + full), bytes_accessed=8 * size * full, transcendentals=0
        ),
        name="muon",
    )(moments, mine)
def newton_step(ortho, gram):
    polynomial = COEF_SECOND * gram + COEF_THIRD * jnp.dot(gram, gram, precision=HIGHEST)
    return COEF_FIRST * ortho + jnp.dot(polynomial, ortho, precision=HIGHEST)


def orthogonal(moment):
    ortho = moment / (jnp.sqrt(jnp.sum(moment * moment)) + 1e-07)
    for sweep in range(5):
        ortho = newton_step(ortho, jnp.dot(ortho, ortho.T, precision=HIGHEST))
    return ortho


def adam_update(param_now, grad_now, first_old, second_old):
    first_new = BETA_FIRST * first_old + (1.0 - BETA_FIRST) * grad_now
    second_new = BETA_SECOND * second_old + (1.0 - BETA_SECOND) * grad_now * grad_now
    first_hat = first_new / (1.0 - BETA_FIRST**STEP)
    second_hat = second_new / (1.0 - BETA_SECOND**STEP)
    updated = param_now * (1.0 - ADAM_RATE * DECAY_RATE) - ADAM_RATE * first_hat / (
        jnp.sqrt(second_hat) + 1e-08
    )
    return (second_new, updated)


def core_index():
    return lax.axis_index("dp") % 2


def swap_core(part):
    return lax.ppermute(part, "dp", [(i, i ^ 1) for i in range(lax.axis_size("dp"))])


def both_cores(mine):
    theirs = swap_core(mine)
    first = core_index() == 0
    return jnp.concatenate([jnp.where(first, mine, theirs), jnp.where(first, theirs, mine)], axis=0)


def exchange_mp(parts):
    return lax.all_to_all(parts, "mp", 0, 0)


def exchange_z(parts):
    size = lax.axis_size("dp")
    groups = [list(range(c, size, 2)) for c in range(2)]
    return lax.all_to_all(parts, "dp", 0, 0, axis_index_groups=groups)


def copies(part, count):
    return jnp.broadcast_to(part[None], (count,) + part.shape)


def gather_mp(part):
    return exchange_mp(copies(part, lax.axis_size("mp")))


def core_rows(rows, core):
    half = rows.shape[0] // 2
    return lax.dynamic_slice_in_dim(rows, core * half, half, 0)


def high_low(v):
    high = lax.reduce_precision(v, 8, 7)
    return high.astype(LOW), (v - high).astype(LOW)


def to_wire(main, small):
    return jnp.concatenate([main.astype(LOW), *high_low(small)], axis=-1)


def from_wire(wire, extra):
    cut = wire.shape[-1] - 2 * extra
    main, high, low = jnp.split(wire, [cut, cut + extra], axis=-1)
    return main.astype(F32), high.astype(F32) + low.astype(F32)


def plane_sum(mine, theirs, small):
    ways = lax.axis_size("mp")
    rows = mine[0].shape[0]
    mains = []
    for own, other in zip(mine, theirs):
        both = own + swap_core(other).astype(F32)
        mains.append(both.reshape(rows, ways, -1).transpose(1, 0, 2))
    main = jnp.concatenate(mains, axis=2)
    if small is None:
        return jnp.sum(exchange_mp(main.astype(LOW)).astype(F32), axis=0), None
    core = core_index()
    other = core_rows(small, 1 - core)
    got = swap_core(jnp.stack(high_low(other))).astype(F32)
    both = core_rows(small, core) + (got[0] + got[1])
    both = both.reshape(rows, ways, -1).transpose(1, 0, 2)
    parts, smalls = from_wire(exchange_mp(to_wire(main, both)), both.shape[2])
    return jnp.sum(parts, axis=0), jnp.sum(smalls, axis=0)


def depth_sum(main, small):
    depth = lax.axis_size("dp") // 2
    rows = main.shape[0]
    extra = small.shape[1]
    wire = to_wire(main, small).reshape(depth, rows // depth, -1)
    parts, smalls = from_wire(exchange_z(wire), extra)
    wire = to_wire(jnp.sum(parts, axis=0), jnp.sum(smalls, axis=0))
    wire = exchange_z(copies(wire, depth)).reshape(rows, -1)
    return from_wire(wire, extra)


def depth_exchange(main):
    depth = lax.axis_size("dp") // 2
    return jnp.sum(exchange_z(copies(main.astype(LOW), depth)).astype(F32), axis=0)


def to_images(rows, patches, count, pad):
    here, width = rows.shape
    spare = count * patches - here
    if spare:
        odd = lax.axis_index("mp") % 2 == 1
        size = lax.axis_size("mp")
        got = lax.ppermute(rows[:spare], "mp", [(i, i - 1) for i in range(1, size, 2)])
        kept = jnp.concatenate([rows[spare:], jnp.zeros((2 * spare, width), rows.dtype)], axis=0)
        rows = jnp.where(odd, kept, jnp.concatenate([rows, got], axis=0))
    images = rows.reshape(count, patches, width)
    return jnp.pad(images, ((0, 0), (0, pad - patches), (0, 0))).reshape(count * pad, width)


def from_images(rows, patches, count, pad, here):
    width = rows.shape[1]
    rows = rows.reshape(count, pad, width)[:, :patches].reshape(count * patches, width)
    spare = count * patches - here
    if spare:
        odd = lax.axis_index("mp") % 2 == 1
        size = lax.axis_size("mp")
        got = lax.ppermute(rows[here:], "mp", [(i, i + 1) for i in range(0, size, 2)])
        kept = jnp.concatenate([got, rows[: here - spare]], axis=0)
        rows = jnp.where(odd, kept, rows[:here])
    return rows


def per_device(
    tokens,
    cotangent,
    w_in,
    w_out,
    spatial,
    model_vectors,
    gate_vectors,
    patch_bias,
    moment_in,
    moment_out,
    moment_mix,
    first_model,
    second_model,
    first_gate,
    second_gate,
    first_patch,
    second_patch,
):
    here, width = tokens.shape
    shard = w_in.shape[2]
    ways = lax.axis_size("mp")
    full = shard * ways
    patches = spatial.shape[0]
    images = -(-here // patches)
    pad = -(-patches // 16) * 16
    total = images * pad
    deep = -(-total // 128) * 128
    core = core_index()
    core_arg = core.astype(jnp.int32).reshape(1)

    vec_all = gather_mp(gate_vectors).transpose(1, 0, 2).reshape(4, full)
    gate_part = gather_mp(core_rows(w_in[:, 1], core).astype(LOW))
    w_gate = both_cores(gate_part.transpose(1, 0, 2).reshape(width // 2, full))
    rest = jnp.concatenate([core_rows(w_in[:, 0], core), core_rows(w_out.T, core)], axis=1)
    rest = gather_mp(rest.astype(LOW))
    rest = jnp.stack([rest[:, :, :shard], rest[:, :, shard:]]).transpose(2, 0, 1, 3)
    rest = both_cores(rest.reshape(width // 2, 2 * full))
    w_value, w_back = rest[:, :full], rest[:, full:]

    tokens_pad = to_images(tokens, patches, images, pad)
    cot_pad = to_images(cotangent, patches, images, pad)
    rows_in = tokens_pad.astype(F32)
    centred = rows_in - jnp.mean(rows_in, axis=1, keepdims=True)
    inv_in = lax.rsqrt(jnp.mean(centred * centred, axis=1, keepdims=True) + EPSILON)
    normed = (centred * inv_in * model_vectors[0] + model_vectors[1]).astype(LOW)
    normed_t = jnp.pad(normed.T, ((0, 0), (0, deep - total)))
    cot_t = jnp.pad(cot_pad.T, ((0, 0), (0, deep - total)))
    mix = jnp.pad(spatial.astype(LOW), ((0, pad - patches), (0, pad - patches)))
    bias = jnp.broadcast_to(jnp.pad(patch_bias, (0, pad - patches))[:, None], (pad, 128))

    normal, unit, slope, scale = gate_forward(normed, w_gate, vec_all, images, pad)
    (
        gated,
        low_value,
        grad_unit,
        mine_value,
        theirs_value,
        mine_out,
        theirs_out,
        sum_one,
        sum_two,
        grad_mix,
        grad_bias,
        columns,
    ) = value_both(
        core_arg, normed, cot_pad, normed_t, cot_t, normal, unit, w_value, w_back, mix, mix.T, bias, vec_all, images, pad
    )
    low_gate, mine_gate, theirs_gate, gate_columns = gate_back(
        core_arg, normed_t, grad_unit, unit, slope, scale, sum_one, sum_two
    )
    output, grad_tokens, model_sums = token_back(
        tokens_pad, cot_pad, gated, low_value, low_gate, w_value, w_gate, w_back, model_vectors, images, pad
    )

    grad_vec = jnp.stack(
        [
            jnp.sum(columns[0:8], axis=0),
            jnp.sum(gate_columns, axis=0),
            jnp.sum(columns[8:16], axis=0),
            jnp.sum(columns[16:24], axis=0),
        ]
    )
    grad_model = jnp.sum(model_sums.reshape(3, 8, width), axis=1)
    grad_patch = jnp.sum(grad_bias[:patches], axis=1)
    flat = [grad_mix[:patches, :patches], grad_patch, grad_model, grad_vec]
    sizes = [math.prod(f.shape) for f in flat]
    unit_size = width * ways
    padded = -(-sum(sizes) // unit_size) * unit_size
    small = jnp.concatenate([f.reshape(-1) for f in flat] + [jnp.zeros(padded - sum(sizes), F32)])
    small = small.reshape(width, padded // width)
    extra = padded // unit_size

    main_one, small_one = plane_sum((mine_value, mine_out), (theirs_value, theirs_out), small)
    main_one, small_one = depth_sum(main_one, small_one)
    main_two, _ = plane_sum((mine_gate,), (theirs_gate,), None)
    main_two = depth_exchange(main_two)

    old_one = jnp.concatenate([moment_in[:, 0], moment_out.T], axis=1)
    half_one = MOMENTUM * core_rows(old_one, core) + main_one
    wire_one = gather_mp(to_wire(half_one, small_one))
    wire_one = both_cores(wire_one.transpose(1, 0, 2))
    grads_one = both_cores(main_one)
    half_two = MOMENTUM * core_rows(moment_in[:, 1], core) + main_two
    wire_two = gather_mp(half_two.astype(LOW))
    wire_two = both_cores(wire_two.transpose(1, 0, 2).reshape(width // 2, full))
    grads_two = both_cores(main_two)

    _, small = from_wire(wire_one, extra)
    small = small.reshape(-1)
    ends = [sum(sizes[: i + 1]) for i in range(4)]
    grad_spatial = small[: ends[0]].reshape(patches, patches)
    grad_patch = small[ends[0] : ends[1]]
    grad_model = small[ends[1] : ends[2]].reshape(3, width)
    grad_vec = small[ends[2] : ends[3]].reshape(4, full)
    grad_vec = lax.dynamic_slice_in_dim(grad_vec, lax.axis_index("mp") * shard, shard, 1)

    all_value = wire_one[:, :, :shard].reshape(width, full)
    all_out = wire_one[:, :, shard : 2 * shard].reshape(width, full)
    moment_out_t = MOMENTUM * moment_out.T + grads_one[:, shard:]
    ortho_out = muon(all_out, moment_out_t).T
    grad_in = jnp.concatenate([grads_one[:, :shard], grads_two], axis=1)
    moment_in_flat = MOMENTUM * moment_in.reshape(width, 2 * shard) + grad_in
    ortho_in = muon(jnp.concatenate([all_value, wire_two], axis=1), moment_in_flat)
    ortho_in = ortho_in.reshape(width, 2, shard)
    new_moment_in = moment_in_flat.reshape(width, 2, shard)
    new_moment_out = moment_out_t.T
    grad_w_in = grad_in.reshape(width, 2, shard)
    grad_w_out = grads_one[:, shard:].T
    new_moment_mix = MOMENTUM * moment_mix + grad_spatial

    shrink_by = 1.0 - MUON_RATE * DECAY_RATE
    new_w_in = w_in * shrink_by - MUON_RATE * 0.2 * math.sqrt(max(width, 2 * full)) * ortho_in
    new_w_out = w_out * shrink_by - MUON_RATE * 0.2 * math.sqrt(max(width, full)) * ortho_out
    new_spatial = spatial * shrink_by - MUON_RATE * 0.2 * math.sqrt(patches) * orthogonal(
        new_moment_mix
    )
    new_second_model, new_model = adam_update(model_vectors, grad_model, first_model, second_model)
    new_second_gate, new_gate = adam_update(gate_vectors, grad_vec, first_gate, second_gate)
    new_second_patch, new_patch = adam_update(patch_bias, grad_patch, first_patch, second_patch)
    return (
        from_images(output, patches, images, pad, here),
        from_images(grad_tokens, patches, images, pad, here),
        grad_w_in,
        grad_w_out,
        grad_spatial,
        grad_model,
        grad_vec,
        grad_patch,
        new_moment_in,
        new_moment_out,
        new_moment_mix,
        new_second_model,
        new_second_gate,
        new_second_patch,
        new_w_in,
        new_w_out,
        new_spatial,
        new_model,
        new_gate,
        new_patch,
    )


def solution(mesh):
    rows = P(("dp", "mp"), None)
    wide = P(None, None, "mp")
    tall = P("mp", None)
    columns = P(None, "mp")
    return jax.shard_map(
        per_device,
        mesh=mesh,
        in_specs=(
            (rows, rows, wide, tall, P(), P(), columns, P())
            + (wide, tall, P(), P(), P(), columns, columns, P(), P())
        ),
        out_specs=(
            (rows, rows, wide, tall, P(), P(), columns, P())
            + (wide, tall, P(), P(), columns, P())
            + (wide, tall, P(), P(), columns, P())
        ),
        check_vma=False,
    )
```

```python
import functools
import math

import jax
import jax.numpy as jnp
from jax import lax
from jax.experimental import pallas as pl
from jax.experimental.pallas import tpu as pltpu
from jax.sharding import PartitionSpec as P

STEP = 10
EPSILON = 1e-05
COEF_FIRST = 3.4445
COEF_SECOND = -4.775
COEF_THIRD = 2.0315
MOMENTUM = 0.95
MUON_RATE = 0.2
ADAM_RATE = 0.3
DECAY_RATE = 0.01
BETA_FIRST = 0.9
BETA_SECOND = 0.95
LOW = jnp.bfloat16
F32 = jnp.float32


ROW_TILE = 16
UNROLL = 3
EXTRA = 32
MIX_ROW = 4
CHUNK = 512
CUBIC = 0.044715
SLOPE = math.sqrt(2.0 / math.pi)


def compiler(megabytes):
    return pltpu.CompilerParams(vmem_limit_bytes=megabytes << 20)


def dot_nn(a, b):
    return jnp.dot(a, b, preferred_element_type=F32)


def dot_nt(a, b):
    return lax.dot_general(a, b, (((1,), (1,)), ((), ())), preferred_element_type=F32)


def gelu_pair(hidden):
    square = hidden * hidden
    half = 0.5 + 0.5 * jnp.tanh(hidden * (SLOPE + (SLOPE * CUBIC) * square))
    active = hidden * half
    slope = half + (active - active * half) * (2.0 * SLOPE + (6.0 * SLOPE * CUBIC) * square)
    return active, slope


def lanes(v):
    total = v[:, :128]
    for at in range(128, v.shape[1], 128):
        total = total + v[:, at : at + 128]
    return total


def eights(v):
    total = v[:8]
    for at in range(8, v.shape[0], 8):
        total = total + v[at : at + 8]
    return total


def wide(v, width):
    return jnp.concatenate([v] * (width // 128), axis=1) if width % 128 == 0 else v[:, :1]


def tiles(count, body, carry=None):
    def step(i, kept):
        return body(pl.ds(pl.multiple_of(i * ROW_TILE, ROW_TILE), ROW_TILE), kept)

    return lax.fori_loop(0, count // ROW_TILE, step, carry, unroll=UNROLL)


def spread_pieces(core, mine, theirs, out, offset):
    half = out.shape[0] // 2
    count = mine.shape[0]
    shard = out.shape[1] // count
    first = pl.ds(pl.multiple_of(core[0] * half, half), half)
    other = pl.ds(pl.multiple_of((1 - core[0]) * half, half), half)
    for piece in range(count):
        cols = slice(piece * shard, (piece + 1) * shard)
        out[first, cols] = mine[piece, :half, offset : offset + shard]
        out[other, cols] = theirs[piece, :half, offset : offset + shard]


def gate_kernel(chunk, core, normed, mine, theirs, normal, unit, slope, scale, weight, vec, active):
    rows, full = active.shape
    half = weight.shape[0] // 2

    @pl.when(pl.program_id(0) == 0)
    def _():
        spread_pieces(core, mine, theirs, weight, 0)
        count, _, shard = mine.shape
        for piece in range(count):
            terms = mine[piece, half:, :].astype(F32)
            vec[:, piece * shard : (piece + 1) * shard] = (terms[0:8] + terms[8:16]) + terms[16:24]

    starts = range(0, full, chunk)
    for at in starts:
        active[:, at : at + chunk] = dot_nn(normed[...], weight[:, at : at + chunk])

    def act(here, _):
        total = jnp.zeros((ROW_TILE, 128), F32)
        for at in starts:
            cols = slice(at, at + chunk)
            value, grad = gelu_pair(active[here, cols] + vec[1:2, cols])
            active[here, cols] = value
            slope[here, cols] = grad.astype(LOW)
            total = total + lanes(value)
        scale[here, :] = total

    tiles(rows, act)
    mean = jnp.sum(scale[...], axis=1, keepdims=True) * (1.0 / full)
    scale[...] = jnp.broadcast_to(mean, scale.shape)

    def spread(here, _):
        total = jnp.zeros((ROW_TILE, 128), F32)
        mean_here = wide(scale[here, :], chunk)
        for at in starts:
            cols = slice(at, at + chunk)
            centred = active[here, cols] - mean_here
            active[here, cols] = centred
            total = total + lanes(centred * centred)
        scale[here, :] = total

    tiles(rows, spread)
    var = jnp.sum(scale[...], axis=1, keepdims=True) * (1.0 / full)
    scale[...] = jnp.broadcast_to(lax.rsqrt(var + EPSILON), scale.shape)

    def finish(here, _):
        inv = wide(scale[here, :], chunk)
        for at in starts:
            cols = slice(at, at + chunk)
            unit_here = active[here, cols] * inv
            unit[here, cols] = unit_here.astype(LOW)
            normal[here, cols] = (unit_here * vec[2:3, cols] + vec[3:4, cols]).astype(LOW)

    tiles(rows, finish)


def gate_forward(core, normed, mine, theirs, images, pad):
    count, _, shard = mine.shape
    full = count * shard
    width = normed.shape[1]
    chunk = 512 if full % 512 == 0 else full
    total = images * pad
    whole = lambda a: pl.BlockSpec(a.shape, lambda i, c: (0,) * a.ndim, pipeline_mode=pl.Buffered(1))
    rows = lambda n: pl.BlockSpec((pad, n), lambda i, c: (i, 0))
    fixed = lambda *f: pl.BlockSpec(f, lambda i, c: (0, 0))
    shape = jax.ShapeDtypeStruct
    return pl.pallas_call(
        functools.partial(gate_kernel, chunk),
        grid_spec=pltpu.PrefetchScalarGridSpec(
            num_scalar_prefetch=1,
            grid=(images,),
            in_specs=[rows(width), whole(mine), whole(theirs)],
            out_specs=[rows(full), rows(full), rows(full), rows(128), fixed(width, full), fixed(8, full)],
            scratch_shapes=[pltpu.VMEM((pad, full), F32)],
        ),
        out_shape=[shape((total, full), LOW)] * 3
        + [shape((total, 128), F32), shape((width, full), LOW), shape((8, full), F32)],
        compiler_params=compiler(48),
        cost_estimate=pl.CostEstimate(
            flops=2 * total * width * full, bytes_accessed=8 * total * full, transcendentals=total * full
        ),
        name="gate_forward",
    )(core, normed, mine, theirs)


def value_kernel(
    pad,
    images,
    core,
    normed,
    cot,
    normed_t,
    cot_t,
    normal,
    unit,
    w_mine,
    w_theirs,
    mix,
    mix_t,
    bias,
    vec,
    gated,
    low_value,
    grad_unit,
    mine,
    theirs,
    sum_one,
    sum_two,
    mix_pieces,
    w_value,
    w_back,
    grad_mix,
    grad_bias,
    hidden,
    back,
    mixed,
    low_mixed,
    low_pad,
    gated_pad,
):
    total, chunk = hidden.shape
    half = w_value.shape[0] // 2
    step = pl.program_id(0)
    cols = pl.ds(pl.multiple_of(step * chunk, chunk), chunk)

    @pl.when(step == 0)
    def _():
        offset = w_mine.shape[2] - w_value.shape[1] // w_mine.shape[0]
        spread_pieces(core, w_mine, w_theirs, w_value, 0)
        spread_pieces(core, w_mine, w_theirs, w_back, offset)
        sum_one[...] = jnp.zeros_like(sum_one)
        sum_two[...] = jnp.zeros_like(sum_two)
        grad_mix[...] = jnp.zeros_like(grad_mix)
        grad_bias[...] = jnp.zeros_like(grad_bias)
        low_pad[total:, :] = jnp.zeros_like(low_pad[total:, :])
        gated_pad[total:, :] = jnp.zeros_like(gated_pad[total:, :])

    hidden[...] = dot_nn(normed[...], w_value[:, cols])
    back[...] = dot_nn(cot[...], w_back[:, cols])
    for image in range(images):
        here = slice(image * pad, (image + 1) * pad)
        mixed[here, :] = dot_nn(mix[...], normal[here, :])

    def forward(i, sums):
        here = pl.ds(pl.multiple_of(i * ROW_TILE, ROW_TILE), ROW_TILE)
        row = pl.ds(pl.multiple_of(lax.rem(i, pad // ROW_TILE) * ROW_TILE, ROW_TILE), ROW_TILE)
        value, slope = gelu_pair(hidden[here, :] + vec[0:1, :])
        mixed_here = mixed[here, :] + wide(bias[row, :], chunk)
        back_here = back[here, :]
        gated_here = (value * mixed_here).astype(LOW)
        gated[here, :] = gated_here
        gated_pad[here, :] = gated_here
        grad_here = (back_here * value).astype(LOW)
        low_mixed[here, :] = grad_here
        grad_bias[row, :] += lanes(grad_here.astype(F32))
        low_here = (back_here * mixed_here * slope).astype(LOW)
        low_value[here, :] = low_here
        low_pad[here, :] = low_here
        return sums + eights(low_here.astype(F32))

    bias_sum = lax.fori_loop(0, total // ROW_TILE, forward, jnp.zeros((8, chunk), F32), unroll=UNROLL)

    for image in range(images):
        here = slice(image * pad, (image + 1) * pad)
        mixed[here, :] = dot_nn(mix_t[...], low_mixed[here, :])
        grad_mix[:, :pad] += dot_nt(low_mixed[here, :], normal[here, :])

    first = pl.multiple_of(core[0] * half, half)
    other = pl.multiple_of((1 - core[0]) * half, half)
    mine[0, :half, :] = dot_nn(normed_t[pl.ds(first, half), :], low_pad[...])
    theirs[0, :half, :] = dot_nn(normed_t[pl.ds(other, half), :], low_pad[...]).astype(LOW)
    mine[1, :half, :] = dot_nn(cot_t[pl.ds(first, half), :], gated_pad[...])
    theirs[1, :half, :] = dot_nn(cot_t[pl.ds(other, half), :], gated_pad[...]).astype(LOW)

    def backward(i, sums):
        here = pl.ds(pl.multiple_of(i * ROW_TILE, ROW_TILE), ROW_TILE)
        grad = mixed[here, :]
        unit_here = unit[here, :].astype(F32)
        gain = vec[2:3, :]
        both = grad * unit_here
        du = grad * gain
        grad_unit[here, :] = du.astype(LOW)
        sum_one[here, :] += lanes(du)
        sum_two[here, :] += lanes(both * gain)
        return sums[0] + eights(both), sums[1] + eights(grad)

    zero = jnp.zeros((8, chunk), F32)
    gain_sum, shift_sum = lax.fori_loop(0, total // ROW_TILE, backward, (zero, zero), unroll=UNROLL)
    total_of = lambda v: jnp.sum(v, axis=0, keepdims=True)
    more = mine.shape[1] - half
    rows = lax.broadcasted_iota(jnp.int32, (more, chunk), 0)
    first_rows = jnp.where(rows == 0, total_of(bias_sum), 0.0)
    second_rows = jnp.where(rows == 0, total_of(gain_sum), jnp.where(rows == 1, total_of(shift_sum), 0.0))
    for i, both_rows in enumerate((first_rows, second_rows)):
        mine[i, half:, :] = both_rows.astype(LOW).astype(F32)
        theirs[i, half:, :] = both_rows.astype(LOW)

    @pl.when(step == pl.num_programs(0) - 1)
    def _():
        patch = jnp.sum(grad_bias[...], axis=1, keepdims=True)
        grad_mix[:, pad:] = jnp.broadcast_to(patch, (pad, grad_mix.shape[1] - pad))
        each = mix_pieces.shape[1]
        for piece in range(mix_pieces.shape[0]):
            mix_pieces[piece] = grad_mix[piece * each : (piece + 1) * each, :]


def value_both(core, normed, cot, normed_t, cot_t, normal, unit, w_mine, w_theirs, mix, mix_t, bias, vec, images, pad, ways):
    width = normed.shape[1]
    full = normal.shape[1]
    total = images * pad
    deep = normed_t.shape[1]
    chunk = CHUNK if full % CHUNK == 0 else full
    half = width // 2
    more = half + EXTRA
    wide_mix = -(-(pad + 1) // 128) * 128
    mix_shape = (ways, pad // ways, wide_mix)
    whole = lambda a: pl.BlockSpec(a.shape, lambda i, c: (0,) * a.ndim, pipeline_mode=pl.Buffered(1))
    cols = lambda n: pl.BlockSpec((n, chunk), lambda i, c: (0, i))
    pair = pl.BlockSpec((2, more, chunk), lambda i, c: (0, 0, i))
    fixed = lambda *f: pl.BlockSpec(f, lambda i, c: (0, 0))
    shape = jax.ShapeDtypeStruct
    return pl.pallas_call(
        functools.partial(value_kernel, pad, images),
        grid_spec=pltpu.PrefetchScalarGridSpec(
            num_scalar_prefetch=1,
            grid=(full // chunk,),
            in_specs=[whole(normed), whole(cot), whole(normed_t), whole(cot_t)]
            + [cols(total), cols(total), whole(w_mine), whole(w_theirs)]
            + [whole(mix), whole(mix_t), whole(bias), cols(8)],
            out_specs=[cols(total), cols(total), cols(total), pair, pair]
            + [fixed(total, 128), fixed(total, 128), pl.BlockSpec(mix_shape, lambda i, c: (0, 0, 0))]
            + [fixed(width, full), fixed(width, full)],
            scratch_shapes=[pltpu.VMEM((pad, wide_mix), F32), pltpu.VMEM((pad, 128), F32)]
            + [pltpu.VMEM((total, chunk), F32)] * 3
            + [pltpu.VMEM((total, chunk), LOW)]
            + [pltpu.VMEM((deep, chunk), LOW)] * 2,
        ),
        out_shape=[shape((total, full), LOW)] * 3
        + [shape((2, more, full), F32), shape((2, more, full), LOW)]
        + [shape((total, 128), F32)] * 2
        + [shape(mix_shape, F32), shape((width, full), LOW), shape((width, full), LOW)],
        compiler_params=compiler(60),
        cost_estimate=pl.CostEstimate(
            flops=12 * total * width * full, bytes_accessed=20 * total * full, transcendentals=total * full
        ),
        name="value_both",
    )(core, normed, cot, normed_t, cot_t, normal, unit, w_mine, w_theirs, mix, mix_t, bias, vec)


def gate_back_kernel(
    full, core, normed_t, grad_unit, unit, slope, scale, sum_one, sum_two, low_gate, mine, theirs, means, low_pad
):
    total, chunk = low_gate.shape
    half = normed_t.shape[0] // 2
    more = mine.shape[0] - half

    @pl.when(pl.program_id(0) == 0)
    def _():
        first = jnp.sum(sum_one[...], axis=1, keepdims=True) * (1.0 / full)
        means[0] = jnp.broadcast_to(first, (total, 128))
        second = jnp.sum(sum_two[...], axis=1, keepdims=True) * (1.0 / full)
        means[1] = jnp.broadcast_to(second, (total, 128))
        low_pad[total:, :] = jnp.zeros_like(low_pad[total:, :])

    def back(i, sums):
        here = pl.ds(pl.multiple_of(i * ROW_TILE, ROW_TILE), ROW_TILE)
        one = wide(means[0, here, :], chunk)
        two = wide(means[1, here, :], chunk)
        inv = wide(scale[here, :], chunk)
        grad = inv * (grad_unit[here, :].astype(F32) - one - unit[here, :].astype(F32) * two)
        low = (grad * slope[here, :].astype(F32)).astype(LOW)
        low_gate[here, :] = low
        low_pad[here, :] = low
        return sums + eights(low.astype(F32))

    sums = lax.fori_loop(0, total // ROW_TILE, back, jnp.zeros((8, chunk), F32), unroll=UNROLL)
    row = lax.broadcasted_iota(jnp.int32, (more, chunk), 0)
    rows = jnp.where(row == 0, jnp.sum(sums, axis=0, keepdims=True), 0.0)
    mine[half:, :] = rows.astype(LOW).astype(F32)
    theirs[half:, :] = rows.astype(LOW)
    first = pl.multiple_of(core[0] * half, half)
    other = pl.multiple_of((1 - core[0]) * half, half)
    mine[:half, :] = dot_nn(normed_t[pl.ds(first, half), :], low_pad[...])
    theirs[:half, :] = dot_nn(normed_t[pl.ds(other, half), :], low_pad[...]).astype(LOW)


def gate_back(core, normed_t, grad_unit, unit, slope, scale, sum_one, sum_two):
    total, full = unit.shape
    width, deep = normed_t.shape
    chunk = CHUNK if full % CHUNK == 0 else full
    more = width // 2 + EXTRA
    whole = lambda a: pl.BlockSpec(a.shape, lambda i, c: (0, 0), pipeline_mode=pl.Buffered(1))
    cols = lambda n: pl.BlockSpec((n, chunk), lambda i, c: (0, i))
    shape = jax.ShapeDtypeStruct
    return pl.pallas_call(
        functools.partial(gate_back_kernel, full),
        grid_spec=pltpu.PrefetchScalarGridSpec(
            num_scalar_prefetch=1,
            grid=(full // chunk,),
            in_specs=[whole(normed_t), cols(total), cols(total), cols(total)]
            + [whole(scale), whole(sum_one), whole(sum_two)],
            out_specs=[cols(total), cols(more), cols(more)],
            scratch_shapes=[pltpu.VMEM((2, total, 128), F32), pltpu.VMEM((deep, chunk), LOW)],
        ),
        out_shape=[
            shape((total, full), LOW),
            shape((more, full), F32),
            shape((more, full), LOW),
        ],
        compiler_params=compiler(48),
        cost_estimate=pl.CostEstimate(
            flops=2 * total * width * full, bytes_accessed=10 * total * full, transcendentals=0
        ),
        name="gate_back",
    )(core, normed_t, grad_unit, unit, slope, scale, sum_one, sum_two)


def gate_wire_kernel(core, w_in, vectors, wire):
    half, _, shard = w_in.shape
    low = w_in[:, 1, :].astype(LOW)
    value = jnp.concatenate([vectors[...], jnp.zeros((4, shard), F32)], axis=0)
    high = value.astype(LOW).astype(F32)
    middle = (value - high).astype(LOW).astype(F32)
    last = value - high - middle
    terms = jnp.concatenate([high, middle, last, jnp.zeros((8, shard), F32)], axis=0).astype(LOW)
    for receiver in range(wire.shape[0]):
        wire[receiver, :half, :] = low
        wire[receiver, half:, :] = terms


def rest_wire_kernel(core, w_in, w_out, wire):
    shard = w_in.shape[2]
    value = w_in[:, 0, :].astype(LOW)
    back = w_out[...].T.astype(LOW)
    for receiver in range(wire.shape[0]):
        wire[receiver, :, :shard] = value
        wire[receiver, :, shard:] = back


def weight_wires(core, w_in, w_out, vectors):
    width, _, shard = w_in.shape
    half = width // 2
    ways = lax.axis_size("mp")
    rows = pl.BlockSpec((half, 2, shard), lambda i, c: (c[0], 0, 0))
    fixed = lambda *f: pl.BlockSpec(f, lambda i, c: (0,) * len(f))
    spec = lambda ins, out: pltpu.PrefetchScalarGridSpec(
        num_scalar_prefetch=1, grid=(1,), in_specs=ins, out_specs=fixed(*out)
    )
    out = (ways, half + 32, shard)
    gate = pl.pallas_call(
        gate_wire_kernel,
        grid_spec=spec([rows, fixed(4, shard)], out),
        out_shape=jax.ShapeDtypeStruct(out, LOW),
        compiler_params=compiler(32),
        name="gate_wire",
    )(core, w_in, vectors)
    out = (ways, half, 2 * shard)
    if shard % 128:
        back = lax.dynamic_slice_in_dim(w_out, core[0] * half, half, 1)
        rest = jnp.concatenate([core_rows(w_in[:, 0], core[0]), back.T], axis=1).astype(LOW)
        return gate, copies(rest, ways)
    rest = pl.pallas_call(
        rest_wire_kernel,
        grid_spec=spec([rows, pl.BlockSpec((shard, half), lambda i, c: (0, c[0]))], out),
        out_shape=jax.ShapeDtypeStruct(out, LOW),
        compiler_params=compiler(32),
        name="rest_wire",
    )(core, w_in, w_out)
    return gate, rest


def merge_kernel(mine, theirs, *refs):
    wire = refs[-1]
    count, rows, shard = mine.shape
    for i in range(count):
        wire[0, :, i * shard : (i + 1) * shard] = (mine[i] + theirs[i].astype(F32)).astype(LOW)
    if len(refs) > 1:
        mix = refs[0][0] + refs[1][0]
        each = mix.shape[0] // count
        top = rows - EXTRA
        for i in range(count):
            block = (mine[i, top:] + theirs[i, top:].astype(F32))[:, : mix.shape[1]]
            part = mix[i * each : (i + 1) * each]
            block = jnp.concatenate([block[:MIX_ROW], part, block[MIX_ROW + each :]], axis=0)
            wire[0, top:, i * shard : i * shard + mix.shape[1]] = block.astype(LOW)


def merge(mine, theirs, ways, mix=()):
    count, rows, full = mine.shape
    shard = full // ways
    if shard % 128:
        both = mine + theirs.astype(F32)
        blocks = both.reshape(count, rows, ways, shard).transpose(2, 1, 0, 3)
        return blocks.reshape(ways, rows, count * shard).astype(LOW)
    block = pl.BlockSpec((count, rows, shard), lambda i: (0, 0, i))
    return pl.pallas_call(
        merge_kernel,
        grid=(ways,),
        in_specs=[block, block] + [pl.BlockSpec((1,) + m.shape[1:], lambda i: (i, 0, 0)) for m in mix],
        out_specs=pl.BlockSpec((1, rows, count * shard), lambda i: (i, 0, 0)),
        out_shape=jax.ShapeDtypeStruct((ways, rows, count * shard), LOW),
        compiler_params=compiler(32),
        name="merge",
    )(mine, theirs, *mix)


def mix_rides(shard, mix):
    return shard % 128 == 0 and mix.shape[2] <= shard and mix.shape[0] > 1 and mix.shape[1] % 2 == 0 and (
        mix.shape[1] // 2 + MIX_ROW <= EXTRA
    )


def moments_kernel(core, one, one_other, two, two_other, old_in, old_out, grad_in, new_in, grad_out, new_out, flat):
    width, _, shard = old_in.shape
    half = width // 2
    rows = (
        pl.ds(pl.multiple_of(core[0] * half, half), half),
        pl.ds(pl.multiple_of((1 - core[0]) * half, half), half),
    )
    for here, first, second in ((rows[0], one, two), (rows[1], one_other, two_other)):
        flat[0, here, :] = first[:half, :shard].astype(F32)
        flat[1, here, :] = second[:half, :].astype(F32)
        flat[2, here, :] = first[:half, shard:].astype(F32)
    for i in range(2):
        grad = flat[i]
        grad_in[:, i, :] = grad
        moment = MOMENTUM * old_in[:, i, :] + grad
        new_in[:, i, :] = moment
        flat[i] = moment
    grad = flat[2].T
    grad_out[...] = grad
    moment = MOMENTUM * old_out[...] + grad
    new_out[...] = moment
    flat[2] = moment.T


def moments(core, one, one_other, two, two_other, old_in, old_out):
    width, _, shard = old_in.shape
    shape = lambda *f: jax.ShapeDtypeStruct(f, F32)
    return pl.pallas_call(
        moments_kernel,
        grid_spec=pltpu.PrefetchScalarGridSpec(
            num_scalar_prefetch=1,
            grid=(1,),
            in_specs=[
                pl.BlockSpec(a.shape, lambda i, c, n=a.ndim: (0,) * n)
                for a in (one, one_other, two, two_other, old_in, old_out)
            ],
            out_specs=[
                pl.BlockSpec(f, lambda i, c, n=len(f): (0,) * n)
                for f in ((width, 2, shard), (width, 2, shard), (shard, width), (shard, width), (3, width, shard))
            ],
        ),
        out_shape=[
            shape(width, 2, shard), shape(width, 2, shard), shape(shard, width), shape(shard, width), shape(3, width, shard)
        ],
        compiler_params=compiler(48),
        name="moments",
    )(core, one, one_other, two, two_other, old_in, old_out)


def square_muon_kernel(moment, ortho, now):
    size = moment.shape[0]
    now[...] = jnp.zeros_like(now)
    start = moment[...]
    norm = jnp.sqrt(jnp.sum(start * start, keepdims=True)) + 1e-07
    now[:size, :size] = start / norm
    for sweep in range(5):
        x = now[...]
        x_two = split_two(x)
        gram = dot_nt(x_two[0], x_two[0]) + (dot_nt(x_two[0], x_two[1]) + dot_nt(x_two[1], x_two[0]))
        gram_two = split_two(gram)
        extra = COEF_SECOND * gram + COEF_THIRD * dot3(gram_two, gram_two)
        now[...] = COEF_FIRST * x + dot3(split_two(extra), x_two)
    ortho[...] = now[:size, :size]


def square_muon(moment):
    size = -(-moment.shape[0] // 128) * 128
    return pl.pallas_call(
        square_muon_kernel,
        out_shape=jax.ShapeDtypeStruct(moment.shape, F32),
        scratch_shapes=[pltpu.VMEM((size, size), F32)],
        name="square_muon",
    )(moment)


def prep_kernel(patches, pad, tokens, cot, model, normed, unit, scale, cot_pad, normed_t, cot_t, keep):
    step = pl.program_id(0)
    group = tokens.shape[1] // patches
    rows = group * pad
    width = tokens.shape[2]

    def padded(block):
        block = block[0].astype(F32)
        gap = jnp.zeros((pad - patches, width), F32)
        parts = []
        for image in range(group):
            parts += [block[image * patches : (image + 1) * patches], gap]
        return jnp.concatenate(parts, axis=0)

    here = pl.ds(pl.multiple_of(step * rows, rows), rows)

    @pl.when(step == 0)
    def _():
        keep[...] = jnp.zeros_like(keep)

    cot_here = padded(cot)
    cot_pad[...] = cot_here.astype(LOW)
    keep[1, here, :] = cot_here
    x = padded(tokens)
    centred = x - jnp.sum(x, axis=1, keepdims=True) * (1.0 / width)
    inv = lax.rsqrt(jnp.sum(centred * centred, axis=1, keepdims=True) * (1.0 / width) + EPSILON)
    unit_here = centred * inv
    scale[...] = jnp.broadcast_to(inv, scale.shape)
    unit[...] = unit_here.astype(LOW)
    low = (unit_here * model[0:1, :] + model[1:2, :]).astype(LOW)
    normed[...] = low
    keep[0, here, :] = low.astype(F32)

    @pl.when(step == pl.num_programs(0) - 1)
    def _():
        for at in range(0, normed_t.shape[1], 128):
            cols = slice(at, at + 128)
            normed_t[:, cols] = keep[0, cols, :].T.astype(LOW)
            cot_t[:, cols] = keep[1, cols, :].T.astype(LOW)


def prep(tokens, cot, model, patches, pad):
    here, width = tokens.shape
    images = here // patches
    group = 2 if images % 2 == 0 else images
    steps = images // group
    total = images * pad
    deep = -(-total // 128) * 128
    block = pl.BlockSpec((1, group * patches, width), lambda i: (i, 0, 0))
    rows = lambda n: pl.BlockSpec((group * pad, n), lambda i: (i, 0))
    fixed = lambda *f: pl.BlockSpec(f, lambda i: (0, 0))
    shape = jax.ShapeDtypeStruct
    return pl.pallas_call(
        functools.partial(prep_kernel, patches, pad),
        grid=(steps,),
        in_specs=[block, block, fixed(3, width)],
        out_specs=[rows(width), rows(width), rows(128), rows(width), fixed(width, deep), fixed(width, deep)],
        out_shape=[
            shape((total, width), LOW),
            shape((total, width), LOW),
            shape((total, 128), F32),
            shape((total, width), LOW),
            shape((width, deep), LOW),
            shape((width, deep), LOW),
        ],
        scratch_shapes=[pltpu.VMEM((2, deep, width), F32)],
        compiler_params=compiler(48),
        cost_estimate=pl.CostEstimate(flops=20 * total * width, bytes_accessed=20 * total * width, transcendentals=total),
        name="prep",
    )(tokens.reshape(steps, group * patches, width), cot.reshape(steps, group * patches, width), model)


def token_kernel(
    patches, pad, tokens, cot, unit, scale, gated, low_value, low_gate, w_value, w_gate, w_back, model, output, grad_tokens, sums, branch, grad
):
    group = tokens.shape[1] // patches
    width = tokens.shape[2]
    rows = group * pad

    @pl.when(pl.program_id(0) == 0)
    def _():
        sums[...] = jnp.zeros_like(sums)

    def packed(v):
        return jnp.concatenate([v[i * pad : i * pad + patches] for i in range(group)], axis=0)

    branch[...] = dot_nt(gated[...], w_back[...])
    output[0] = (tokens[0].astype(F32) + packed(branch) + model[2:3, :]).astype(LOW)
    grad[...] = dot_nt(low_value[...], w_value[...]) + dot_nt(low_gate[...], w_gate[...])

    def back(i, kept):
        here = pl.ds(pl.multiple_of(i * ROW_TILE, ROW_TILE), ROW_TILE)
        grad_here = grad[here, :]
        unit_here = unit[here, :].astype(F32)
        both = grad_here * unit_here
        du = grad_here * model[0:1, :]
        first = jnp.sum(du, axis=1, keepdims=True) * (1.0 / width)
        second = jnp.sum(both * model[0:1, :], axis=1, keepdims=True) * (1.0 / width)
        branch[here, :] = wide(scale[here, :], width) * (du - first - unit_here * second)
        return kept[0] + eights(both), kept[1] + eights(grad_here)

    zero = jnp.zeros((8, width), F32)
    gain, shift = lax.fori_loop(0, rows // ROW_TILE, back, (zero, zero), unroll=2)
    cot_here = cot[0].astype(F32)
    grad_tokens[0] = (cot_here + packed(branch)).astype(LOW)
    sums[0:1, :] += jnp.sum(gain, axis=0, keepdims=True)
    sums[1:2, :] += jnp.sum(shift, axis=0, keepdims=True)
    sums[2:3, :] += jnp.sum(eights(cot_here), axis=0, keepdims=True)


def token_back(tokens, cot, unit, scale, gated, low_value, low_gate, w_value, w_gate, w_back, model, patches, pad):
    here, width = tokens.shape
    full = w_value.shape[1]
    images = here // patches
    group = 2 if images % 2 == 0 else images
    steps = images // group
    total = images * pad
    block = pl.BlockSpec((1, group * patches, width), lambda i: (i, 0, 0))
    rows = lambda n: pl.BlockSpec((group * pad, n), lambda i: (i, 0))
    whole = lambda a: pl.BlockSpec(a.shape, lambda i: (0, 0), pipeline_mode=pl.Buffered(1))
    shape = jax.ShapeDtypeStruct
    output, grad_tokens, sums = pl.pallas_call(
        functools.partial(token_kernel, patches, pad),
        grid=(steps,),
        in_specs=[block, block, rows(width), rows(128), rows(full), rows(full), rows(full)]
        + [whole(w_value), whole(w_gate), whole(w_back), whole(model)],
        out_specs=[block, block, pl.BlockSpec((8, width), lambda i: (0, 0))],
        out_shape=[shape((steps, group * patches, width), LOW)] * 2 + [shape((8, width), F32)],
        scratch_shapes=[pltpu.VMEM((group * pad, width), F32)] * 2,
        compiler_params=compiler(48),
        cost_estimate=pl.CostEstimate(
            flops=6 * total * width * full, bytes_accessed=8 * total * full, transcendentals=0
        ),
        name="token_back",
    )(
        tokens.reshape(steps, group * patches, width),
        cot.reshape(steps, group * patches, width),
        unit, scale, gated, low_value, low_gate, w_value, w_gate, w_back, model,
    )
    return output.reshape(here, width), grad_tokens.reshape(here, width), sums


def split_two(v):
    high = v.astype(LOW)
    return high, (v - high.astype(F32)).astype(LOW)


def dot3(a, b):
    return dot_nn(a[0], b[0]) + (dot_nn(a[0], b[1]) + dot_nn(a[1], b[0]))


def muon_kernel(offsets, rate, core, *refs):
    count = len(offsets)
    pieces = refs[: 2 * count]
    mine, weight, updated, moments, gram_now, total = refs[2 * count :]
    size = gram_now.shape[0]
    each = moments.shape[1] // count
    for i, offset in enumerate(offsets):
        part = moments.at[:, i * each : (i + 1) * each]
        spread_pieces(core, pieces[2 * i], pieces[2 * i + 1], part, offset)
    gram = dot_nt(moments[...], moments[...])
    row = lax.broadcasted_iota(jnp.int32, (size, size), 0)
    col = lax.broadcasted_iota(jnp.int32, (size, size), 1)
    same = row == col
    norm = jnp.sqrt(jnp.sum(jnp.where(same, gram, 0.0), keepdims=True)) + 1e-07
    inv = 1.0 / norm
    gram_now[...] = gram * (inv * inv)
    for sweep in range(5):
        now = gram_now[...]
        now_two = split_two(now)
        extra = COEF_SECOND * now + COEF_THIRD * dot3(now_two, now_two)
        extra_two = split_two(extra)
        if sweep == 0:
            total[...] = jnp.where(same, COEF_FIRST + extra, extra)
        else:
            total[...] = COEF_FIRST * total[...] + dot3(extra_two, split_two(total[...]))
        if sweep < 4:
            half = COEF_FIRST * now + dot3(extra_two, now_two)
            gram_now[...] = COEF_FIRST * half + dot3(extra_two, split_two(half))
    total_two = split_two(total[...])
    shrink_by = 1.0 - MUON_RATE * DECAY_RATE
    for i in range(mine.shape[0]):
        step = dot3(total_two, split_two(mine[i])) * (inv * rate)
        if count == 1:
            updated[...] = weight[...] * shrink_by - step.T
        else:
            updated[:, i, :] = weight[:, i, :] * shrink_by - step


def muon(core, sources, full, mine, first, weight):
    size = mine.shape[1]
    count = len(sources)
    moments = full * count
    rate = MUON_RATE * 0.2 * math.sqrt(max(size, moments))
    arrays = [a for source in sources for a in source[:2]]
    whole = lambda a: pl.BlockSpec(a.shape, lambda i, c: (0,) * a.ndim, pipeline_mode=pl.Buffered(1))
    part = pl.BlockSpec((count,) + mine.shape[1:], lambda i, c: (first, 0, 0), pipeline_mode=pl.Buffered(1))
    return pl.pallas_call(
        functools.partial(muon_kernel, [source[2] for source in sources], rate),
        grid_spec=pltpu.PrefetchScalarGridSpec(
            num_scalar_prefetch=1,
            grid=(1,),
            in_specs=[whole(a) for a in arrays] + [part, whole(weight)],
            out_specs=pl.BlockSpec(weight.shape, lambda i, c: (0,) * weight.ndim),
            scratch_shapes=[pltpu.VMEM((size, moments), LOW)] + [pltpu.VMEM((size, size), F32)] * 2,
        ),
        out_shape=jax.ShapeDtypeStruct(weight.shape, F32),
        compiler_params=compiler(48),
        cost_estimate=pl.CostEstimate(
            flops=2 * size * size * (51 * size + moments), bytes_accessed=8 * size * moments, transcendentals=0
        ),
        name="muon_in" if count > 1 else "muon_out",
    )(core, *arrays, mine, weight)


def adam_update(param_now, grad_now, first_old, second_old):
    first_new = BETA_FIRST * first_old + (1.0 - BETA_FIRST) * grad_now
    second_new = BETA_SECOND * second_old + (1.0 - BETA_SECOND) * grad_now * grad_now
    first_hat = first_new / (1.0 - BETA_FIRST**STEP)
    second_hat = second_new / (1.0 - BETA_SECOND**STEP)
    updated = param_now * (1.0 - ADAM_RATE * DECAY_RATE) - ADAM_RATE * first_hat / (
        jnp.sqrt(second_hat) + 1e-08
    )
    return (second_new, updated)


def core_index():
    return lax.axis_index("dp") % 2


def swap_core(part):
    return lax.ppermute(part, "dp", [(i, i ^ 1) for i in range(lax.axis_size("dp"))])


def exchange_mp(parts):
    return lax.all_to_all(parts, "mp", 0, 0)


def send_z(part, step):
    size = lax.axis_size("dp")
    return lax.ppermute(part, "dp", [(i, i ^ (2 * step)) for i in range(size)])


def after(value, *others):
    return lax.optimization_barrier((value, *others))[0]


def copies(part, count):
    return jnp.broadcast_to(part[None], (count,) + part.shape)


def gather_mp(part):
    return exchange_mp(copies(part, lax.axis_size("mp")))


def core_rows(rows, core):
    half = rows.shape[0] // 2
    return lax.dynamic_slice_in_dim(rows, core * half, half, 0)


def regroup(pieces, parts):
    ways, rows, columns = pieces.shape
    shard = columns // parts
    if shard % 128 == 0:
        return [(pieces, i * shard) for i in range(parts)]
    split = pieces.reshape(ways, rows, parts, shard).transpose(2, 1, 0, 3)
    return [(split[i].reshape(1, rows, ways * shard), 0) for i in range(parts)]


def plane_sum(parts):
    return jnp.sum(parts.astype(F32), axis=0)


def depth_sum(main):
    depth = lax.axis_size("dp") // 2
    place = lax.axis_index("dp") // 2
    rows, columns = main.shape
    each = rows // depth
    low = main.astype(LOW)
    parts = [
        send_z(lax.dynamic_slice_in_dim(low, jnp.bitwise_xor(place, step) * each, each, 0), step)
        for step in range(1, depth)
    ]
    mine = lax.dynamic_slice_in_dim(main, place * each, each, 0)
    mine = (mine + sum(p.astype(F32) for p in parts)).astype(LOW)
    parts = [mine] + [send_z(mine, step) for step in range(1, depth)]
    pieces = []
    for piece in range(depth):
        here = parts[piece]
        for other in range(1, depth):
            here = jnp.where(place == other, parts[piece ^ other], here)
        pieces.append(here)
    return jnp.concatenate(pieces, axis=0)


def whole_images(rows, patches, count):
    here, width = rows.shape
    spare = count * patches - here
    if spare:
        odd = lax.axis_index("mp") % 2 == 1
        size = lax.axis_size("mp")
        got = lax.ppermute(rows[:spare], "mp", [(i, i - 1) for i in range(1, size, 2)])
        kept = jnp.concatenate([rows[spare:], jnp.zeros((2 * spare, width), rows.dtype)], axis=0)
        rows = jnp.where(odd, kept, jnp.concatenate([rows, got], axis=0))
    return rows


def held_rows(rows, here):
    spare = rows.shape[0] - here
    if spare:
        odd = lax.axis_index("mp") % 2 == 1
        size = lax.axis_size("mp")
        got = lax.ppermute(rows[here:], "mp", [(i, i + 1) for i in range(0, size, 2)])
        kept = jnp.concatenate([got, rows[: here - spare]], axis=0)
        rows = jnp.where(odd, kept, rows[:here])
    return rows


def per_device(
    tokens,
    cotangent,
    w_in,
    w_out,
    spatial,
    model_vectors,
    gate_vectors,
    patch_bias,
    moment_in,
    moment_out,
    moment_mix,
    first_model,
    second_model,
    first_gate,
    second_gate,
    first_patch,
    second_patch,
):
    here, width = tokens.shape
    shard = w_in.shape[2]
    ways = lax.axis_size("mp")
    full = shard * ways
    patches = spatial.shape[0]
    images = -(-here // patches)
    pad = -(-patches // 16) * 16
    core = core_index()
    core_arg = core.astype(jnp.int32).reshape(1)

    half = width // 2

    gate_wire, rest_wire = weight_wires(core_arg, w_in, w_out, gate_vectors)
    gate_mine = exchange_mp(gate_wire)
    tokens_rows = whole_images(tokens, patches, images)
    cot_rows = whole_images(cotangent, patches, images)
    normed, unit_in, inv_in, cot_pad, normed_t, cot_t = prep(tokens_rows, cot_rows, model_vectors, patches, pad)
    mix = jnp.pad(spatial.astype(LOW), ((0, pad - patches), (0, pad - patches)))
    mix_t = mix.T
    bias = jnp.broadcast_to(jnp.pad(patch_bias, (0, pad - patches))[:, None], (pad, 128))
    gate_mine, mix, mix_t, bias = lax.optimization_barrier((gate_mine, mix, mix_t, bias, normed, rest_wire))[:4]
    rest_mine = exchange_mp(after(rest_wire, gate_mine))
    gate_theirs = swap_core(gate_mine)

    [(gate_mine, _)], [(gate_theirs, _)] = regroup(gate_mine, 1), regroup(gate_theirs, 1)
    normal, unit, slope, scale, w_gate, vec_all = gate_forward(core_arg, normed, gate_mine, gate_theirs, images, pad)
    rest_mine = after(rest_mine, normal)
    rest_theirs = swap_core(rest_mine)
    rest_mine, rest_theirs = (
        (parts[0][0] if parts[0][0] is parts[1][0] else jnp.concatenate([p[0] for p in parts], axis=2))
        for parts in (regroup(rest_mine, 2), regroup(rest_theirs, 2))
    )
    gated, low_value, grad_unit, mine_one, theirs_one, sum_one, sum_two, grad_mix, w_value, w_back = value_both(
        core_arg, normed, cot_pad, normed_t, cot_t, normal, unit, rest_mine, rest_theirs, mix, mix_t, bias, vec_all, images, pad, ways if pad % ways == 0 else 1
    )
    rides = mix_rides(shard, grad_mix)
    wire_one = merge(
        mine_one, swap_core(theirs_one), ways, (grad_mix, swap_core(grad_mix)) if rides else ()
    )
    low_gate, mine_two, theirs_two = gate_back(
        core_arg, normed_t, grad_unit, unit, slope, scale, after(sum_one, wire_one), sum_two
    )
    wire_two = merge(mine_two[None], swap_core(theirs_two)[None], ways)
    parts_one = after(exchange_mp(wire_one), wire_two)
    parts_two = exchange_mp(after(wire_two, parts_one))
    output, grad_tokens, model_sums = token_back(
        tokens_rows, cot_rows, unit_in, inv_in, gated, low_value, after(low_gate, wire_two), w_value, w_gate, w_back, model_vectors, patches, pad
    )

    main_one = depth_sum(plane_sum(parts_one))
    parts_two = after(parts_two, model_sums)
    plane_two = plane_sum(parts_two)
    tail = jnp.pad(model_sums[:3].reshape(-1), (0, EXTRA // 2 * shard - 3 * width)).reshape(EXTRA // 2, shard)
    main_two = jnp.concatenate([plane_two[: half + EXTRA // 2], tail], axis=0)
    main_two = depth_sum(main_two)

    old_one = jnp.concatenate([core_rows(moment_in[:, 0], core), core_rows(moment_out.T, core)], axis=1)
    half_one = MOMENTUM * old_one + main_one[:half].astype(F32)
    mine_one = gather_mp(jnp.concatenate([half_one.astype(LOW), main_one[half:]], axis=0))
    half_two = MOMENTUM * core_rows(moment_in[:, 1], core) + main_two[:half].astype(F32)
    mine_two = jnp.concatenate([half_two.astype(LOW), main_two[half:]], axis=0)
    mine_two = gather_mp(after(mine_two, mine_one))
    grad_w_in, new_moment_in, grad_w_out, new_moment_out, flat = moments(
        core_arg, main_one, swap_core(main_one), main_two, swap_core(main_two), moment_in, moment_out
    )
    theirs_one = swap_core(mine_one)
    pieces_one = [(m[0], t[0], m[1]) for m, t in zip(regroup(mine_one, 2), regroup(theirs_one, 2))]
    new_w_out = muon(core_arg, pieces_one[1:], full, flat, 2, w_out)
    mine_two = after(mine_two, new_w_out, grad_w_in)
    theirs_two = swap_core(mine_two)

    vec_one = main_one[half : half + 2].astype(F32)
    grad_vec = jnp.stack(
        [vec_one[0, :shard], main_two[half].astype(F32), vec_one[0, shard:], vec_one[1, shard:]]
    )
    tails = [jnp.sum(t[:, half + EXTRA // 2 :].astype(F32), axis=0) for t in (mine_two, theirs_two)]
    grad_model = (tails[0] + tails[1]).reshape(-1)[: 3 * width].reshape(3, width)
    if rides:
        each = grad_mix.shape[1] // 2
        rows = mine_one[:, half + MIX_ROW : half + MIX_ROW + each].astype(F32)
        cuts = [rows[:, :, at : at + grad_mix.shape[2]] for at in (0, shard)]
        grad_mix = jnp.concatenate(cuts, axis=1)
    else:
        grad_mix = lax.psum(grad_mix, ("dp", "mp"))
    grad_mix = grad_mix.reshape(pad, -1)
    grad_spatial = grad_mix[:patches, :patches]
    grad_patch = grad_mix[:patches, pad]

    pieces_two = [(m[0], t[0], m[1]) for m, t in zip(regroup(mine_two, 1), regroup(theirs_two, 1))]
    new_w_in = muon(core_arg, [pieces_one[0], pieces_two[0]], full, flat, 0, w_in)
    new_moment_mix = MOMENTUM * moment_mix + grad_spatial

    shrink_by = 1.0 - MUON_RATE * DECAY_RATE
    new_spatial = spatial * shrink_by - MUON_RATE * 0.2 * math.sqrt(patches) * square_muon(new_moment_mix)
    new_second_model, new_model = adam_update(model_vectors, grad_model, first_model, second_model)
    new_second_gate, new_gate = adam_update(gate_vectors, grad_vec, first_gate, second_gate)
    new_second_patch, new_patch = adam_update(patch_bias, grad_patch, first_patch, second_patch)
    return (
        held_rows(output, here),
        held_rows(grad_tokens, here),
        grad_w_in,
        grad_w_out,
        grad_spatial,
        grad_model,
        grad_vec,
        grad_patch,
        new_moment_in,
        new_moment_out,
        new_moment_mix,
        new_second_model,
        new_second_gate,
        new_second_patch,
        new_w_in,
        new_w_out,
        new_spatial,
        new_model,
        new_gate,
        new_patch,
    )


def solution(mesh):
    rows = P(("dp", "mp"), None)
    wide = P(None, None, "mp")
    tall = P("mp", None)
    columns = P(None, "mp")
    return jax.shard_map(
        per_device,
        mesh=mesh,
        in_specs=(
            (rows, rows, wide, tall, P(), P(), columns, P())
            + (wide, tall, P(), P(), P(), columns, columns, P(), P())
        ),
        out_specs=(
            (rows, rows, wide, tall, P(), P(), columns, P())
            + (wide, tall, P(), P(), columns, P())
            + (wide, tall, P(), P(), columns, P())
        ),
        check_vma=False,
    )
```

```python
import functools
import math

import jax
import jax.numpy as jnp
from jax import lax
from jax.experimental import pallas as pl
from jax.experimental.pallas import tpu as pltpu
from jax.sharding import PartitionSpec as P

STEP = 10
EPSILON = 1e-05
COEF_FIRST = 3.4445
COEF_SECOND = -4.775
COEF_THIRD = 2.0315
MOMENTUM = 0.95
MUON_RATE = 0.2
ADAM_RATE = 0.3
DECAY_RATE = 0.01
BETA_FIRST = 0.9
BETA_SECOND = 0.95
LOW = jnp.bfloat16
F32 = jnp.float32


ROW_TILE = 16
UNROLL = 3
EXTRA = 32
MIX_ROW = 4
CHUNK = 512
CUBIC = 0.044715
SLOPE = math.sqrt(2.0 / math.pi)


def compiler(megabytes):
    return pltpu.CompilerParams(vmem_limit_bytes=megabytes << 20)


def dot_nn(a, b):
    return jnp.dot(a, b, preferred_element_type=F32)


def dot_nt(a, b):
    return lax.dot_general(a, b, (((1,), (1,)), ((), ())), preferred_element_type=F32)


def gelu_pair(hidden):
    square = hidden * hidden
    half = 0.5 + 0.5 * jnp.tanh(hidden * (SLOPE + (SLOPE * CUBIC) * square))
    active = hidden * half
    slope = half + (active - active * half) * (2.0 * SLOPE + (6.0 * SLOPE * CUBIC) * square)
    return active, slope


def lanes(v):
    total = v[:, :128]
    for at in range(128, v.shape[1], 128):
        total = total + v[:, at : at + 128]
    return total


def eights(v):
    total = v[:8]
    for at in range(8, v.shape[0], 8):
        total = total + v[at : at + 8]
    return total


def wide(v, width):
    return jnp.concatenate([v] * (width // 128), axis=1) if width % 128 == 0 else v[:, :1]


def tiles(count, body, carry=None):
    def step(i, kept):
        return body(pl.ds(pl.multiple_of(i * ROW_TILE, ROW_TILE), ROW_TILE), kept)

    return lax.fori_loop(0, count // ROW_TILE, step, carry, unroll=UNROLL)


def spread_pieces(core, mine, theirs, out, offset):
    half = out.shape[0] // 2
    count = mine.shape[0]
    shard = out.shape[1] // count
    first = pl.ds(pl.multiple_of(core[0] * half, half), half)
    other = pl.ds(pl.multiple_of((1 - core[0]) * half, half), half)
    for piece in range(count):
        cols = slice(piece * shard, (piece + 1) * shard)
        out[first, cols] = mine[piece, :half, offset : offset + shard]
        out[other, cols] = theirs[piece, :half, offset : offset + shard]


def gate_kernel(chunk, core, normed, mine, theirs, normal, unit, slope, scale, weight, vec, active):
    rows, full = active.shape
    half = weight.shape[0] // 2

    @pl.when(pl.program_id(0) == 0)
    def _():
        spread_pieces(core, mine, theirs, weight, 0)
        count, _, shard = mine.shape
        for piece in range(count):
            terms = mine[piece, half:, :].astype(F32)
            vec[:, piece * shard : (piece + 1) * shard] = (terms[0:8] + terms[8:16]) + terms[16:24]

    starts = range(0, full, chunk)
    for at in starts:
        active[:, at : at + chunk] = dot_nn(normed[...], weight[:, at : at + chunk])

    def act(here, _):
        total = jnp.zeros((ROW_TILE, 128), F32)
        for at in starts:
            cols = slice(at, at + chunk)
            value, grad = gelu_pair(active[here, cols] + vec[1:2, cols])
            active[here, cols] = value
            slope[here, cols] = grad.astype(LOW)
            total = total + lanes(value)
        scale[here, :] = total

    tiles(rows, act)
    mean = jnp.sum(scale[...], axis=1, keepdims=True) * (1.0 / full)
    scale[...] = jnp.broadcast_to(mean, scale.shape)

    def spread(here, _):
        total = jnp.zeros((ROW_TILE, 128), F32)
        mean_here = wide(scale[here, :], chunk)
        for at in starts:
            cols = slice(at, at + chunk)
            centred = active[here, cols] - mean_here
            active[here, cols] = centred
            total = total + lanes(centred * centred)
        scale[here, :] = total

    tiles(rows, spread)
    var = jnp.sum(scale[...], axis=1, keepdims=True) * (1.0 / full)
    scale[...] = jnp.broadcast_to(lax.rsqrt(var + EPSILON), scale.shape)

    def finish(here, _):
        inv = wide(scale[here, :], chunk)
        for at in starts:
            cols = slice(at, at + chunk)
            unit_here = active[here, cols] * inv
            unit[here, cols] = unit_here.astype(LOW)
            normal[here, cols] = (unit_here * vec[2:3, cols] + vec[3:4, cols]).astype(LOW)

    tiles(rows, finish)


def gate_forward(core, normed, mine, theirs, images, pad):
    count, _, shard = mine.shape
    full = count * shard
    width = normed.shape[1]
    chunk = 512 if full % 512 == 0 else full
    total = images * pad
    whole = lambda a: pl.BlockSpec(a.shape, lambda i, c: (0,) * a.ndim, pipeline_mode=pl.Buffered(1))
    rows = lambda n: pl.BlockSpec((pad, n), lambda i, c: (i, 0))
    fixed = lambda *f: pl.BlockSpec(f, lambda i, c: (0, 0))
    shape = jax.ShapeDtypeStruct
    return pl.pallas_call(
        functools.partial(gate_kernel, chunk),
        grid_spec=pltpu.PrefetchScalarGridSpec(
            num_scalar_prefetch=1,
            grid=(images,),
            in_specs=[rows(width), whole(mine), whole(theirs)],
            out_specs=[rows(full), rows(full), rows(full), rows(128), fixed(width, full), fixed(8, full)],
            scratch_shapes=[pltpu.VMEM((pad, full), F32)],
        ),
        out_shape=[shape((total, full), LOW)] * 3
        + [shape((total, 128), F32), shape((width, full), LOW), shape((8, full), F32)],
        compiler_params=compiler(60),
        cost_estimate=pl.CostEstimate(
            flops=2 * total * width * full, bytes_accessed=8 * total * full, transcendentals=total * full
        ),
        name="gate_forward",
    )(core, normed, mine, theirs)


def value_kernel(
    pad,
    images,
    core,
    normed,
    cot,
    normed_t,
    cot_t,
    normal,
    unit,
    slope_gate,
    scale,
    w_mine,
    w_theirs,
    mix,
    mix_t,
    bias,
    vec,
    gated,
    low_value,
    low_gate,
    mine,
    theirs,
    mine_gate,
    theirs_gate,
    mix_pieces,
    w_value,
    w_back,
    sums,
    grad_mix,
    grad_bias,
    grad_unit,
    hidden,
    back,
    mixed,
    turned,
    low_mixed,
    low_pad,
    gated_pad,
):
    total, chunk = gated.shape
    half = w_value.shape[0] // 2
    step = pl.program_id(0)
    count = pl.num_programs(0) // 2
    cols = pl.ds(pl.multiple_of(lax.rem(step, count) * chunk, chunk), chunk)

    @pl.when(step == 0)
    def _():
        offset = w_mine.shape[2] - w_value.shape[1] // w_mine.shape[0]
        spread_pieces(core, w_mine, w_theirs, w_value, 0)
        spread_pieces(core, w_mine, w_theirs, w_back, offset)
        sums[...] = jnp.zeros_like(sums)
        grad_mix[...] = jnp.zeros_like(grad_mix)
        grad_bias[...] = jnp.zeros_like(grad_bias)
        low_pad[total:, :] = jnp.zeros_like(low_pad[total:, :])
        gated_pad[total:, :] = jnp.zeros_like(gated_pad[total:, :])

    pairs = ((hidden.at[0], back.at[0], mixed.at[0]), (hidden.at[1], back.at[1], mixed.at[1]))

    def products(image):
        here = slice(image * pad, (image + 1) * pad)
        hid, bck, mxd = pairs[image % 2]
        hid[...] = dot_nn(normed[here, :], w_value[:, cols])
        bck[...] = dot_nn(cot[here, :], w_back[:, cols])
        mxd[...] = dot_nn(mix[...], normal[here, :])

    def forward(image, sums):
        hid, bck, mxd = pairs[image % 2]
        for row in range(0, pad, ROW_TILE):
            at = slice(row, row + ROW_TILE)
            here = slice(image * pad + row, image * pad + row + ROW_TILE)
            value, slope = gelu_pair(hid[at, :] + vec[0:1, :])
            mixed_here = mxd[at, :] + wide(bias[at, :], chunk)
            back_here = bck[at, :]
            gated_here = (value * mixed_here).astype(LOW)
            gated[here, :] = gated_here
            gated_pad[here, :] = gated_here
            grad_here = (back_here * value).astype(LOW)
            low_mixed[image % 2, at, :] = grad_here
            grad_bias[at, :] += lanes(grad_here.astype(F32))
            low_here = (back_here * mixed_here * slope).astype(LOW)
            low_value[here, :] = low_here
            low_pad[here, :] = low_here
            sums = sums + eights(low_here.astype(F32))
        return sums

    def turn(image):
        here = slice(image * pad, (image + 1) * pad)
        turned[image % 2] = dot_nn(mix_t[...], low_mixed[image % 2])
        grad_mix[:, :pad] += dot_nt(low_mixed[image % 2], normal[here, :])

    def backward(image, kept):
        for row in range(0, pad, ROW_TILE):
            at = slice(row, row + ROW_TILE)
            here = slice(image * pad + row, image * pad + row + ROW_TILE)
            grad = turned[image % 2, at, :]
            unit_here = unit[here, :].astype(F32)
            gain = vec[2:3, :]
            both = grad * unit_here
            du = grad * gain
            grad_unit[here, cols] = du.astype(LOW)
            sums[0, here, :] += lanes(du)
            sums[1, here, :] += lanes(both * gain)
            kept = kept[0] + eights(both), kept[1] + eights(grad)
        return kept

    @pl.when(step < count)
    def _():
        zero = jnp.zeros((8, chunk), F32)
        bias_sum, norm_sums = zero, (zero, zero)
        products(0)
        for image in range(images):
            if image + 1 < images:
                products(image + 1)
            bias_sum = forward(image, bias_sum)
            turn(image)
            if image:
                norm_sums = backward(image - 1, norm_sums)
        norm_sums = backward(images - 1, norm_sums)
        gain_sum, shift_sum = norm_sums

        for i, product in enumerate((dot_nn(normed_t[...], low_pad[...]), dot_nn(cot_t[...], gated_pad[...]))):
            mine[i, :half, :] = product[:half]
            theirs[i, :half, :] = product[half:].astype(LOW)

        total_of = lambda v: jnp.sum(v, axis=0, keepdims=True)
        more = mine.shape[1] - half
        rows = lax.broadcasted_iota(jnp.int32, (more, chunk), 0)
        first_rows = jnp.where(rows == 0, total_of(bias_sum), 0.0)
        second_rows = jnp.where(rows == 0, total_of(gain_sum), jnp.where(rows == 1, total_of(shift_sum), 0.0))
        for i, both_rows in enumerate((first_rows, second_rows)):
            mine[i, half:, :] = both_rows.astype(LOW).astype(F32)
            theirs[i, half:, :] = both_rows.astype(LOW)

    @pl.when(step == count - 1)
    def _():
        patch = jnp.sum(grad_bias[...], axis=1, keepdims=True)
        grad_mix[:, pad:] = jnp.broadcast_to(patch, (pad, grad_mix.shape[1] - pad))
        each = mix_pieces.shape[1]
        for piece in range(mix_pieces.shape[0]):
            mix_pieces[piece] = grad_mix[piece * each : (piece + 1) * each, :]


    def gate_tile(i, total_here):
        here = slice(i * ROW_TILE, (i + 1) * ROW_TILE)
        one = wide(sums[0, here, :], chunk)
        two = wide(sums[1, here, :], chunk)
        inv = wide(scale[here, :], chunk)
        grad = inv * (grad_unit[here, cols].astype(F32) - one - unit[here, :].astype(F32) * two)
        low = (grad * slope_gate[here, :].astype(F32)).astype(LOW)
        low_gate[here, :] = low
        low_pad[here, :] = low
        return total_here + eights(low.astype(F32))

    @pl.when(step == count)
    def _():
        for i in range(2):
            mean = jnp.sum(sums[i], axis=1, keepdims=True) * (1.0 / w_value.shape[1])
            sums[i] = jnp.broadcast_to(mean, (total, 128))

    @pl.when(step >= count)
    def _():
        kept = jnp.zeros((8, chunk), F32)
        for at in range(total // ROW_TILE):
            kept = gate_tile(at, kept)
        more = mine_gate.shape[0] - half
        row = lax.broadcasted_iota(jnp.int32, (more, chunk), 0)
        rows = jnp.where(row == 0, jnp.sum(kept, axis=0, keepdims=True), 0.0)
        mine_gate[half:, :] = rows.astype(LOW).astype(F32)
        theirs_gate[half:, :] = rows.astype(LOW)
        product = dot_nn(normed_t[...], low_pad[...])
        mine_gate[:half, :] = product[:half]
        theirs_gate[:half, :] = product[half:].astype(LOW)


def channels_both(
    core, normed, cot, normed_t, cot_t, normal, unit, slope, scale, w_mine, w_theirs, mix, mix_t, bias, vec, images, pad, ways
):
    width = normed.shape[1]
    full = normal.shape[1]
    total = images * pad
    deep = normed_t.shape[1]
    chunk = CHUNK if full % CHUNK == 0 else full
    count = full // chunk
    half = width // 2
    more = half + EXTRA
    wide_mix = -(-(pad + 1) // 128) * 128
    mix_shape = (ways, pad // ways, wide_mix)
    whole = lambda a: pl.BlockSpec(a.shape, lambda i, c: (0,) * a.ndim, pipeline_mode=pl.Buffered(1))
    early = lambda n: pl.BlockSpec((n, chunk), lambda i, c: (0, jnp.minimum(i, count - 1)))
    late = lambda n: pl.BlockSpec((n, chunk), lambda i, c: (0, jnp.maximum(i - count, 0)))
    twice = lambda n: pl.BlockSpec((n, chunk), lambda i, c: (0, lax.rem(i, count)))
    pair = pl.BlockSpec((2, more, chunk), lambda i, c: (0, 0, jnp.minimum(i, count - 1)))
    shape = jax.ShapeDtypeStruct
    return pl.pallas_call(
        functools.partial(value_kernel, pad, images),
        grid_spec=pltpu.PrefetchScalarGridSpec(
            num_scalar_prefetch=1,
            grid=(2 * count,),
            in_specs=[whole(normed), whole(cot), whole(normed_t), whole(cot_t)]
            + [early(total), twice(total), late(total), whole(scale), whole(w_mine), whole(w_theirs)]
            + [whole(mix), whole(mix_t), whole(bias), early(8)],
            out_specs=[early(total), early(total), late(total), pair, pair, late(more), late(more)]
            + [pl.BlockSpec(mix_shape, lambda i, c: (0, 0, 0))],
            scratch_shapes=[pltpu.VMEM((width, full), LOW)] * 2
            + [pltpu.VMEM((2, total, 128), F32), pltpu.VMEM((pad, wide_mix), F32), pltpu.VMEM((pad, 128), F32)]
            + [pltpu.VMEM((total, full), LOW)]
            + [pltpu.VMEM((2, pad, chunk), F32)] * 4
            + [pltpu.VMEM((2, pad, chunk), LOW)]
            + [pltpu.VMEM((deep, chunk), LOW)] * 2,
        ),
        out_shape=[shape((total, full), LOW)] * 3
        + [shape((2, more, full), F32), shape((2, more, full), LOW)]
        + [shape((more, full), F32), shape((more, full), LOW), shape(mix_shape, F32)],
        compiler_params=compiler(60),
        cost_estimate=pl.CostEstimate(
            flops=14 * total * width * full, bytes_accessed=24 * total * full, transcendentals=total * full
        ),
        name="channels_both",
    )(core, normed, cot, normed_t, cot_t, normal, unit, slope, scale, w_mine, w_theirs, mix, mix_t, bias, vec)


def gate_wire_kernel(core, w_in, vectors, wire):
    half, _, shard = w_in.shape
    low = w_in[:, 1, :].astype(LOW)
    value = jnp.concatenate([vectors[...], jnp.zeros((4, shard), F32)], axis=0)
    high = value.astype(LOW).astype(F32)
    middle = (value - high).astype(LOW).astype(F32)
    last = value - high - middle
    terms = jnp.concatenate([high, middle, last, jnp.zeros((8, shard), F32)], axis=0).astype(LOW)
    for receiver in range(wire.shape[0]):
        wire[receiver, :half, :] = low
        wire[receiver, half:, :] = terms


def rest_wire_kernel(core, w_in, w_out, wire):
    shard = w_in.shape[2]
    value = w_in[:, 0, :].astype(LOW)
    back = w_out[...].T.astype(LOW)
    for receiver in range(wire.shape[0]):
        wire[receiver, :, :shard] = value
        wire[receiver, :, shard:] = back


def weight_wires(core, w_in, w_out, vectors):
    width, _, shard = w_in.shape
    half = width // 2
    ways = lax.axis_size("mp")
    rows = pl.BlockSpec((half, 2, shard), lambda i, c: (c[0], 0, 0))
    fixed = lambda *f: pl.BlockSpec(f, lambda i, c: (0,) * len(f))
    spec = lambda ins, out: pltpu.PrefetchScalarGridSpec(
        num_scalar_prefetch=1, grid=(1,), in_specs=ins, out_specs=fixed(*out)
    )
    out = (ways, half + 32, shard)
    gate = pl.pallas_call(
        gate_wire_kernel,
        grid_spec=spec([rows, fixed(4, shard)], out),
        out_shape=jax.ShapeDtypeStruct(out, LOW),
        compiler_params=compiler(60),
        name="gate_wire",
    )(core, w_in, vectors)
    out = (ways, half, 2 * shard)
    if shard % 128:
        back = lax.dynamic_slice_in_dim(w_out, core[0] * half, half, 1)
        rest = jnp.concatenate([core_rows(w_in[:, 0], core[0]), back.T], axis=1).astype(LOW)
        return gate, copies(rest, ways)
    rest = pl.pallas_call(
        rest_wire_kernel,
        grid_spec=spec([rows, pl.BlockSpec((shard, half), lambda i, c: (0, c[0]))], out),
        out_shape=jax.ShapeDtypeStruct(out, LOW),
        compiler_params=compiler(60),
        name="rest_wire",
    )(core, w_in, w_out)
    return gate, rest


def merge_kernel(mine, theirs, mine_gate, theirs_gate, *refs):
    wire = refs[-1]
    _, rows, shard = mine.shape
    parts = ((mine.at[0], theirs.at[0]), (mine_gate, theirs_gate), (mine.at[1], theirs.at[1]))
    for i, (own, other) in enumerate(parts):
        wire[0, :, i * shard : (i + 1) * shard] = (own[...] + other[...].astype(F32)).astype(LOW)
    if len(refs) > 1:
        mix = refs[0][0]
        each = mix.shape[0]
        top = rows - EXTRA
        high = mix.astype(LOW).astype(F32)
        for i, part in enumerate((high, mix - high)):
            own, other = parts[i]
            block = (own[top:, :] + other[top:, :].astype(F32))[:, : mix.shape[1]]
            block = jnp.concatenate([block[:MIX_ROW], part, block[MIX_ROW + each :]], axis=0)
            wire[0, top:, i * shard : i * shard + mix.shape[1]] = block.astype(LOW)


def merge(mine, theirs, mine_gate, theirs_gate, ways, mix):
    _, rows, full = mine.shape
    shard = full // ways
    if shard % 128:
        both = mine + theirs.astype(F32)
        both = jnp.stack([both[0], mine_gate + theirs_gate.astype(F32), both[1]])
        blocks = both.reshape(3, rows, ways, shard).transpose(2, 1, 0, 3)
        return blocks.reshape(ways, rows, 3 * shard).astype(LOW)
    pair = pl.BlockSpec((2, rows, shard), lambda i: (0, 0, i))
    block = pl.BlockSpec((rows, shard), lambda i: (0, i))
    return pl.pallas_call(
        merge_kernel,
        grid=(ways,),
        in_specs=[pair, pair, block, block] + [pl.BlockSpec((1,) + m.shape[1:], lambda i: (i, 0, 0)) for m in mix],
        out_specs=pl.BlockSpec((1, rows, 3 * shard), lambda i: (i, 0, 0)),
        out_shape=jax.ShapeDtypeStruct((ways, rows, 3 * shard), LOW),
        compiler_params=compiler(60),
        name="merge",
    )(mine, theirs, mine_gate, theirs_gate, *mix)


def mix_rides(shard, mix):
    return shard % 128 == 0 and mix.shape[2] <= shard and mix.shape[0] > 1 and mix.shape[1] % 2 == 0 and (
        mix.shape[1] // 2 + MIX_ROW <= EXTRA
    )


def moment_wire_kernel(core, main, old_in, old_out, wire):
    half, _, shard = old_in.shape
    part = lambda i: main[:half, i * shard : (i + 1) * shard].astype(F32)
    out = (MOMENTUM * old_out[...].T + part(2)).astype(LOW)
    value = (MOMENTUM * old_in[:, 0, :] + part(0)).astype(LOW)
    gate = (MOMENTUM * old_in[:, 1, :] + part(1)).astype(LOW)
    for receiver in range(wire.shape[0]):
        for i, rows in enumerate((value, gate, out)):
            wire[receiver, :half, i * shard : (i + 1) * shard] = rows
        wire[receiver, half:, :] = main[half:, :]


def moment_wires(core, main, old_in, old_out):
    width, _, shard = old_in.shape
    half = width // 2
    fixed = lambda *f: pl.BlockSpec(f, lambda i, c: (0,) * len(f))
    out = (lax.axis_size("mp"),) + main.shape
    return pl.pallas_call(
        moment_wire_kernel,
        grid_spec=pltpu.PrefetchScalarGridSpec(
            num_scalar_prefetch=1,
            grid=(1,),
            in_specs=[
                fixed(*main.shape),
                pl.BlockSpec((half, 2, shard), lambda i, c: (c[0], 0, 0)),
                pl.BlockSpec((shard, half), lambda i, c: (0, c[0])),
            ],
            out_specs=fixed(*out),
        ),
        out_shape=jax.ShapeDtypeStruct(out, LOW),
        compiler_params=compiler(60),
        name="moment_wires",
    )(core, main, old_in, old_out)


def moments_kernel(core, main, other, old_in, old_out, grad_in, new_in, grad_out, new_out, flat):
    width, _, shard = old_in.shape
    half = width // 2
    rows = (
        pl.ds(pl.multiple_of(core[0] * half, half), half),
        pl.ds(pl.multiple_of((1 - core[0]) * half, half), half),
    )
    for here, part in ((rows[0], main), (rows[1], other)):
        for i in range(3):
            flat[i, here, :] = part[:half, i * shard : (i + 1) * shard].astype(F32)
    for i in range(2):
        grad = flat[i]
        grad_in[:, i, :] = grad
        moment = MOMENTUM * old_in[:, i, :] + grad
        new_in[:, i, :] = moment
        flat[i] = moment
    grad = flat[2].T
    grad_out[...] = grad
    moment = MOMENTUM * old_out[...] + grad
    new_out[...] = moment
    flat[2] = moment.T


def moments(core, main, other, old_in, old_out):
    width, _, shard = old_in.shape
    ins = (main, other, old_in, old_out)
    shapes = (width, 2, shard), (width, 2, shard), (shard, width), (shard, width), (3, width, shard)
    fixed = lambda f: pl.BlockSpec(f, lambda i, c, n=len(f): (0,) * n)
    return pl.pallas_call(
        moments_kernel,
        grid_spec=pltpu.PrefetchScalarGridSpec(
            num_scalar_prefetch=1,
            grid=(1,),
            in_specs=[fixed(a.shape) for a in ins],
            out_specs=[fixed(f) for f in shapes],
        ),
        out_shape=[jax.ShapeDtypeStruct(f, F32) for f in shapes],
        compiler_params=compiler(60),
        name="moments",
    )(core, *ins)


def prep_kernel(patches, pad, core, tokens, cot, model, normed, unit, scale, cot_pad, normed_t, cot_t, keep):
    step = pl.program_id(0)
    group = tokens.shape[1] // patches
    rows = group * pad
    width = tokens.shape[2]

    def padded(block):
        block = block[0].astype(F32)
        gap = jnp.zeros((pad - patches, width), F32)
        parts = []
        for image in range(group):
            parts += [block[image * patches : (image + 1) * patches], gap]
        return jnp.concatenate(parts, axis=0)

    here = pl.ds(pl.multiple_of(step * rows, rows), rows)

    @pl.when(step == 0)
    def _():
        keep[...] = jnp.zeros_like(keep)

    cot_here = padded(cot)
    cot_pad[...] = cot_here.astype(LOW)
    keep[1, here, :] = cot_here
    x = padded(tokens)
    centred = x - jnp.sum(x, axis=1, keepdims=True) * (1.0 / width)
    inv = lax.rsqrt(jnp.sum(centred * centred, axis=1, keepdims=True) * (1.0 / width) + EPSILON)
    unit_here = centred * inv
    scale[...] = jnp.broadcast_to(inv, scale.shape)
    unit[...] = unit_here.astype(LOW)
    low = (unit_here * model[0:1, :] + model[1:2, :]).astype(LOW)
    normed[...] = low
    keep[0, here, :] = low.astype(F32)

    @pl.when(step == pl.num_programs(0) - 1)
    def _():
        half = width // 2
        for i, place in enumerate((core[0], 1 - core[0])):
            features = pl.ds(pl.multiple_of(place * half, half), half)
            rows_out = slice(i * half, (i + 1) * half)
            for at in range(0, normed_t.shape[1], 128):
                cols = slice(at, at + 128)
                normed_t[rows_out, cols] = keep[0, cols, features].T.astype(LOW)
                cot_t[rows_out, cols] = keep[1, cols, features].T.astype(LOW)


def prep(core, tokens, cot, model, patches, pad):
    here, width = tokens.shape
    images = here // patches
    group = 2 if images % 2 == 0 else images
    steps = images // group
    total = images * pad
    deep = -(-total // 128) * 128
    block = pl.BlockSpec((1, group * patches, width), lambda i, c: (i, 0, 0))
    rows = lambda n: pl.BlockSpec((group * pad, n), lambda i, c: (i, 0))
    fixed = lambda *f: pl.BlockSpec(f, lambda i, c: (0, 0))
    shape = jax.ShapeDtypeStruct
    return pl.pallas_call(
        functools.partial(prep_kernel, patches, pad),
        grid_spec=pltpu.PrefetchScalarGridSpec(
            num_scalar_prefetch=1,
            grid=(steps,),
            in_specs=[block, block, fixed(3, width)],
            out_specs=[rows(width), rows(width), rows(128), rows(width), fixed(width, deep), fixed(width, deep)],
            scratch_shapes=[pltpu.VMEM((2, deep, width), F32)],
        ),
        out_shape=[
            shape((total, width), LOW),
            shape((total, width), LOW),
            shape((total, 128), F32),
            shape((total, width), LOW),
            shape((width, deep), LOW),
            shape((width, deep), LOW),
        ],
        compiler_params=compiler(60),
        cost_estimate=pl.CostEstimate(flops=20 * total * width, bytes_accessed=20 * total * width, transcendentals=total),
        name="prep",
    )(core, tokens.reshape(steps, group * patches, width), cot.reshape(steps, group * patches, width), model)


def token_kernel(
    patches,
    pad,
    core,
    tokens,
    cot,
    unit,
    scale,
    gated,
    low_value,
    low_gate,
    w_mine,
    w_theirs,
    w_gate,
    model,
    output,
    grad_tokens,
    sums,
    w_value,
    w_back,
    branch,
    grad,
):
    group = tokens.shape[1] // patches
    width = tokens.shape[2]
    rows = group * pad

    @pl.when(pl.program_id(0) == 0)
    def _():
        sums[...] = jnp.zeros_like(sums)
        offset = w_mine.shape[2] - w_value.shape[1] // w_mine.shape[0]
        spread_pieces(core, w_mine, w_theirs, w_value, 0)
        spread_pieces(core, w_mine, w_theirs, w_back, offset)

    def packed(v):
        return jnp.concatenate([v[i * pad : i * pad + patches] for i in range(group)], axis=0)

    branch[...] = dot_nt(gated[...], w_back[...])
    output[0] = (tokens[0].astype(F32) + packed(branch) + model[2:3, :]).astype(LOW)
    grad[...] = dot_nt(low_value[...], w_value[...]) + dot_nt(low_gate[...], w_gate[...])

    def back(i, kept):
        here = pl.ds(pl.multiple_of(i * ROW_TILE, ROW_TILE), ROW_TILE)
        grad_here = grad[here, :]
        unit_here = unit[here, :].astype(F32)
        both = grad_here * unit_here
        du = grad_here * model[0:1, :]
        first = jnp.sum(du, axis=1, keepdims=True) * (1.0 / width)
        second = jnp.sum(both * model[0:1, :], axis=1, keepdims=True) * (1.0 / width)
        branch[here, :] = wide(scale[here, :], width) * (du - first - unit_here * second)
        return kept[0] + eights(both), kept[1] + eights(grad_here)

    zero = jnp.zeros((8, width), F32)
    gain, shift = lax.fori_loop(0, rows // ROW_TILE, back, (zero, zero), unroll=2)
    cot_here = cot[0].astype(F32)
    grad_tokens[0] = (cot_here + packed(branch)).astype(LOW)
    sums[0:1, :] += jnp.sum(gain, axis=0, keepdims=True)
    sums[1:2, :] += jnp.sum(shift, axis=0, keepdims=True)
    sums[2:3, :] += jnp.sum(eights(cot_here), axis=0, keepdims=True)


def token_back(core, tokens, cot, unit, scale, gated, low_value, low_gate, w_mine, w_theirs, w_gate, model, patches, pad):
    here, width = tokens.shape
    full = w_gate.shape[1]
    images = here // patches
    group = 2 if images % 2 == 0 else images
    steps = images // group
    total = images * pad
    block = pl.BlockSpec((1, group * patches, width), lambda i, c: (i, 0, 0))
    rows = lambda n: pl.BlockSpec((group * pad, n), lambda i, c: (i, 0))
    whole = lambda a: pl.BlockSpec(a.shape, lambda i, c: (0,) * a.ndim, pipeline_mode=pl.Buffered(1))
    shape = jax.ShapeDtypeStruct
    output, grad_tokens, sums = pl.pallas_call(
        functools.partial(token_kernel, patches, pad),
        grid_spec=pltpu.PrefetchScalarGridSpec(
            num_scalar_prefetch=1,
            grid=(steps,),
            in_specs=[block, block, rows(width), rows(128), rows(full), rows(full), rows(full)]
            + [whole(w_mine), whole(w_theirs), whole(w_gate), whole(model)],
            out_specs=[block, block, pl.BlockSpec((8, width), lambda i, c: (0, 0))],
            scratch_shapes=[pltpu.VMEM((width, full), LOW)] * 2 + [pltpu.VMEM((group * pad, width), F32)] * 2,
        ),
        out_shape=[shape((steps, group * patches, width), LOW)] * 2 + [shape((8, width), F32)],
        compiler_params=compiler(60),
        cost_estimate=pl.CostEstimate(
            flops=6 * total * width * full, bytes_accessed=8 * total * full, transcendentals=0
        ),
        name="token_back",
    )(
        core,
        tokens.reshape(steps, group * patches, width),
        cot.reshape(steps, group * patches, width),
        unit, scale, gated, low_value, low_gate, w_mine, w_theirs, w_gate, model,
    )
    return output.reshape(here, width), grad_tokens.reshape(here, width), sums


def split_two(v):
    high = v.astype(LOW)
    return high, (v - high.astype(F32)).astype(LOW)


def dot3(a, b):
    return dot_nn(a[0], b[0]) + (dot_nn(a[0], b[1]) + dot_nn(a[1], b[0]))


def polynomial_kernel(own, given, count, rates, core, *refs):
    arrays = refs[:count]
    square, poly, square_out, moments, gram_now, total, now = refs[count:]
    size = gram_now.shape[0]
    full = moments.shape[1] // 2
    half = size // 2
    first = pl.ds(pl.multiple_of(core[0] * half, half), half)
    other = pl.ds(pl.multiple_of((1 - core[0]) * half, half), half)

    def spread(rows, source, slot):
        pieces, offset = arrays[source[0]], source[1]
        shard = full // pieces.shape[0]
        for piece in range(pieces.shape[0]):
            at = slot * full + piece * shard
            moments[rows, at : at + shard] = pieces[piece, :half, offset : offset + shard]

    spread(other, given[0], 0)
    spread(other, given[1], 1)

    @pl.when(core[0] == 0)
    def _():
        spread(first, own[2], 0)
        moments[:, full:] = jnp.zeros((size, full), LOW)

    @pl.when(core[0] == 1)
    def _():
        spread(first, own[0], 0)
        spread(first, own[1], 1)

    few = square.shape[0]
    now[...] = jnp.zeros_like(now)
    start = square[...]
    now[:few, :few] = start / (jnp.sqrt(jnp.sum(start * start, keepdims=True)) + 1e-07)

    gram = dot_nt(moments[...], moments[...])
    row = lax.broadcasted_iota(jnp.int32, (size, size), 0)
    col = lax.broadcasted_iota(jnp.int32, (size, size), 1)
    same = row == col
    norm = jnp.sqrt(jnp.sum(jnp.where(same, gram, 0.0), keepdims=True)) + 1e-07
    inv = 1.0 / norm
    gram_now[...] = gram * (inv * inv)
    for sweep in range(5):
        x = now[...]
        x_two = split_two(x)
        small = dot_nt(x_two[0], x_two[0]) + (dot_nt(x_two[0], x_two[1]) + dot_nt(x_two[1], x_two[0]))
        small_two = split_two(small)
        matrix = gram_now[...]
        matrix_two = split_two(matrix)
        extra = COEF_SECOND * matrix + COEF_THIRD * dot3(matrix_two, matrix_two)
        extra_two = split_two(extra)
        small_extra = COEF_SECOND * small + COEF_THIRD * dot3(small_two, small_two)
        now[...] = COEF_FIRST * x + dot3(split_two(small_extra), x_two)
        if sweep == 0:
            total[...] = jnp.where(same, COEF_FIRST + extra, extra)
        else:
            total[...] = COEF_FIRST * total[...] + dot3(extra_two, split_two(total[...]))
        if sweep < 4:
            partial = COEF_FIRST * matrix + dot3(extra_two, matrix_two)
            gram_now[...] = COEF_FIRST * partial + dot3(extra_two, split_two(partial))
    rate = jnp.where(core[0] == 0, rates[0], rates[1])
    poly[...] = total[...] * (inv * rate)
    square_out[...] = now[:few, :few]


def polynomials(core, own, given, full, square, size):
    arrays = []

    def place(source):
        for i, array in enumerate(arrays):
            if array is source[0]:
                return i, source[1]
        arrays.append(source[0])
        return len(arrays) - 1, source[1]

    own, given = [place(p) for p in own], [place(p) for p in given]
    rates = [MUON_RATE * 0.2 * math.sqrt(max(size, n)) for n in (full, 2 * full)]
    whole = lambda a: pl.BlockSpec(a.shape, lambda i, c: (0,) * a.ndim, pipeline_mode=pl.Buffered(1))
    fixed = lambda *f: pl.BlockSpec(f, lambda i, c: (0,) * len(f))
    edge = -(-square.shape[0] // 128) * 128
    return pl.pallas_call(
        functools.partial(polynomial_kernel, own, given, len(arrays), rates),
        grid_spec=pltpu.PrefetchScalarGridSpec(
            num_scalar_prefetch=1,
            grid=(1,),
            in_specs=[whole(a) for a in arrays] + [whole(square)],
            out_specs=[fixed(size, size), fixed(*square.shape)],
            scratch_shapes=[pltpu.VMEM((size, 2 * full), LOW)]
            + [pltpu.VMEM((size, size), F32)] * 2
            + [pltpu.VMEM((edge, edge), F32)],
        ),
        out_shape=[jax.ShapeDtypeStruct((size, size), F32), jax.ShapeDtypeStruct(square.shape, F32)],
        compiler_params=compiler(60),
        cost_estimate=pl.CostEstimate(
            flops=2 * size * size * (51 * size + 2 * full), bytes_accessed=16 * size * full, transcendentals=0
        ),
        name="polynomials",
    )(core, *arrays, square)


def update_kernel(core, mine, theirs, flat, w_in, w_out, new_in, new_out):
    zero = core[0] == 0
    shrink_by = 1.0 - MUON_RATE * DECAY_RATE
    poly_out = split_two(jnp.where(zero, mine[...], theirs[...]))
    new_out[...] = w_out[...] * shrink_by - dot3(poly_out, split_two(flat[2])).T
    poly_in = split_two(jnp.where(zero, theirs[...], mine[...]))
    for i in range(2):
        new_in[:, i, :] = w_in[:, i, :] * shrink_by - dot3(poly_in, split_two(flat[i]))


def update(core, mine, theirs, flat, w_in, w_out):
    ins = (mine, theirs, flat, w_in, w_out)
    fixed = lambda a: pl.BlockSpec(a.shape, lambda i, c: (0,) * a.ndim)
    return pl.pallas_call(
        update_kernel,
        grid_spec=pltpu.PrefetchScalarGridSpec(
            num_scalar_prefetch=1,
            grid=(1,),
            in_specs=[fixed(a) for a in ins],
            out_specs=[fixed(w_in), fixed(w_out)],
        ),
        out_shape=[jax.ShapeDtypeStruct(w.shape, F32) for w in (w_in, w_out)],
        compiler_params=compiler(60),
        name="update",
    )(core, *ins)


def adam_update(param_now, grad_now, first_old, second_old):
    first_new = BETA_FIRST * first_old + (1.0 - BETA_FIRST) * grad_now
    second_new = BETA_SECOND * second_old + (1.0 - BETA_SECOND) * grad_now * grad_now
    first_hat = first_new / (1.0 - BETA_FIRST**STEP)
    second_hat = second_new / (1.0 - BETA_SECOND**STEP)
    updated = param_now * (1.0 - ADAM_RATE * DECAY_RATE) - ADAM_RATE * first_hat / (
        jnp.sqrt(second_hat) + 1e-08
    )
    return (second_new, updated)


def core_index():
    return lax.axis_index("dp") % 2


def swap_core(part):
    return lax.ppermute(part, "dp", [(i, i ^ 1) for i in range(lax.axis_size("dp"))])


def exchange_mp(parts):
    return lax.all_to_all(parts, "mp", 0, 0)


def send_z(part, step):
    size = lax.axis_size("dp")
    return lax.ppermute(part, "dp", [(i, i ^ (2 * step)) for i in range(size)])


def after(value, *others):
    return lax.optimization_barrier((value, *others))[0]


def copies(part, count):
    return jnp.broadcast_to(part[None], (count,) + part.shape)


def gather_mp(part):
    return exchange_mp(copies(part, lax.axis_size("mp")))


def core_rows(rows, core):
    half = rows.shape[0] // 2
    return lax.dynamic_slice_in_dim(rows, core * half, half, 0)


def regroup(pieces, parts):
    ways, rows, columns = pieces.shape
    shard = columns // parts
    if shard % 128 == 0:
        return [(pieces, i * shard) for i in range(parts)]
    split = pieces.reshape(ways, rows, parts, shard).transpose(2, 1, 0, 3)
    return [(split[i].reshape(1, rows, ways * shard), 0) for i in range(parts)]


def plane_sum(parts):
    return jnp.sum(parts.astype(F32), axis=0)


def core_part(mix, core):
    each = mix.shape[1] // 2
    return jnp.where(core == 0, mix[:, :each], mix[:, each:])


def split_again(half, shard, mix_shape, main, first_row):
    each, wide_mix = mix_shape[1] // 2, mix_shape[2]
    row = lax.broadcasted_iota(jnp.int32, main.shape, 0) + first_row
    column = lax.broadcasted_iota(jnp.int32, main.shape, 1)
    here = (row >= half + MIX_ROW) & (row < half + MIX_ROW + each)
    here = here & (column < 2 * shard)
    value = main + jnp.concatenate([main[:, shard : 2 * shard], main[:, :shard], main[:, 2 * shard :]], axis=1)
    high = lax.reduce_precision(value, 8, 7)
    return jnp.where(here, jnp.where(column < shard, high, value - high), main)


def depth_sum(main, again):
    depth = lax.axis_size("dp") // 2
    place = lax.axis_index("dp") // 2
    rows, columns = main.shape
    each = rows // depth
    if again:
        main = again(main, 0)
    low = main.astype(LOW)
    parts = [
        send_z(lax.dynamic_slice_in_dim(low, jnp.bitwise_xor(place, step) * each, each, 0), step)
        for step in range(1, depth)
    ]
    mine = lax.dynamic_slice_in_dim(main, place * each, each, 0)
    mine = mine + sum(p.astype(F32) for p in parts)
    if again:
        mine = again(mine, place * each)
    mine = mine.astype(LOW)
    parts = [mine] + [send_z(mine, step) for step in range(1, depth)]
    pieces = []
    for piece in range(depth):
        here = parts[piece]
        for other in range(1, depth):
            here = jnp.where(place == other, parts[piece ^ other], here)
        pieces.append(here)
    return jnp.concatenate(pieces, axis=0)


def whole_images(rows, patches, count):
    here, width = rows.shape
    spare = count * patches - here
    if spare:
        odd = lax.axis_index("mp") % 2 == 1
        size = lax.axis_size("mp")
        got = lax.ppermute(rows[:spare], "mp", [(i, i - 1) for i in range(1, size, 2)])
        kept = jnp.concatenate([rows[spare:], jnp.zeros((2 * spare, width), rows.dtype)], axis=0)
        rows = jnp.where(odd, kept, jnp.concatenate([rows, got], axis=0))
    return rows


def held_rows(rows, here):
    spare = rows.shape[0] - here
    if spare:
        odd = lax.axis_index("mp") % 2 == 1
        size = lax.axis_size("mp")
        got = lax.ppermute(rows[here:], "mp", [(i, i + 1) for i in range(0, size, 2)])
        kept = jnp.concatenate([got, rows[: here - spare]], axis=0)
        rows = jnp.where(odd, kept, rows[:here])
    return rows


def per_device(
    tokens,
    cotangent,
    w_in,
    w_out,
    spatial,
    model_vectors,
    gate_vectors,
    patch_bias,
    moment_in,
    moment_out,
    moment_mix,
    first_model,
    second_model,
    first_gate,
    second_gate,
    first_patch,
    second_patch,
):
    here, width = tokens.shape
    shard = w_in.shape[2]
    ways = lax.axis_size("mp")
    full = shard * ways
    patches = spatial.shape[0]
    images = -(-here // patches)
    pad = -(-patches // 16) * 16
    core = core_index()
    core_arg = core.astype(jnp.int32).reshape(1)

    half = width // 2

    gate_wire, rest_wire = weight_wires(core_arg, w_in, w_out, gate_vectors)
    gate_mine = exchange_mp(gate_wire)
    tokens_rows = whole_images(tokens, patches, images)
    cot_rows = whole_images(cotangent, patches, images)
    normed, unit_in, inv_in, cot_pad, normed_t, cot_t = prep(core_arg, tokens_rows, cot_rows, model_vectors, patches, pad)
    mix = jnp.pad(spatial.astype(LOW), ((0, pad - patches), (0, pad - patches)))
    mix_t = mix.T
    bias = jnp.broadcast_to(jnp.pad(patch_bias, (0, pad - patches))[:, None], (pad, 128))
    gate_mine, mix, mix_t, bias = lax.optimization_barrier((gate_mine, mix, mix_t, bias, normed, rest_wire))[:4]
    rest_mine = exchange_mp(after(rest_wire, gate_mine))
    gate_theirs = swap_core(gate_mine)

    [(gate_mine, _)], [(gate_theirs, _)] = regroup(gate_mine, 1), regroup(gate_theirs, 1)
    normal, unit, slope, scale, w_gate, vec_all = gate_forward(core_arg, normed, gate_mine, gate_theirs, images, pad)
    rest_mine = after(rest_mine, normal)
    rest_theirs = swap_core(rest_mine)
    rest_mine, rest_theirs = (
        (parts[0][0] if parts[0][0] is parts[1][0] else jnp.concatenate([p[0] for p in parts], axis=2))
        for parts in (regroup(rest_mine, 2), regroup(rest_theirs, 2))
    )
    gated, low_value, low_gate, mine_one, theirs_one, mine_two, theirs_two, grad_mix = channels_both(
        core_arg, normed, cot_pad, normed_t, cot_t, normal, unit, slope, scale, rest_mine, rest_theirs,
        mix, mix_t, bias, vec_all, images, pad, ways if pad % ways == 0 else 1,
    )
    rides = mix_rides(shard, grad_mix)
    theirs_one = swap_core(theirs_one)
    mix_rows = (core_part(grad_mix + swap_core(grad_mix), core),) if rides else ()
    wire = merge(mine_one, theirs_one, mine_two, swap_core(theirs_two), ways, mix_rows)
    again = functools.partial(split_again, half, shard, grad_mix.shape) if rides else None
    output, grad_tokens, model_sums = token_back(
        core_arg, tokens_rows, cot_rows, unit_in, inv_in, gated, low_value, after(low_gate, wire),
        rest_mine, rest_theirs, w_gate, model_vectors, patches, pad,
    )

    parts = after(exchange_mp(wire), model_sums)
    plane = plane_sum(parts)
    tail = jnp.pad(model_sums[:3].reshape(-1), (0, EXTRA // 2 * shard - 3 * width)).reshape(EXTRA // 2, shard)
    plane = lax.dynamic_update_slice(plane, tail, (half + EXTRA // 2, 2 * shard))
    main = depth_sum(plane, again)
    everything = exchange_mp(moment_wires(core_arg, main, moment_in, moment_out))
    grad_w_in, new_moment_in, grad_w_out, new_moment_out, flat = moments(
        core_arg, main, swap_core(main), moment_in, moment_out
    )
    everything = after(everything, flat)
    extra_rows = everything[:, half:]
    extra_rows = jnp.stack([extra_rows, swap_core(extra_rows)])
    out_only = jnp.pad(everything[:, :half, 2 * shard :], ((0, 0), (0, 0), (0, shard)))
    given = swap_core(jnp.where(core == 0, everything[:, :half, : 2 * shard], out_only))

    vec = main[half : half + 2].astype(F32)
    grad_vec = jnp.stack(
        [vec[0, :shard], vec[0, shard : 2 * shard], vec[0, 2 * shard :], vec[1, 2 * shard :]]
    )
    tails = jnp.sum(extra_rows[:, :, EXTRA // 2 :, 2 * shard :].astype(F32), axis=1)
    grad_model = (tails[0] + tails[1]).reshape(-1)[: 3 * width].reshape(3, width)
    if rides:
        each = grad_mix.shape[1] // 2
        rows = extra_rows[:, :, MIX_ROW : MIX_ROW + each].astype(F32)
        rows = rows[:, :, :, :shard] + rows[:, :, :, shard : 2 * shard]
        rows = rows[:, :, :, : grad_mix.shape[2]]
        rows = jnp.where(core == 0, rows, rows[::-1])
        grad_mix = jnp.concatenate([rows[0], rows[1]], axis=1)
    else:
        grad_mix = lax.psum(grad_mix, ("dp", "mp"))
    grad_mix = grad_mix.reshape(pad, -1)
    grad_spatial = grad_mix[:patches, :patches]
    grad_patch = grad_mix[:patches, pad]

    new_moment_mix = MOMENTUM * moment_mix + grad_spatial
    poly, ortho_mix = polynomials(core_arg, regroup(everything, 3), regroup(given, 2), full, new_moment_mix, width)
    new_w_in, new_w_out = update(core_arg, poly, swap_core(poly), flat, w_in, w_out)
    shrink_by = 1.0 - MUON_RATE * DECAY_RATE
    new_spatial = spatial * shrink_by - MUON_RATE * 0.2 * math.sqrt(patches) * ortho_mix
    new_second_model, new_model = adam_update(model_vectors, grad_model, first_model, second_model)
    new_second_gate, new_gate = adam_update(gate_vectors, grad_vec, first_gate, second_gate)
    new_second_patch, new_patch = adam_update(patch_bias, grad_patch, first_patch, second_patch)
    return (
        held_rows(output, here),
        held_rows(grad_tokens, here),
        grad_w_in,
        grad_w_out,
        grad_spatial,
        grad_model,
        grad_vec,
        grad_patch,
        new_moment_in,
        new_moment_out,
        new_moment_mix,
        new_second_model,
        new_second_gate,
        new_second_patch,
        new_w_in,
        new_w_out,
        new_spatial,
        new_model,
        new_gate,
        new_patch,
    )


def solution(mesh):
    rows = P(("dp", "mp"), None)
    wide = P(None, None, "mp")
    tall = P("mp", None)
    columns = P(None, "mp")
    return jax.shard_map(
        per_device,
        mesh=mesh,
        in_specs=(
            (rows, rows, wide, tall, P(), P(), columns, P())
            + (wide, tall, P(), P(), P(), columns, columns, P(), P())
        ),
        out_specs=(
            (rows, rows, wide, tall, P(), P(), columns, P())
            + (wide, tall, P(), P(), columns, P())
            + (wide, tall, P(), P(), columns, P())
        ),
        check_vma=False,
    )
```

```python
import functools
import math

import jax
import jax.numpy as jnp
from jax import lax
from jax.experimental import pallas as pl
from jax.experimental.pallas import tpu as pltpu
from jax.sharding import PartitionSpec as P

STEP = 10
EPSILON = 1e-05
COEF_FIRST = 3.4445
COEF_SECOND = -4.775
COEF_THIRD = 2.0315
MOMENTUM = 0.95
MUON_RATE = 0.2
ADAM_RATE = 0.3
DECAY_RATE = 0.01
BETA_FIRST = 0.9
BETA_SECOND = 0.95
LOW = jnp.bfloat16
F32 = jnp.float32


ROW_TILE = 16
UNROLL = 3
EXTRA = 32
MIX_ROW = 4
CHUNK = 512
CUBIC = 0.044715
SLOPE = math.sqrt(2.0 / math.pi)


def compiler(megabytes):
    return pltpu.CompilerParams(vmem_limit_bytes=megabytes << 20)


def dot_nn(a, b):
    return jnp.dot(a, b, preferred_element_type=F32)


def dot_nt(a, b):
    return lax.dot_general(a, b, (((1,), (1,)), ((), ())), preferred_element_type=F32)


def gelu_pair(hidden):
    square = hidden * hidden
    half = 0.5 + 0.5 * jnp.tanh(hidden * (SLOPE + (SLOPE * CUBIC) * square))
    active = hidden * half
    slope = half + (active - active * half) * (2.0 * SLOPE + (6.0 * SLOPE * CUBIC) * square)
    return active, slope


def lanes(v):
    total = v[:, :128]
    for at in range(128, v.shape[1], 128):
        total = total + v[:, at : at + 128]
    return total


def eights(v):
    total = v[:8]
    for at in range(8, v.shape[0], 8):
        total = total + v[at : at + 8]
    return total


def wide(v, width):
    return jnp.concatenate([v] * (width // 128), axis=1) if width % 128 == 0 else v[:, :1]


def tiles(count, body, carry=None):
    for at in range(0, count, ROW_TILE):
        carry = body(slice(at, at + ROW_TILE), carry)
    return carry


def spread_pieces(core, mine, theirs, out, offset):
    half = out.shape[0] // 2
    count = mine.shape[0]
    shard = out.shape[1] // count
    first = pl.ds(pl.multiple_of(core[0] * half, half), half)
    other = pl.ds(pl.multiple_of((1 - core[0]) * half, half), half)
    for piece in range(count):
        cols = slice(piece * shard, (piece + 1) * shard)
        out[first, cols] = mine[piece, :half, offset : offset + shard]
        out[other, cols] = theirs[piece, :half, offset : offset + shard]


def gate_kernel(chunk, core, normed, mine, theirs, normal, unit, slope, scale, weight, vec, active):
    rows, full = active.shape
    half = weight.shape[0] // 2

    @pl.when(pl.program_id(0) == 0)
    def _():
        count, _, shard = mine.shape
        first = pl.ds(pl.multiple_of(core[0] * half, half), half)
        other = pl.ds(pl.multiple_of((1 - core[0]) * half, half), half)
        for piece in range(count):
            owner = jnp.bitwise_xor(core[1], piece) if count > 1 else 0
            cols = pl.ds(pl.multiple_of(owner * shard, shard), shard) if count > 1 else slice(0, shard)
            weight[first, cols] = mine[piece, :half, :]
            weight[other, cols] = theirs[piece, :half, :]
            terms = mine[piece, half:, :].astype(F32)
            vec[:, cols] = (terms[0:8] + terms[8:16]) + terms[16:24]

    starts = range(0, full, chunk)
    for at in starts:
        active[:, at : at + chunk] = dot_nn(normed[...], weight[:, at : at + chunk])

    def act(here, _):
        total = jnp.zeros((ROW_TILE, 128), F32)
        for at in starts:
            cols = slice(at, at + chunk)
            value, grad = gelu_pair(active[here, cols] + vec[1:2, cols])
            active[here, cols] = value
            slope[here, cols] = grad.astype(LOW)
            total = total + lanes(value)
        scale[here, :] = total

    tiles(rows, act)
    mean = jnp.sum(scale[...], axis=1, keepdims=True) * (1.0 / full)
    scale[...] = jnp.broadcast_to(mean, scale.shape)

    def spread(here, _):
        total = jnp.zeros((ROW_TILE, 128), F32)
        mean_here = wide(scale[here, :], chunk)
        for at in starts:
            cols = slice(at, at + chunk)
            centred = active[here, cols] - mean_here
            active[here, cols] = centred
            total = total + lanes(centred * centred)
        scale[here, :] = total

    tiles(rows, spread)
    var = jnp.sum(scale[...], axis=1, keepdims=True) * (1.0 / full)
    scale[...] = jnp.broadcast_to(lax.rsqrt(var + EPSILON), scale.shape)

    def finish(here, _):
        inv = wide(scale[here, :], chunk)
        for at in starts:
            cols = slice(at, at + chunk)
            unit_here = active[here, cols] * inv
            unit[here, cols] = unit_here.astype(LOW)
            normal[here, cols] = (unit_here * vec[2:3, cols] + vec[3:4, cols]).astype(LOW)

    tiles(rows, finish)


def gate_forward(core, normed, mine, theirs, images, pad):
    count, _, shard = mine.shape
    full = count * shard
    width = normed.shape[1]
    chunk = 512 if full % 512 == 0 else full
    total = images * pad
    whole = lambda a: pl.BlockSpec(a.shape, lambda i, c: (0,) * a.ndim, pipeline_mode=pl.Buffered(1))
    rows = lambda n: pl.BlockSpec((pad, n), lambda i, c: (i, 0))
    fixed = lambda *f: pl.BlockSpec(f, lambda i, c: (0, 0))
    shape = jax.ShapeDtypeStruct
    return pl.pallas_call(
        functools.partial(gate_kernel, chunk),
        grid_spec=pltpu.PrefetchScalarGridSpec(
            num_scalar_prefetch=1,
            grid=(images,),
            in_specs=[rows(width), whole(mine), whole(theirs)],
            out_specs=[rows(full), rows(full), rows(full), rows(128), fixed(width, full), fixed(8, full)],
            scratch_shapes=[pltpu.VMEM((pad, full), F32)],
        ),
        out_shape=[shape((total, full), LOW)] * 3
        + [shape((total, 128), F32), shape((width, full), LOW), shape((8, full), F32)],
        compiler_params=compiler(60),
        cost_estimate=pl.CostEstimate(
            flops=2 * total * width * full, bytes_accessed=8 * total * full, transcendentals=total * full
        ),
        name="gate_forward",
    )(core, normed, mine, theirs)


def value_kernel(
    pad,
    images,
    core,
    normed,
    cot,
    normed_t,
    cot_t,
    normal,
    unit,
    slope_gate,
    scale,
    w_mine,
    w_theirs,
    mix,
    mix_t,
    bias,
    vec,
    gated,
    low_value,
    low_gate,
    mine,
    theirs,
    mine_gate,
    theirs_gate,
    mix_pieces,
    vec_sums,
    w_value,
    w_back,
    sums,
    grad_mix,
    grad_bias,
    grad_unit,
    hidden,
    back,
    mixed,
    turned,
    low_mixed,
    low_pad,
    gated_pad,
):
    total, chunk = gated.shape
    half = w_value.shape[0] // 2
    step = pl.program_id(0)
    count = pl.num_programs(0) // 2
    cols = pl.ds(pl.multiple_of(lax.rem(step, count) * chunk, chunk), chunk)

    @pl.when(step == 0)
    def _():
        offset = w_mine.shape[2] - w_value.shape[1] // w_mine.shape[0]
        spread_pieces(core, w_mine, w_theirs, w_value, 0)
        spread_pieces(core, w_mine, w_theirs, w_back, offset)
        sums[...] = jnp.zeros_like(sums)
        vec_sums[...] = jnp.zeros_like(vec_sums)
        grad_mix[...] = jnp.zeros_like(grad_mix)
        grad_bias[...] = jnp.zeros_like(grad_bias)
        low_pad[total:, :] = jnp.zeros_like(low_pad[total:, :])
        gated_pad[total:, :] = jnp.zeros_like(gated_pad[total:, :])

    pairs = ((hidden.at[0], back.at[0], mixed.at[0]), (hidden.at[1], back.at[1], mixed.at[1]))

    def products(image):
        here = slice(image * pad, (image + 1) * pad)
        hid, bck, mxd = pairs[image % 2]
        hid[...] = dot_nn(normed[here, :], w_value[:, cols])
        bck[...] = dot_nn(cot[here, :], w_back[:, cols])
        mxd[...] = dot_nn(mix[...], normal[here, :])

    def forward(image, sums):
        hid, bck, mxd = pairs[image % 2]
        for row in range(0, pad, ROW_TILE):
            at = slice(row, row + ROW_TILE)
            here = slice(image * pad + row, image * pad + row + ROW_TILE)
            value, slope = gelu_pair(hid[at, :] + vec[0:1, :])
            mixed_here = mxd[at, :] + wide(bias[at, :], chunk)
            back_here = bck[at, :]
            gated_here = (value * mixed_here).astype(LOW)
            gated[here, :] = gated_here
            gated_pad[here, :] = gated_here
            grad_here = (back_here * value).astype(LOW)
            low_mixed[image % 2, at, :] = grad_here
            grad_bias[at, :] += lanes(grad_here.astype(F32))
            low_here = (back_here * mixed_here * slope).astype(LOW)
            low_value[here, :] = low_here
            low_pad[here, :] = low_here
            sums = sums + eights(low_here.astype(F32))
        return sums

    def turn(image):
        here = slice(image * pad, (image + 1) * pad)
        turned[image % 2] = dot_nn(mix_t[...], low_mixed[image % 2])
        grad_mix[:, :pad] += dot_nt(low_mixed[image % 2], normal[here, :])

    def backward(image, kept):
        for row in range(0, pad, ROW_TILE):
            at = slice(row, row + ROW_TILE)
            here = slice(image * pad + row, image * pad + row + ROW_TILE)
            grad = turned[image % 2, at, :]
            unit_here = unit[here, :].astype(F32)
            gain = vec[2:3, :]
            both = grad * unit_here
            du = grad * gain
            grad_unit[here, cols] = du.astype(LOW)
            sums[0, here, :] += lanes(du)
            sums[1, here, :] += lanes(both * gain)
            kept = kept[0] + eights(both), kept[1] + eights(grad)
        return kept

    @pl.when(step < count)
    def _():
        zero = jnp.zeros((8, chunk), F32)
        bias_sum, norm_sums = zero, (zero, zero)
        products(0)
        for image in range(images):
            if image + 1 < images:
                products(image + 1)
            bias_sum = forward(image, bias_sum)
            turn(image)
            if image:
                norm_sums = backward(image - 1, norm_sums)
        norm_sums = backward(images - 1, norm_sums)
        gain_sum, shift_sum = norm_sums

        for i, product in enumerate((dot_nn(normed_t[...], low_pad[...]), dot_nn(cot_t[...], gated_pad[...]))):
            mine[i, :half, :] = product[:half].astype(LOW)
            theirs[i, :half, :] = product[half:].astype(LOW)

        total_of = lambda v: jnp.sum(v, axis=0, keepdims=True)
        vec_sums[0:1, cols] = total_of(bias_sum)
        vec_sums[2:3, cols] = total_of(gain_sum)
        vec_sums[3:4, cols] = total_of(shift_sum)

    @pl.when(step == count - 1)
    def _():
        patch = jnp.sum(grad_bias[...], axis=1, keepdims=True)
        grad_mix[:, pad:] = jnp.broadcast_to(patch, (pad, grad_mix.shape[1] - pad))
        each = mix_pieces.shape[1]
        for piece in range(mix_pieces.shape[0]):
            mix_pieces[piece] = grad_mix[piece * each : (piece + 1) * each, :]


    def gate_tile(i, total_here):
        here = slice(i * ROW_TILE, (i + 1) * ROW_TILE)
        one = wide(sums[0, here, :], chunk)
        two = wide(sums[1, here, :], chunk)
        inv = wide(scale[here, :], chunk)
        grad = inv * (grad_unit[here, cols].astype(F32) - one - unit[here, :].astype(F32) * two)
        low = (grad * slope_gate[here, :].astype(F32)).astype(LOW)
        low_gate[here, :] = low
        low_pad[here, :] = low
        return total_here + eights(low.astype(F32))

    @pl.when(step == count)
    def _():
        for i in range(2):
            mean = jnp.sum(sums[i], axis=1, keepdims=True) * (1.0 / w_value.shape[1])
            sums[i] = jnp.broadcast_to(mean, (total, 128))

    @pl.when(step >= count)
    def _():
        kept = jnp.zeros((8, chunk), F32)
        for at in range(total // ROW_TILE):
            kept = gate_tile(at, kept)
        vec_sums[1:2, cols] = jnp.sum(kept, axis=0, keepdims=True)
        product = dot_nn(normed_t[...], low_pad[...])
        mine_gate[:half, :] = product[:half].astype(LOW)
        theirs_gate[:half, :] = product[half:].astype(LOW)


def channels_both(
    core, normed, cot, normed_t, cot_t, normal, unit, slope, scale, w_mine, w_theirs, mix, mix_t, bias, vec, images, pad, ways
):
    width = normed.shape[1]
    full = normal.shape[1]
    total = images * pad
    deep = normed_t.shape[1]
    chunk = CHUNK if full % CHUNK == 0 else full
    count = full // chunk
    half = width // 2
    wide_mix = -(-(pad + 1) // 128) * 128
    mix_shape = (ways, pad // ways, wide_mix)
    whole = lambda a: pl.BlockSpec(a.shape, lambda i, c: (0,) * a.ndim, pipeline_mode=pl.Buffered(1))
    early = lambda n: pl.BlockSpec((n, chunk), lambda i, c: (0, jnp.minimum(i, count - 1)))
    late = lambda n: pl.BlockSpec((n, chunk), lambda i, c: (0, jnp.maximum(i - count, 0)))
    twice = lambda n: pl.BlockSpec((n, chunk), lambda i, c: (0, lax.rem(i, count)))
    pair = pl.BlockSpec((2, half, chunk), lambda i, c: (0, 0, jnp.minimum(i, count - 1)))
    shape = jax.ShapeDtypeStruct
    return pl.pallas_call(
        functools.partial(value_kernel, pad, images),
        grid_spec=pltpu.PrefetchScalarGridSpec(
            num_scalar_prefetch=1,
            grid=(2 * count,),
            in_specs=[whole(normed), whole(cot), whole(normed_t), whole(cot_t)]
            + [early(total), twice(total), late(total), whole(scale), whole(w_mine), whole(w_theirs)]
            + [whole(mix), whole(mix_t), whole(bias), early(8)],
            out_specs=[early(total), early(total), late(total), pair, pair, late(half), late(half)]
            + [pl.BlockSpec(mix_shape, lambda i, c: (0, 0, 0)), pl.BlockSpec((8, full), lambda i, c: (0, 0))],
            scratch_shapes=[pltpu.VMEM((width, full), LOW)] * 2
            + [pltpu.VMEM((2, total, 128), F32), pltpu.VMEM((pad, wide_mix), F32), pltpu.VMEM((pad, 128), F32)]
            + [pltpu.VMEM((total, full), LOW)]
            + [pltpu.VMEM((2, pad, chunk), F32)] * 4
            + [pltpu.VMEM((2, pad, chunk), LOW)]
            + [pltpu.VMEM((deep, chunk), LOW)] * 2,
        ),
        out_shape=[shape((total, full), LOW)] * 3
        + [shape((2, half, full), LOW)] * 2
        + [shape((half, full), LOW)] * 2 + [shape(mix_shape, F32), shape((8, full), F32)],
        compiler_params=compiler(60),
        cost_estimate=pl.CostEstimate(
            flops=14 * total * width * full, bytes_accessed=24 * total * full, transcendentals=total * full
        ),
        name="channels_both",
    )(core, normed, cot, normed_t, cot_t, normal, unit, slope, scale, w_mine, w_theirs, mix, mix_t, bias, vec)


def gate_wire_kernel(core, w_in, vectors, wire):
    half, _, shard = w_in.shape
    low = w_in[:, 1, :].astype(LOW)
    value = jnp.concatenate([vectors[...], jnp.zeros((4, shard), F32)], axis=0)
    high = value.astype(LOW).astype(F32)
    middle = (value - high).astype(LOW).astype(F32)
    last = value - high - middle
    terms = jnp.concatenate([high, middle, last, jnp.zeros((8, shard), F32)], axis=0).astype(LOW)
    wire[:half, :] = low
    wire[half:, :] = terms


def rest_wire_kernel(core, w_in, w_out, wire):
    shard = w_in.shape[2]
    value = w_in[:, 0, :].astype(LOW)
    back = w_out[...].T.astype(LOW)
    for receiver in range(wire.shape[0]):
        wire[receiver, :, :shard] = value
        wire[receiver, :, shard:] = back


def weight_wires(core, w_in, w_out, vectors):
    width, _, shard = w_in.shape
    half = width // 2
    ways = lax.axis_size("mp")
    rows = pl.BlockSpec((half, 2, shard), lambda i, c: (c[0], 0, 0))
    fixed = lambda *f: pl.BlockSpec(f, lambda i, c: (0,) * len(f))
    spec = lambda ins, out: pltpu.PrefetchScalarGridSpec(
        num_scalar_prefetch=1, grid=(1,), in_specs=ins, out_specs=fixed(*out)
    )
    out = (half + 32, shard)
    gate = pl.pallas_call(
        gate_wire_kernel,
        grid_spec=spec([rows, fixed(4, shard)], out),
        out_shape=jax.ShapeDtypeStruct(out, LOW),
        compiler_params=compiler(60),
        name="gate_wire",
    )(core, w_in, vectors)
    out = (ways, half, 2 * shard)
    if shard % 128:
        back = lax.dynamic_slice_in_dim(w_out, core[0] * half, half, 1)
        rest = jnp.concatenate([core_rows(w_in[:, 0], core[0]), back.T], axis=1).astype(LOW)
        return gate, copies(rest, ways)
    rest = pl.pallas_call(
        rest_wire_kernel,
        grid_spec=spec([rows, pl.BlockSpec((shard, half), lambda i, c: (0, c[0]))], out),
        out_shape=jax.ShapeDtypeStruct(out, LOW),
        compiler_params=compiler(60),
        name="rest_wire",
    )(core, w_in, w_out)
    return gate, rest


def merge_kernel(core, mine, theirs, mine_gate, theirs_gate, vec, vec_other, *refs):
    wire = refs[-1]
    _, half, shard = mine.shape
    parts = ((mine.at[0], theirs.at[0]), (mine_gate, theirs_gate), (mine.at[1], theirs.at[1]))
    for i, (own, other) in enumerate(parts):
        wire[0, :half, i * shard : (i + 1) * shard] = (own[...].astype(F32) + other[...].astype(F32)).astype(LOW)
    extra = wire.shape[1] - half
    rows = [(vec[...] + vec_other[...])[:MIX_ROW]]
    if len(refs) > 1:
        mix = refs[0][0] + refs[1][0]
        each = mix.shape[0] // 2
        mix = jnp.where(core[0] == 0, mix[:each], mix[each:])
        rows.append(jnp.concatenate([mix, jnp.zeros((mix.shape[0], shard - mix.shape[1]), F32)], axis=1))
    rows.append(jnp.zeros((extra - sum(r.shape[0] for r in rows), shard), F32))
    rows = jnp.concatenate(rows, axis=0)
    high = rows.astype(LOW).astype(F32)
    for i, part in enumerate((high, rows - high, jnp.zeros_like(rows))):
        wire[0, half:, i * shard : (i + 1) * shard] = part.astype(LOW)


def merge(core, mine, theirs, mine_gate, theirs_gate, vec, vec_other, ways, extra, mix):
    _, rows, full = mine.shape
    shard = full // ways
    if shard % 128:
        both = mine.astype(F32) + theirs.astype(F32)
        both = jnp.stack([both[0], mine_gate.astype(F32) + theirs_gate.astype(F32), both[1]])
        more = jnp.pad((vec + vec_other)[:MIX_ROW], ((0, extra - MIX_ROW), (0, 0)))
        high = lax.reduce_precision(more, 8, 7)
        both = jnp.concatenate([both, jnp.stack([high, more - high, jnp.zeros_like(more)])], axis=1)
        blocks = both.reshape(3, rows + extra, ways, shard).transpose(2, 1, 0, 3)
        return blocks.reshape(ways, rows + extra, 3 * shard).astype(LOW)
    pair = pl.BlockSpec((2, rows, shard), lambda i, c: (0, 0, i))
    block = lambda n: pl.BlockSpec((n, shard), lambda i, c: (0, i))
    return pl.pallas_call(
        merge_kernel,
        grid_spec=pltpu.PrefetchScalarGridSpec(
            num_scalar_prefetch=1,
            grid=(ways,),
            in_specs=[pair, pair, block(rows), block(rows), block(8), block(8)]
            + [pl.BlockSpec((1,) + m.shape[1:], lambda i, c: (i, 0, 0)) for m in mix],
            out_specs=pl.BlockSpec((1, rows + extra, 3 * shard), lambda i, c: (i, 0, 0)),
        ),
        out_shape=jax.ShapeDtypeStruct((ways, rows + extra, 3 * shard), LOW),
        compiler_params=compiler(60),
        name="merge",
    )(core, mine, theirs, mine_gate, theirs_gate, vec, vec_other, *mix)


def mix_rides(shard, mix):
    return shard % 128 == 0 and mix.shape[2] + 128 <= shard and mix.shape[0] > 1 and mix.shape[1] % 2 == 0 and (
        mix.shape[1] // 2 + MIX_ROW <= EXTRA
    )


def gram_kernel(count, core, main, other, old_in, old_out, wire, moment):
    width, _, shard = old_in.shape
    half = width // 2
    halves = (
        (pl.ds(pl.multiple_of(core[0] * half, half), half), main),
        (pl.ds(pl.multiple_of((1 - core[0]) * half, half), half), other),
    )

    @pl.when(core[0] == 0)
    def _():
        moment[:, :shard] = MOMENTUM * old_out[...].T
        moment[:, shard:] = jnp.zeros((width, shard), F32)
        for rows, part in halves:
            moment[rows, :shard] += part[:half, 2 * shard :].astype(F32)

    @pl.when(core[0] == 1)
    def _():
        for i in range(2):
            cols = slice(i * shard, (i + 1) * shard)
            moment[:, cols] = MOMENTUM * old_in[:, i, :]
            for rows, part in halves:
                moment[rows, cols] += part[:half, cols].astype(F32)

    high, low = split_two(moment[...])
    rows = (slice(0, half), slice(half, width))
    blocks = []
    for i, j in ((0, 0), (0, 1), (1, 1)):
        i, j = rows[i], rows[j]
        cross = dot_nt(high[i], low[j]) + dot_nt(low[i], high[j])
        blocks.append(dot_nt(high[i], high[j]) + cross)
    blocks = jnp.concatenate(blocks, axis=0)
    terms = main[half:, :].astype(F32)
    terms = terms[:, :shard] + terms[:, shard : 2 * shard]
    extra = terms.shape[0]
    for receiver in range(wire.shape[0]):
        wire[receiver, :count, :] = blocks[receiver * count : (receiver + 1) * count]
        for i, at in enumerate(range(0, shard, 128)):
            part = terms[:, at : at + 128]
            top, left = count + i // 2 * extra, i % 2 * 128
            wire[receiver, top : top + extra, left : left + part.shape[1]] = part


def gram_wires(core, main, old_in, old_out):
    width, _, shard = old_in.shape
    half = width // 2
    ways = lax.axis_size("mp")
    count = 3 * half // ways
    extra = main.shape[0] - half
    rows = count + extra * -(-shard // 256)
    fixed = lambda *f: pl.BlockSpec(f, lambda i, c: (0,) * len(f))
    ins = (main, swap_core(main), old_in, old_out)
    out = (ways, rows, half)
    return ins[1], count, pl.pallas_call(
        functools.partial(gram_kernel, count),
        grid_spec=pltpu.PrefetchScalarGridSpec(
            num_scalar_prefetch=1,
            grid=(1,),
            in_specs=[fixed(*a.shape) for a in ins],
            out_specs=fixed(*out),
            scratch_shapes=[pltpu.VMEM((width, 2 * shard), F32)],
        ),
        out_shape=jax.ShapeDtypeStruct(out, F32),
        compiler_params=compiler(60),
        name="gram_wires",
    )(core, *ins)


def extra_rows_of(parts, extra, shard):
    pieces = []
    for i, at in enumerate(range(0, shard, 128)):
        top, left = i // 2 * extra, i % 2 * 128
        pieces.append(parts[..., top : top + extra, left : left + min(128, shard - at)])
    return jnp.concatenate(pieces, axis=-1)


def moments_kernel(core, main, other, old_in, old_out, w_in, grad_in, new_in, grad_out, new_out, terms, kept, flat):
    width, _, shard = old_in.shape
    half = width // 2
    rows = (
        pl.ds(pl.multiple_of(core[0] * half, half), half),
        pl.ds(pl.multiple_of((1 - core[0]) * half, half), half),
    )
    for here, part in ((rows[0], main), (rows[1], other)):
        for i in range(3):
            flat[i, here, :] = part[:half, i * shard : (i + 1) * shard].astype(F32)
    for i in range(2):
        grad = flat[i]
        grad_in[:, i, :] = grad
        moment = MOMENTUM * old_in[:, i, :] + grad
        new_in[:, i, :] = moment
        terms[0, i], terms[1, i] = split_two(moment)
        kept[i] = w_in[:, i, :] * (1.0 - MUON_RATE * DECAY_RATE)
    grad = flat[2].T
    grad_out[...] = grad
    moment = MOMENTUM * old_out[...] + grad
    new_out[...] = moment
    terms[0, 2], terms[1, 2] = split_two(moment.T)


def moments(core, main, other, old_in, old_out, w_in):
    width, _, shard = old_in.shape
    ins = (main, other, old_in, old_out, w_in)
    shapes = (
        [(width, 2, shard)] * 2 + [(shard, width)] * 2 + [(2, 3, width, shard), (2, width, shard)]
    )
    fixed = lambda f: pl.BlockSpec(f, lambda i, c, n=len(f): (0,) * n)
    return pl.pallas_call(
        moments_kernel,
        grid_spec=pltpu.PrefetchScalarGridSpec(
            num_scalar_prefetch=1,
            grid=(1,),
            in_specs=[fixed(a.shape) for a in ins],
            out_specs=[fixed(f) for f in shapes],
            scratch_shapes=[pltpu.VMEM((3, width, shard), F32)],
        ),
        out_shape=[jax.ShapeDtypeStruct(f, LOW if len(f) == 4 else F32) for f in shapes],
        compiler_params=compiler(60),
        name="moments",
    )(core, *ins)


def prep_kernel(patches, pad, core, tokens, cot, model, normed, unit, scale, cot_pad, normed_t, cot_t, keep):
    step = pl.program_id(0)
    group = tokens.shape[1] // patches
    rows = group * pad
    width = tokens.shape[2]

    def padded(block):
        block = block[0].astype(F32)
        gap = jnp.zeros((pad - patches, width), F32)
        parts = []
        for image in range(group):
            parts += [block[image * patches : (image + 1) * patches], gap]
        return jnp.concatenate(parts, axis=0)

    here = pl.ds(pl.multiple_of(step * rows, rows), rows)

    @pl.when(step == 0)
    def _():
        keep[...] = jnp.zeros_like(keep)

    cot_here = padded(cot)
    cot_pad[...] = cot_here.astype(LOW)
    keep[1, here, :] = cot_here
    x = padded(tokens)
    centred = x - jnp.sum(x, axis=1, keepdims=True) * (1.0 / width)
    inv = lax.rsqrt(jnp.sum(centred * centred, axis=1, keepdims=True) * (1.0 / width) + EPSILON)
    unit_here = centred * inv
    scale[...] = jnp.broadcast_to(inv, scale.shape)
    unit[...] = unit_here.astype(LOW)
    low = (unit_here * model[0:1, :] + model[1:2, :]).astype(LOW)
    normed[...] = low
    keep[0, here, :] = low.astype(F32)

    @pl.when(step == pl.num_programs(0) - 1)
    def _():
        half = width // 2
        for i, place in enumerate((core[0], 1 - core[0])):
            features = pl.ds(pl.multiple_of(place * half, half), half)
            rows_out = slice(i * half, (i + 1) * half)
            for at in range(0, normed_t.shape[1], 128):
                cols = slice(at, at + 128)
                normed_t[rows_out, cols] = keep[0, cols, features].T.astype(LOW)
                cot_t[rows_out, cols] = keep[1, cols, features].T.astype(LOW)


def prep(core, tokens, cot, model, patches, pad):
    here, width = tokens.shape
    images = here // patches
    group = 2 if images % 2 == 0 else images
    steps = images // group
    total = images * pad
    deep = -(-total // 128) * 128
    block = pl.BlockSpec((1, group * patches, width), lambda i, c: (i, 0, 0))
    rows = lambda n: pl.BlockSpec((group * pad, n), lambda i, c: (i, 0))
    fixed = lambda *f: pl.BlockSpec(f, lambda i, c: (0, 0))
    shape = jax.ShapeDtypeStruct
    return pl.pallas_call(
        functools.partial(prep_kernel, patches, pad),
        grid_spec=pltpu.PrefetchScalarGridSpec(
            num_scalar_prefetch=1,
            grid=(steps,),
            in_specs=[block, block, fixed(3, width)],
            out_specs=[rows(width), rows(width), rows(128), rows(width), fixed(width, deep), fixed(width, deep)],
            scratch_shapes=[pltpu.VMEM((2, deep, width), F32)],
        ),
        out_shape=[
            shape((total, width), LOW),
            shape((total, width), LOW),
            shape((total, 128), F32),
            shape((total, width), LOW),
            shape((width, deep), LOW),
            shape((width, deep), LOW),
        ],
        compiler_params=compiler(60),
        cost_estimate=pl.CostEstimate(flops=20 * total * width, bytes_accessed=20 * total * width, transcendentals=total),
        name="prep",
    )(core, tokens.reshape(steps, group * patches, width), cot.reshape(steps, group * patches, width), model)


def token_kernel(
    patches,
    pad,
    core,
    tokens,
    cot,
    unit,
    scale,
    gated,
    low_value,
    low_gate,
    w_mine,
    w_theirs,
    w_gate,
    model,
    output,
    grad_tokens,
    sums,
    w_value,
    w_back,
    branch,
    grad,
):
    group = tokens.shape[1] // patches
    width = tokens.shape[2]
    rows = group * pad

    @pl.when(pl.program_id(0) == 0)
    def _():
        sums[...] = jnp.zeros_like(sums)
        offset = w_mine.shape[2] - w_value.shape[1] // w_mine.shape[0]
        spread_pieces(core, w_mine, w_theirs, w_value, 0)
        spread_pieces(core, w_mine, w_theirs, w_back, offset)

    def packed(v):
        return jnp.concatenate([v[i * pad : i * pad + patches] for i in range(group)], axis=0)

    branch[...] = dot_nt(gated[...], w_back[...])
    output[0] = (tokens[0].astype(F32) + packed(branch) + model[2:3, :]).astype(LOW)
    grad[...] = dot_nt(low_value[...], w_value[...]) + dot_nt(low_gate[...], w_gate[...])

    def back(i, kept):
        here = pl.ds(pl.multiple_of(i * ROW_TILE, ROW_TILE), ROW_TILE)
        grad_here = grad[here, :]
        unit_here = unit[here, :].astype(F32)
        both = grad_here * unit_here
        du = grad_here * model[0:1, :]
        first = jnp.sum(du, axis=1, keepdims=True) * (1.0 / width)
        second = jnp.sum(both * model[0:1, :], axis=1, keepdims=True) * (1.0 / width)
        branch[here, :] = wide(scale[here, :], width) * (du - first - unit_here * second)
        return kept[0] + eights(both), kept[1] + eights(grad_here)

    zero = jnp.zeros((8, width), F32)
    gain, shift = lax.fori_loop(0, rows // ROW_TILE, back, (zero, zero), unroll=2)
    cot_here = cot[0].astype(F32)
    grad_tokens[0] = (cot_here + packed(branch)).astype(LOW)
    sums[0:1, :] += jnp.sum(gain, axis=0, keepdims=True)
    sums[1:2, :] += jnp.sum(shift, axis=0, keepdims=True)
    sums[2:3, :] += jnp.sum(eights(cot_here), axis=0, keepdims=True)


def token_back(core, tokens, cot, unit, scale, gated, low_value, low_gate, w_mine, w_theirs, w_gate, model, patches, pad):
    here, width = tokens.shape
    full = w_gate.shape[1]
    images = here // patches
    group = 2 if images % 2 == 0 else images
    steps = images // group
    total = images * pad
    block = pl.BlockSpec((1, group * patches, width), lambda i, c: (i, 0, 0))
    rows = lambda n: pl.BlockSpec((group * pad, n), lambda i, c: (i, 0))
    whole = lambda a: pl.BlockSpec(a.shape, lambda i, c: (0,) * a.ndim, pipeline_mode=pl.Buffered(1))
    shape = jax.ShapeDtypeStruct
    output, grad_tokens, sums = pl.pallas_call(
        functools.partial(token_kernel, patches, pad),
        grid_spec=pltpu.PrefetchScalarGridSpec(
            num_scalar_prefetch=1,
            grid=(steps,),
            in_specs=[block, block, rows(width), rows(128), rows(full), rows(full), rows(full)]
            + [whole(w_mine), whole(w_theirs), whole(w_gate), whole(model)],
            out_specs=[block, block, pl.BlockSpec((8, width), lambda i, c: (0, 0))],
            scratch_shapes=[pltpu.VMEM((width, full), LOW)] * 2 + [pltpu.VMEM((group * pad, width), F32)] * 2,
        ),
        out_shape=[shape((steps, group * patches, width), LOW)] * 2 + [shape((8, width), F32)],
        compiler_params=compiler(60),
        cost_estimate=pl.CostEstimate(
            flops=6 * total * width * full, bytes_accessed=8 * total * full, transcendentals=0
        ),
        name="token_back",
    )(
        core,
        tokens.reshape(steps, group * patches, width),
        cot.reshape(steps, group * patches, width),
        unit, scale, gated, low_value, low_gate, w_mine, w_theirs, w_gate, model,
    )
    return output.reshape(here, width), grad_tokens.reshape(here, width), sums


def split_two(v):
    high = v.astype(LOW)
    return high, (v - high.astype(F32)).astype(LOW)


def dot3(a, b):
    return dot_nn(a[0], b[0]) + (dot_nn(a[0], b[1]) + dot_nn(a[1], b[0]))


def symmetric3(a, b):
    half = a[0].shape[0] // 2
    top = dot3([v[:half] for v in a], b)
    corner = dot3([v[half:] for v in a], [v[:, half:] for v in b])
    bottom = jnp.concatenate([top[:, half:].T, corner], axis=1)
    return jnp.concatenate([top, bottom], axis=0)


def polynomial_kernel(rates, core, pieces, square, poly, square_out, blocks, gram_now, total, now):
    size = gram_now.shape[0]
    half = size // 2
    count = pieces.shape[1]
    for piece in range(pieces.shape[0]):
        blocks[piece * count : (piece + 1) * count, :] = pieces[piece]
    gram_now[:half, :half] = blocks[:half]
    gram_now[:half, half:] = blocks[half:size]
    gram_now[half:, :half] = blocks[half:size].T
    gram_now[half:, half:] = blocks[size:]
    few = square.shape[0]
    now[...] = jnp.zeros_like(now)
    start = square[...]
    now[:few, :few] = start / (jnp.sqrt(jnp.sum(start * start, keepdims=True)) + 1e-07)

    gram = gram_now[...]
    row = lax.broadcasted_iota(jnp.int32, (size, size), 0)
    col = lax.broadcasted_iota(jnp.int32, (size, size), 1)
    same = row == col
    norm = jnp.sqrt(jnp.sum(jnp.where(same, gram, 0.0), keepdims=True)) + 1e-07
    inv = 1.0 / norm
    gram_now[...] = gram * (inv * inv)
    for sweep in range(5):
        x = now[...]
        x_two = split_two(x)
        small = dot_nt(x_two[0], x_two[0]) + (dot_nt(x_two[0], x_two[1]) + dot_nt(x_two[1], x_two[0]))
        small_two = split_two(small)
        matrix = gram_now[...]
        matrix_two = split_two(matrix)
        extra = COEF_SECOND * matrix + COEF_THIRD * symmetric3(matrix_two, matrix_two)
        extra_two = split_two(extra)
        small_extra = COEF_SECOND * small + COEF_THIRD * dot3(small_two, small_two)
        now[...] = COEF_FIRST * x + dot3(split_two(small_extra), x_two)
        if sweep == 0:
            total[...] = jnp.where(same, COEF_FIRST + extra, extra)
        else:
            total[...] = COEF_FIRST * total[...] + symmetric3(extra_two, split_two(total[...]))
        if sweep < 4:
            partial = COEF_FIRST * matrix + symmetric3(extra_two, matrix_two)
            gram_now[...] = COEF_FIRST * partial + symmetric3(extra_two, split_two(partial))
    rate = jnp.where(core[0] == 0, rates[0], rates[1])
    poly[...] = total[...] * (inv * rate)
    square_out[...] = now[:few, :few]


def polynomials(core, pieces, full, square):
    half = pieces.shape[2]
    size = 2 * half
    rates = [MUON_RATE * 0.2 * math.sqrt(max(size, n)) for n in (full, 2 * full)]
    fixed = lambda *f: pl.BlockSpec(f, lambda i, c: (0,) * len(f))
    edge = -(-square.shape[0] // 128) * 128
    return pl.pallas_call(
        functools.partial(polynomial_kernel, rates),
        grid_spec=pltpu.PrefetchScalarGridSpec(
            num_scalar_prefetch=1,
            grid=(1,),
            in_specs=[fixed(*pieces.shape), fixed(*square.shape)],
            out_specs=[fixed(size, size), fixed(*square.shape)],
            scratch_shapes=[pltpu.VMEM((3 * half, half), F32)]
            + [pltpu.VMEM((size, size), F32)] * 2
            + [pltpu.VMEM((edge, edge), F32)],
        ),
        out_shape=[jax.ShapeDtypeStruct((size, size), F32), jax.ShapeDtypeStruct(square.shape, F32)],
        compiler_params=compiler(60),
        cost_estimate=pl.CostEstimate(
            flops=2 * size * size * 51 * size, bytes_accessed=16 * size * size, transcendentals=0
        ),
        name="polynomials",
    )(core, pieces, square)


def update_kernel(core, mine, theirs, terms, kept, w_out, new_in, new_out):
    zero = core[0] == 0
    shrink_by = 1.0 - MUON_RATE * DECAY_RATE
    poly_out = split_two(jnp.where(zero, mine[...], theirs[...]))
    new_out[...] = w_out[...] * shrink_by - dot3(poly_out, (terms[0, 2], terms[1, 2])).T
    poly_in = split_two(jnp.where(zero, theirs[...], mine[...]))
    for i in range(2):
        new_in[:, i, :] = kept[i] - dot3(poly_in, (terms[0, i], terms[1, i]))


def update(core, mine, theirs, terms, kept, w_out):
    _, width, shard = kept.shape
    rows = 256 if width % 256 == 0 else width
    tall = pl.BlockSpec((rows, width), lambda i, c: (i, 0))
    fixed = pl.BlockSpec(terms.shape, lambda i, c: (0, 0, 0, 0), pipeline_mode=pl.Buffered(1))
    outer = pl.BlockSpec((shard, rows), lambda i, c: (0, i))
    return pl.pallas_call(
        update_kernel,
        grid_spec=pltpu.PrefetchScalarGridSpec(
            num_scalar_prefetch=1,
            grid=(width // rows,),
            in_specs=[tall, tall, fixed, pl.BlockSpec((2, rows, shard), lambda i, c: (0, i, 0)), outer],
            out_specs=[pl.BlockSpec((rows, 2, shard), lambda i, c: (i, 0, 0)), outer],
        ),
        out_shape=[jax.ShapeDtypeStruct((width, 2, shard), F32), jax.ShapeDtypeStruct(w_out.shape, F32)],
        compiler_params=compiler(60),
        name="update",
    )(core, mine, theirs, terms, kept, w_out)


def adam_update(param_now, grad_now, first_old, second_old):
    first_new = BETA_FIRST * first_old + (1.0 - BETA_FIRST) * grad_now
    second_new = BETA_SECOND * second_old + (1.0 - BETA_SECOND) * grad_now * grad_now
    first_hat = first_new / (1.0 - BETA_FIRST**STEP)
    second_hat = second_new / (1.0 - BETA_SECOND**STEP)
    updated = param_now * (1.0 - ADAM_RATE * DECAY_RATE) - ADAM_RATE * first_hat / (
        jnp.sqrt(second_hat) + 1e-08
    )
    return (second_new, updated)


def core_index():
    return lax.axis_index("dp") % 2


def swap_core(part):
    return lax.ppermute(part, "dp", [(i, i ^ 1) for i in range(lax.axis_size("dp"))])


def exchange_mp(parts):
    return lax.all_to_all(parts, "mp", 0, 0)


def send_z(part, step):
    size = lax.axis_size("dp")
    return lax.ppermute(part, "dp", [(i, i ^ (2 * step)) for i in range(size)])


def after(value, *others):
    return lax.optimization_barrier((value, *others))[0]


def copies(part, count):
    return jnp.broadcast_to(part[None], (count,) + part.shape)


def gather_quick(part):
    ways = lax.axis_size("mp")
    if ways != 4:
        return gather_mp(part), 0
    sent = [lax.ppermute(part, "mp", [(i, i ^ j) for i in range(ways)]) for j in range(1, ways)]
    return jnp.stack([part, *sent]), lax.axis_index("mp")


def gather_mp(part):
    return exchange_mp(copies(part, lax.axis_size("mp")))


def core_rows(rows, core):
    half = rows.shape[0] // 2
    return lax.dynamic_slice_in_dim(rows, core * half, half, 0)


def regroup(pieces, parts):
    ways, rows, columns = pieces.shape
    shard = columns // parts
    if shard % 128 == 0:
        return [(pieces, i * shard) for i in range(parts)]
    split = pieces.reshape(ways, rows, parts, shard).transpose(2, 1, 0, 3)
    return [(split[i].reshape(1, rows, ways * shard), 0) for i in range(parts)]


def plane_sum(parts):
    return jnp.sum(parts.astype(F32), axis=0)


def split_again(half, shard, main, first_row):
    row = lax.broadcasted_iota(jnp.int32, main.shape, 0) + first_row
    column = lax.broadcasted_iota(jnp.int32, main.shape, 1)
    here = (row >= half) & (column < 2 * shard)
    value = main + jnp.concatenate([main[:, shard : 2 * shard], main[:, :shard], main[:, 2 * shard :]], axis=1)
    high = lax.reduce_precision(value, 8, 7)
    return jnp.where(here, jnp.where(column < shard, high, value - high), main)


def depth_sum(main, again):
    depth = lax.axis_size("dp") // 2
    place = lax.axis_index("dp") // 2
    rows, columns = main.shape
    each = rows // depth
    main = again(main, 0)
    low = main.astype(LOW)
    parts = [
        send_z(lax.dynamic_slice_in_dim(low, jnp.bitwise_xor(place, step) * each, each, 0), step)
        for step in range(1, depth)
    ]
    mine = lax.dynamic_slice_in_dim(main, place * each, each, 0)
    mine = mine + sum(p.astype(F32) for p in parts)
    mine = again(mine, place * each)
    mine = mine.astype(LOW)
    parts = [mine] + [send_z(mine, step) for step in range(1, depth)]
    pieces = []
    for piece in range(depth):
        here = parts[piece]
        for other in range(1, depth):
            here = jnp.where(place == other, parts[piece ^ other], here)
        pieces.append(here)
    return jnp.concatenate(pieces, axis=0)


def whole_images(rows, patches, count):
    here, width = rows.shape
    spare = count * patches - here
    if spare:
        odd = lax.axis_index("mp") % 2 == 1
        size = lax.axis_size("mp")
        got = lax.ppermute(rows[:spare], "mp", [(i, i - 1) for i in range(1, size, 2)])
        kept = jnp.concatenate([rows[spare:], jnp.zeros((2 * spare, width), rows.dtype)], axis=0)
        rows = jnp.where(odd, kept, jnp.concatenate([rows, got], axis=0))
    return rows


def held_rows(rows, here):
    spare = rows.shape[0] - here
    if spare:
        odd = lax.axis_index("mp") % 2 == 1
        size = lax.axis_size("mp")
        got = lax.ppermute(rows[here:], "mp", [(i, i + 1) for i in range(0, size, 2)])
        kept = jnp.concatenate([got, rows[: here - spare]], axis=0)
        rows = jnp.where(odd, kept, rows[:here])
    return rows


def per_device(
    tokens,
    cotangent,
    w_in,
    w_out,
    spatial,
    model_vectors,
    gate_vectors,
    patch_bias,
    moment_in,
    moment_out,
    moment_mix,
    first_model,
    second_model,
    first_gate,
    second_gate,
    first_patch,
    second_patch,
):
    here, width = tokens.shape
    shard = w_in.shape[2]
    ways = lax.axis_size("mp")
    full = shard * ways
    patches = spatial.shape[0]
    images = -(-here // patches)
    pad = -(-patches // 16) * 16
    core = core_index()
    core_arg = core.astype(jnp.int32).reshape(1)

    half = width // 2

    gate_wire, rest_wire = weight_wires(core_arg, w_in, w_out, gate_vectors)
    gate_mine, base = gather_quick(gate_wire)
    tokens_rows = whole_images(tokens, patches, images)
    cot_rows = whole_images(cotangent, patches, images)
    normed, unit_in, inv_in, cot_pad, normed_t, cot_t = prep(core_arg, tokens_rows, cot_rows, model_vectors, patches, pad)
    mix = jnp.pad(spatial.astype(LOW), ((0, pad - patches), (0, pad - patches)))
    mix_t = mix.T
    bias = jnp.broadcast_to(jnp.pad(patch_bias, (0, pad - patches))[:, None], (pad, 128))
    rest_mine = exchange_mp(rest_wire)
    gate_mine, mix, mix_t, bias = lax.optimization_barrier((gate_mine, mix, mix_t, bias, normed, rest_wire))[:4]
    gate_theirs = swap_core(gate_mine)
    gate_arg = jnp.stack([core, base]).astype(jnp.int32)

    [(gate_mine, _)], [(gate_theirs, _)] = regroup(gate_mine, 1), regroup(gate_theirs, 1)
    normal, unit, slope, scale, w_gate, vec_all = gate_forward(gate_arg, normed, gate_mine, gate_theirs, images, pad)
    rest_mine = after(rest_mine, normal)
    rest_theirs = swap_core(rest_mine)
    rest_mine, rest_theirs = (
        (parts[0][0] if parts[0][0] is parts[1][0] else jnp.concatenate([p[0] for p in parts], axis=2))
        for parts in (regroup(rest_mine, 2), regroup(rest_theirs, 2))
    )
    gated, low_value, low_gate, mine_one, theirs_one, mine_two, theirs_two, grad_mix, vec_sums = channels_both(
        core_arg, normed, cot_pad, normed_t, cot_t, normal, unit, slope, scale, rest_mine, rest_theirs,
        mix, mix_t, bias, vec_all, images, pad, ways if pad % ways == 0 else 1,
    )
    rides = mix_rides(shard, grad_mix)
    extra = EXTRA if shard % 128 == 0 else 2 * EXTRA
    mix_rows = (grad_mix, swap_core(grad_mix)) if rides else ()
    wire = merge(
        core_arg, mine_one, swap_core(theirs_one), mine_two, swap_core(theirs_two), vec_sums, swap_core(vec_sums), ways, extra, mix_rows
    )
    again = functools.partial(split_again, half, shard)
    output, grad_tokens, model_sums = token_back(
        core_arg, tokens_rows, cot_rows, unit_in, inv_in, gated, low_value, after(low_gate, wire),
        rest_mine, rest_theirs, w_gate, model_vectors, patches, pad,
    )

    parts = after(exchange_mp(wire), model_sums)
    model_at, model_width = (grad_mix.shape[2], 128) if rides else (0, shard)
    model_rows = 3 * width // model_width
    tail = model_sums[:3].reshape(model_rows, model_width)
    below = (half + MIX_ROW, extra - MIX_ROW - model_rows)
    plane = plane_sum(parts) + jnp.pad(tail, (below, (model_at, 3 * shard - model_at - model_width)))
    main = depth_sum(plane, again)
    main_other, count, wire = gram_wires(core_arg, main, moment_in, moment_out)
    parts = exchange_mp(wire)
    grad_w_in, new_moment_in, grad_w_out, new_moment_out, terms, kept = moments(
        core_arg, main, main_other, moment_in, moment_out, w_in
    )
    parts = after(parts, kept)
    grams = gather_mp(jnp.sum(parts[:, :count], axis=0))
    extra_rows = extra_rows_of(parts[:, count:], extra, shard)
    extra_rows = jnp.stack([extra_rows, swap_core(extra_rows)])

    vec = main[half : half + MIX_ROW, : 2 * shard].astype(F32)
    grad_vec = vec[:, :shard] + vec[:, shard:]
    tails = extra_rows[:, :, MIX_ROW : MIX_ROW + model_rows, model_at : model_at + model_width]
    tails = jnp.sum(tails, axis=1)
    grad_model = (tails[0] + tails[1]).reshape(3, width)
    if rides:
        each = grad_mix.shape[1] // 2
        rows = extra_rows[:, :, MIX_ROW : MIX_ROW + each, : grad_mix.shape[2]]
        rows = jnp.where(core == 0, rows, rows[::-1])
        grad_mix = jnp.concatenate([rows[0], rows[1]], axis=1)
    else:
        grad_mix = lax.psum(grad_mix, ("dp", "mp"))
    grad_mix = grad_mix.reshape(pad, -1)
    grad_spatial = grad_mix[:patches, :patches]
    grad_patch = grad_mix[:patches, pad]

    new_moment_mix = MOMENTUM * moment_mix + grad_spatial
    grams = after(grams, new_moment_mix)
    poly, ortho_mix = polynomials(core_arg, grams, full, new_moment_mix)
    new_w_in, new_w_out = update(core_arg, poly, swap_core(poly), terms, kept, w_out)
    shrink_by = 1.0 - MUON_RATE * DECAY_RATE
    new_spatial = spatial * shrink_by - MUON_RATE * 0.2 * math.sqrt(patches) * ortho_mix
    new_second_model, new_model = adam_update(model_vectors, grad_model, first_model, second_model)
    new_second_gate, new_gate = adam_update(gate_vectors, grad_vec, first_gate, second_gate)
    new_second_patch, new_patch = adam_update(patch_bias, grad_patch, first_patch, second_patch)
    return (
        held_rows(output, here),
        held_rows(grad_tokens, here),
        grad_w_in,
        grad_w_out,
        grad_spatial,
        grad_model,
        grad_vec,
        grad_patch,
        new_moment_in,
        new_moment_out,
        new_moment_mix,
        new_second_model,
        new_second_gate,
        new_second_patch,
        new_w_in,
        new_w_out,
        new_spatial,
        new_model,
        new_gate,
        new_patch,
    )


def solution(mesh):
    rows = P(("dp", "mp"), None)
    wide = P(None, None, "mp")
    tall = P("mp", None)
    columns = P(None, "mp")
    return jax.shard_map(
        per_device,
        mesh=mesh,
        in_specs=(
            (rows, rows, wide, tall, P(), P(), columns, P())
            + (wide, tall, P(), P(), P(), columns, columns, P(), P())
        ),
        out_specs=(
            (rows, rows, wide, tall, P(), P(), columns, P())
            + (wide, tall, P(), P(), columns, P())
            + (wide, tall, P(), P(), columns, P())
        ),
        check_vma=False,
    )
```

```python
import functools
import math

import jax
import jax.numpy as jnp
from jax import lax
from jax.experimental import pallas as pl
from jax.experimental.pallas import tpu as pltpu
from jax.sharding import PartitionSpec as P

STEP = 10
EPSILON = 1e-05
COEF_FIRST = 3.4445
COEF_SECOND = -4.775
COEF_THIRD = 2.0315
MOMENTUM = 0.95
MUON_RATE = 0.2
ADAM_RATE = 0.3
DECAY_RATE = 0.01
BETA_FIRST = 0.9
BETA_SECOND = 0.95
LOW = jnp.bfloat16
F32 = jnp.float32


ROW_TILE = 16
UNROLL = 3
EXTRA = 32
MIX_ROW = 4
CHUNK = 512
CUBIC = 0.044715
SLOPE = math.sqrt(2.0 / math.pi)


def compiler(megabytes):
    return pltpu.CompilerParams(vmem_limit_bytes=megabytes << 20)


def dot_nn(a, b):
    return jnp.dot(a, b, preferred_element_type=F32)


def dot_nt(a, b):
    return lax.dot_general(a, b, (((1,), (1,)), ((), ())), preferred_element_type=F32)


def gelu_pair(hidden):
    square = hidden * hidden
    half = 0.5 + 0.5 * jnp.tanh(hidden * (SLOPE + (SLOPE * CUBIC) * square))
    active = hidden * half
    slope = half + (active - active * half) * (2.0 * SLOPE + (6.0 * SLOPE * CUBIC) * square)
    return active, slope


def lanes(v):
    total = v[:, :128]
    for at in range(128, v.shape[1], 128):
        total = total + v[:, at : at + 128]
    return total


def eights(v):
    total = v[:8]
    for at in range(8, v.shape[0], 8):
        total = total + v[at : at + 8]
    return total


def wide(v, width):
    return jnp.concatenate([v] * (width // 128), axis=1) if width % 128 == 0 else v[:, :1]


def tiles(count, body, carry=None):
    for at in range(0, count, ROW_TILE):
        carry = body(slice(at, at + ROW_TILE), carry)
    return carry


def spread_pieces(core, mine, theirs, out, offset):
    half = out.shape[0] // 2
    count = mine.shape[0]
    shard = out.shape[1] // count
    first = pl.ds(pl.multiple_of(core[0] * half, half), half)
    other = pl.ds(pl.multiple_of((1 - core[0]) * half, half), half)
    for piece in range(count):
        cols = slice(piece * shard, (piece + 1) * shard)
        out[first, cols] = mine[piece, :half, offset : offset + shard]
        out[other, cols] = theirs[piece, :half, offset : offset + shard]


def gate_kernel(chunk, core, normed, mine, theirs, normal, unit, slope, scale, weight, vec, active):
    rows, full = active.shape
    half = weight.shape[0] // 2

    @pl.when(pl.program_id(0) == 0)
    def _():
        count, _, shard = mine.shape
        first = pl.ds(pl.multiple_of(core[0] * half, half), half)
        other = pl.ds(pl.multiple_of((1 - core[0]) * half, half), half)
        for piece in range(count):
            owner = jnp.bitwise_xor(core[1], piece) if count > 1 else 0
            cols = pl.ds(pl.multiple_of(owner * shard, shard), shard) if count > 1 else slice(0, shard)
            weight[first, cols] = mine[piece, :half, :]
            weight[other, cols] = theirs[piece, :half, :]
            terms = mine[piece, half:, :].astype(F32)
            vec[:, cols] = (terms[0:8] + terms[8:16]) + terms[16:24]

    starts = range(0, full, chunk)
    for at in starts:
        active[:, at : at + chunk] = dot_nn(normed[...], weight[:, at : at + chunk])

    def act(here, _):
        total = jnp.zeros((ROW_TILE, 128), F32)
        for at in starts:
            cols = slice(at, at + chunk)
            value, grad = gelu_pair(active[here, cols] + vec[1:2, cols])
            active[here, cols] = value
            slope[here, cols] = grad.astype(LOW)
            total = total + lanes(value)
        scale[here, :] = total

    tiles(rows, act)
    mean = jnp.sum(scale[...], axis=1, keepdims=True) * (1.0 / full)
    scale[...] = jnp.broadcast_to(mean, scale.shape)

    def spread(here, _):
        total = jnp.zeros((ROW_TILE, 128), F32)
        mean_here = wide(scale[here, :], chunk)
        for at in starts:
            cols = slice(at, at + chunk)
            centred = active[here, cols] - mean_here
            active[here, cols] = centred
            total = total + lanes(centred * centred)
        scale[here, :] = total

    tiles(rows, spread)
    var = jnp.sum(scale[...], axis=1, keepdims=True) * (1.0 / full)
    scale[...] = jnp.broadcast_to(lax.rsqrt(var + EPSILON), scale.shape)

    def finish(here, _):
        inv = wide(scale[here, :], chunk)
        for at in starts:
            cols = slice(at, at + chunk)
            unit_here = active[here, cols] * inv
            unit[here, cols] = unit_here.astype(LOW)
            normal[here, cols] = (unit_here * vec[2:3, cols] + vec[3:4, cols]).astype(LOW)

    tiles(rows, finish)


def gate_forward(core, normed, mine, theirs, images, pad):
    count, _, shard = mine.shape
    full = count * shard
    width = normed.shape[1]
    chunk = 512 if full % 512 == 0 else full
    total = images * pad
    whole = lambda a: pl.BlockSpec(a.shape, lambda i, c: (0,) * a.ndim, pipeline_mode=pl.Buffered(1))
    rows = lambda n: pl.BlockSpec((pad, n), lambda i, c: (i, 0))
    fixed = lambda *f: pl.BlockSpec(f, lambda i, c: (0, 0))
    shape = jax.ShapeDtypeStruct
    return pl.pallas_call(
        functools.partial(gate_kernel, chunk),
        grid_spec=pltpu.PrefetchScalarGridSpec(
            num_scalar_prefetch=1,
            grid=(images,),
            in_specs=[rows(width), whole(mine), whole(theirs)],
            out_specs=[rows(full), rows(full), rows(full), rows(128), fixed(width, full), fixed(8, full)],
            scratch_shapes=[pltpu.VMEM((pad, full), F32)],
        ),
        out_shape=[shape((total, full), LOW)] * 3
        + [shape((total, 128), F32), shape((width, full), LOW), shape((8, full), F32)],
        compiler_params=compiler(60),
        cost_estimate=pl.CostEstimate(
            flops=2 * total * width * full, bytes_accessed=8 * total * full, transcendentals=total * full
        ),
        name="gate_forward",
    )(core, normed, mine, theirs)


def value_kernel(
    pad,
    images,
    core,
    normed,
    cot,
    normed_t_far,
    cot_t_far,
    normal,
    unit,
    slope_far,
    scale_far,
    w_mine,
    w_theirs,
    mix,
    mix_t,
    bias,
    vec,
    gated,
    low_value,
    low_gate,
    mine,
    theirs,
    mine_gate,
    theirs_gate,
    mix_pieces,
    vec_sums,
    w_value,
    w_back,
    sums,
    grad_mix,
    grad_bias,
    grad_unit,
    hidden,
    back,
    mixed,
    turned,
    low_mixed,
    low_pad,
    gated_pad,
    normed_t,
    cot_t,
    slope_gate,
    scale,
    arrived,
):
    total, chunk = gated.shape
    half = w_value.shape[0] // 2
    step = pl.program_id(0)
    count = pl.num_programs(0) // 2
    cols = pl.ds(pl.multiple_of(lax.rem(step, count) * chunk, chunk), chunk)

    late = (
        pltpu.make_async_copy(normed_t_far, normed_t, arrived.at[0]),
        pltpu.make_async_copy(cot_t_far, cot_t, arrived.at[1]),
        pltpu.make_async_copy(slope_far, slope_gate, arrived.at[2]),
        pltpu.make_async_copy(scale_far, scale, arrived.at[3]),
    )

    @pl.when(step == 0)
    def _():
        for copy in late:
            copy.start()
        offset = w_mine.shape[2] - w_value.shape[1] // w_mine.shape[0]
        spread_pieces(core, w_mine, w_theirs, w_value, 0)
        spread_pieces(core, w_mine, w_theirs, w_back, offset)
        sums[...] = jnp.zeros_like(sums)
        vec_sums[...] = jnp.zeros_like(vec_sums)
        grad_mix[...] = jnp.zeros_like(grad_mix)
        grad_bias[...] = jnp.zeros_like(grad_bias)
        low_pad[total:, :] = jnp.zeros_like(low_pad[total:, :])
        gated_pad[total:, :] = jnp.zeros_like(gated_pad[total:, :])

    pairs = ((hidden.at[0], back.at[0], mixed.at[0]), (hidden.at[1], back.at[1], mixed.at[1]))

    def products(image):
        here = slice(image * pad, (image + 1) * pad)
        hid, bck, mxd = pairs[image % 2]
        hid[...] = dot_nn(normed[here, :], w_value[:, cols])
        bck[...] = dot_nn(cot[here, :], w_back[:, cols])
        mxd[...] = dot_nn(mix[...], normal[here, :])

    def forward(image, sums):
        hid, bck, mxd = pairs[image % 2]
        for row in range(0, pad, ROW_TILE):
            at = slice(row, row + ROW_TILE)
            here = slice(image * pad + row, image * pad + row + ROW_TILE)
            value, slope = gelu_pair(hid[at, :] + vec[0:1, :])
            mixed_here = mxd[at, :] + wide(bias[at, :], chunk)
            back_here = bck[at, :]
            gated_here = (value * mixed_here).astype(LOW)
            gated[here, :] = gated_here
            gated_pad[here, :] = gated_here
            grad_here = (back_here * value).astype(LOW)
            low_mixed[image % 2, at, :] = grad_here
            grad_bias[at, :] += lanes(grad_here.astype(F32))
            low_here = (back_here * mixed_here * slope).astype(LOW)
            low_value[here, :] = low_here
            low_pad[here, :] = low_here
            sums = sums + eights(low_here.astype(F32))
        return sums

    def turn(image):
        here = slice(image * pad, (image + 1) * pad)
        turned[image % 2] = dot_nn(mix_t[...], low_mixed[image % 2])
        grad_mix[:, :pad] += dot_nt(low_mixed[image % 2], normal[here, :])

    def backward(image, kept):
        for row in range(0, pad, ROW_TILE):
            at = slice(row, row + ROW_TILE)
            here = slice(image * pad + row, image * pad + row + ROW_TILE)
            grad = turned[image % 2, at, :]
            unit_here = unit[here, :].astype(F32)
            gain = vec[2:3, :]
            both = grad * unit_here
            du = grad * gain
            grad_unit[here, cols] = du.astype(LOW)
            sums[0, here, :] += lanes(du)
            sums[1, here, :] += lanes(both * gain)
            kept = kept[0] + eights(both), kept[1] + eights(grad)
        return kept

    @pl.when(step < count)
    def _():
        zero = jnp.zeros((8, chunk), F32)
        bias_sum, norm_sums = zero, (zero, zero)
        products(0)
        for image in range(images):
            if image + 1 < images:
                products(image + 1)
            bias_sum = forward(image, bias_sum)
            turn(image)
            if image:
                norm_sums = backward(image - 1, norm_sums)
        norm_sums = backward(images - 1, norm_sums)
        gain_sum, shift_sum = norm_sums


        @pl.when(step == 0)
        def _():
            late[0].wait()
            late[1].wait()

        for i, product in enumerate((dot_nn(normed_t[...], low_pad[...]), dot_nn(cot_t[...], gated_pad[...]))):
            mine[i, :half, :] = product[:half].astype(LOW)
            theirs[i, :half, :] = product[half:].astype(LOW)

        total_of = lambda v: jnp.sum(v, axis=0, keepdims=True)
        vec_sums[0:1, cols] = total_of(bias_sum)
        vec_sums[2:3, cols] = total_of(gain_sum)
        vec_sums[3:4, cols] = total_of(shift_sum)

    @pl.when(step == count - 1)
    def _():
        patch = jnp.sum(grad_bias[...], axis=1, keepdims=True)
        grad_mix[:, pad:] = jnp.broadcast_to(patch, (pad, grad_mix.shape[1] - pad))
        each = mix_pieces.shape[1]
        for piece in range(mix_pieces.shape[0]):
            mix_pieces[piece] = grad_mix[piece * each : (piece + 1) * each, :]


    def gate_tile(i, total_here):
        here = slice(i * ROW_TILE, (i + 1) * ROW_TILE)
        one = wide(sums[0, here, :], chunk)
        two = wide(sums[1, here, :], chunk)
        inv = wide(scale[here, :], chunk)
        grad = inv * (grad_unit[here, cols].astype(F32) - one - unit[here, :].astype(F32) * two)
        low = (grad * slope_gate[here, cols].astype(F32)).astype(LOW)
        low_gate[here, :] = low
        low_pad[here, :] = low
        return total_here + eights(low.astype(F32))

    @pl.when(step == count)
    def _():
        late[2].wait()
        late[3].wait()
        for i in range(2):
            mean = jnp.sum(sums[i], axis=1, keepdims=True) * (1.0 / w_value.shape[1])
            sums[i] = jnp.broadcast_to(mean, (total, 128))

    @pl.when(step >= count)
    def _():
        kept = jnp.zeros((8, chunk), F32)
        for at in range(total // ROW_TILE):
            kept = gate_tile(at, kept)
        vec_sums[1:2, cols] = jnp.sum(kept, axis=0, keepdims=True)
        product = dot_nn(normed_t[...], low_pad[...])
        mine_gate[:half, :] = product[:half].astype(LOW)
        theirs_gate[:half, :] = product[half:].astype(LOW)


def channels_both(
    core, normed, cot, normed_t, cot_t, normal, unit, slope, scale, w_mine, w_theirs, mix, mix_t, bias, vec, images, pad, ways
):
    width = normed.shape[1]
    full = normal.shape[1]
    total = images * pad
    deep = normed_t.shape[1]
    chunk = CHUNK if full % CHUNK == 0 else full
    count = full // chunk
    half = width // 2
    wide_mix = -(-(pad + 1) // 128) * 128
    mix_shape = (ways, pad // ways, wide_mix)
    whole = lambda a: pl.BlockSpec(a.shape, lambda i, c: (0,) * a.ndim, pipeline_mode=pl.Buffered(1))
    early = lambda n: pl.BlockSpec((n, chunk), lambda i, c: (0, jnp.minimum(i, count - 1)))
    late = lambda n: pl.BlockSpec((n, chunk), lambda i, c: (0, jnp.maximum(i - count, 0)))
    twice = lambda n: pl.BlockSpec((n, chunk), lambda i, c: (0, lax.rem(i, count)))
    pair = pl.BlockSpec((2, half, chunk), lambda i, c: (0, 0, jnp.minimum(i, count - 1)))
    shape = jax.ShapeDtypeStruct
    far = pl.BlockSpec(memory_space=pl.ANY)
    return pl.pallas_call(
        functools.partial(value_kernel, pad, images),
        grid_spec=pltpu.PrefetchScalarGridSpec(
            num_scalar_prefetch=1,
            grid=(2 * count,),
            in_specs=[whole(normed), whole(cot), far, far]
            + [early(total), twice(total), far, far, whole(w_mine), whole(w_theirs)]
            + [whole(mix), whole(mix_t), whole(bias), early(8)],
            out_specs=[early(total), early(total), late(total), pair, pair, late(half), late(half)]
            + [pl.BlockSpec(mix_shape, lambda i, c: (0, 0, 0)), pl.BlockSpec((8, full), lambda i, c: (0, 0))],
            scratch_shapes=[pltpu.VMEM((width, full), LOW)] * 2
            + [pltpu.VMEM((2, total, 128), F32), pltpu.VMEM((pad, wide_mix), F32), pltpu.VMEM((pad, 128), F32)]
            + [pltpu.VMEM((total, full), LOW)]
            + [pltpu.VMEM((2, pad, chunk), F32)] * 4
            + [pltpu.VMEM((2, pad, chunk), LOW)]
            + [pltpu.VMEM((deep, chunk), LOW)] * 2
            + [pltpu.VMEM((width, deep), LOW)] * 2
            + [pltpu.VMEM((total, full), LOW), pltpu.VMEM((total, 128), F32), pltpu.SemaphoreType.DMA((4,))],
        ),
        out_shape=[shape((total, full), LOW)] * 3
        + [shape((2, half, full), LOW)] * 2
        + [shape((half, full), LOW)] * 2 + [shape(mix_shape, F32), shape((8, full), F32)],
        compiler_params=compiler(60),
        cost_estimate=pl.CostEstimate(
            flops=14 * total * width * full, bytes_accessed=24 * total * full, transcendentals=total * full
        ),
        name="channels_both",
    )(core, normed, cot, normed_t, cot_t, normal, unit, slope, scale, w_mine, w_theirs, mix, mix_t, bias, vec)


def gate_wire_kernel(core, w_in, vectors, wire):
    half, _, shard = w_in.shape
    low = w_in[:, 1, :].astype(LOW)
    value = jnp.concatenate([vectors[...], jnp.zeros((4, shard), F32)], axis=0)
    high = value.astype(LOW).astype(F32)
    middle = (value - high).astype(LOW).astype(F32)
    last = value - high - middle
    terms = jnp.concatenate([high, middle, last, jnp.zeros((8, shard), F32)], axis=0).astype(LOW)
    wire[:half, :] = low
    wire[half:, :] = terms


def rest_wire_kernel(core, w_in, w_out, wire):
    shard = w_in.shape[2]
    value = w_in[:, 0, :].astype(LOW)
    back = w_out[...].T.astype(LOW)
    for receiver in range(wire.shape[0]):
        wire[receiver, :, :shard] = value
        wire[receiver, :, shard:] = back


def weight_wires(core, w_in, w_out, vectors):
    width, _, shard = w_in.shape
    half = width // 2
    ways = lax.axis_size("mp")
    rows = pl.BlockSpec((half, 2, shard), lambda i, c: (c[0], 0, 0))
    fixed = lambda *f: pl.BlockSpec(f, lambda i, c: (0,) * len(f))
    spec = lambda ins, out: pltpu.PrefetchScalarGridSpec(
        num_scalar_prefetch=1, grid=(1,), in_specs=ins, out_specs=fixed(*out)
    )
    out = (half + 32, shard)
    gate = pl.pallas_call(
        gate_wire_kernel,
        grid_spec=spec([rows, fixed(4, shard)], out),
        out_shape=jax.ShapeDtypeStruct(out, LOW),
        compiler_params=compiler(60),
        name="gate_wire",
    )(core, w_in, vectors)
    out = (ways, half, 2 * shard)
    if shard % 128:
        back = lax.dynamic_slice_in_dim(w_out, core[0] * half, half, 1)
        rest = jnp.concatenate([core_rows(w_in[:, 0], core[0]), back.T], axis=1).astype(LOW)
        return gate, copies(rest, ways)
    rest = pl.pallas_call(
        rest_wire_kernel,
        grid_spec=spec([rows, pl.BlockSpec((shard, half), lambda i, c: (0, c[0]))], out),
        out_shape=jax.ShapeDtypeStruct(out, LOW),
        compiler_params=compiler(60),
        name="rest_wire",
    )(core, w_in, w_out)
    return gate, rest


def merge_kernel(core, mine, theirs, mine_gate, theirs_gate, vec, vec_other, *refs):
    wire = refs[-1]
    _, half, shard = mine.shape
    parts = ((mine.at[0], theirs.at[0]), (mine_gate, theirs_gate), (mine.at[1], theirs.at[1]))
    for i, (own, other) in enumerate(parts):
        wire[0, :half, i * shard : (i + 1) * shard] = (own[...].astype(F32) + other[...].astype(F32)).astype(LOW)
    extra = wire.shape[1] - half
    rows = [(vec[...] + vec_other[...])[:MIX_ROW]]
    if len(refs) > 1:
        mix = refs[0][0] + refs[1][0]
        each = mix.shape[0] // 2
        mix = jnp.where(core[0] == 0, mix[:each], mix[each:])
        rows.append(jnp.concatenate([mix, jnp.zeros((mix.shape[0], shard - mix.shape[1]), F32)], axis=1))
    rows.append(jnp.zeros((extra - sum(r.shape[0] for r in rows), shard), F32))
    rows = jnp.concatenate(rows, axis=0)
    high = rows.astype(LOW).astype(F32)
    for i, part in enumerate((high, rows - high, jnp.zeros_like(rows))):
        wire[0, half:, i * shard : (i + 1) * shard] = part.astype(LOW)


def merge(core, mine, theirs, mine_gate, theirs_gate, vec, vec_other, ways, extra, mix):
    _, rows, full = mine.shape
    shard = full // ways
    if shard % 128:
        both = mine.astype(F32) + theirs.astype(F32)
        both = jnp.stack([both[0], mine_gate.astype(F32) + theirs_gate.astype(F32), both[1]])
        more = jnp.pad((vec + vec_other)[:MIX_ROW], ((0, extra - MIX_ROW), (0, 0)))
        high = lax.reduce_precision(more, 8, 7)
        both = jnp.concatenate([both, jnp.stack([high, more - high, jnp.zeros_like(more)])], axis=1)
        blocks = both.reshape(3, rows + extra, ways, shard).transpose(2, 1, 0, 3)
        return blocks.reshape(ways, rows + extra, 3 * shard).astype(LOW)
    pair = pl.BlockSpec((2, rows, shard), lambda i, c: (0, 0, i))
    block = lambda n: pl.BlockSpec((n, shard), lambda i, c: (0, i))
    return pl.pallas_call(
        merge_kernel,
        grid_spec=pltpu.PrefetchScalarGridSpec(
            num_scalar_prefetch=1,
            grid=(ways,),
            in_specs=[pair, pair, block(rows), block(rows), block(8), block(8)]
            + [pl.BlockSpec((1,) + m.shape[1:], lambda i, c: (i, 0, 0)) for m in mix],
            out_specs=pl.BlockSpec((1, rows + extra, 3 * shard), lambda i, c: (i, 0, 0)),
        ),
        out_shape=jax.ShapeDtypeStruct((ways, rows + extra, 3 * shard), LOW),
        compiler_params=compiler(60),
        name="merge",
    )(core, mine, theirs, mine_gate, theirs_gate, vec, vec_other, *mix)


def mix_rides(shard, mix):
    return shard % 128 == 0 and mix.shape[2] + 128 <= shard and mix.shape[0] > 1 and mix.shape[1] % 2 == 0 and (
        mix.shape[1] // 2 + MIX_ROW <= EXTRA
    )


def gram_kernel(count, core, main, other, old_in, old_out, wire, moment):
    width, _, shard = old_in.shape
    half = width // 2
    halves = (
        (pl.ds(pl.multiple_of(core[0] * half, half), half), main),
        (pl.ds(pl.multiple_of((1 - core[0]) * half, half), half), other),
    )

    @pl.when(core[0] == 0)
    def _():
        moment[:, :shard] = MOMENTUM * old_out[...].T
        moment[:, shard:] = jnp.zeros((width, shard), F32)
        for rows, part in halves:
            moment[rows, :shard] += part[:half, 2 * shard :].astype(F32)

    @pl.when(core[0] == 1)
    def _():
        for i in range(2):
            cols = slice(i * shard, (i + 1) * shard)
            moment[:, cols] = MOMENTUM * old_in[:, i, :]
            for rows, part in halves:
                moment[rows, cols] += part[:half, cols].astype(F32)

    high, low = split_two(moment[...])
    rows = (slice(0, half), slice(half, width))
    blocks = []
    for i, j in ((0, 0), (0, 1), (1, 1)):
        i, j = rows[i], rows[j]
        cross = dot_nt(high[i], low[j]) + dot_nt(low[i], high[j])
        blocks.append(dot_nt(high[i], high[j]) + cross)
    blocks = jnp.concatenate(blocks, axis=0)
    terms = main[half:, :].astype(F32)
    terms = terms[:, :shard] + terms[:, shard : 2 * shard]
    extra = terms.shape[0]
    for receiver in range(wire.shape[0]):
        wire[receiver, :count, :] = blocks[receiver * count : (receiver + 1) * count]
        for i, at in enumerate(range(0, shard, 128)):
            part = terms[:, at : at + 128]
            top, left = count + i // 2 * extra, i % 2 * 128
            wire[receiver, top : top + extra, left : left + part.shape[1]] = part


def gram_wires(core, main, old_in, old_out):
    width, _, shard = old_in.shape
    half = width // 2
    ways = lax.axis_size("mp")
    count = 3 * half // ways
    extra = main.shape[0] - half
    rows = count + extra * -(-shard // 256)
    fixed = lambda *f: pl.BlockSpec(f, lambda i, c: (0,) * len(f))
    ins = (main, swap_core(main), old_in, old_out)
    out = (ways, rows, half)
    return ins[1], count, pl.pallas_call(
        functools.partial(gram_kernel, count),
        grid_spec=pltpu.PrefetchScalarGridSpec(
            num_scalar_prefetch=1,
            grid=(1,),
            in_specs=[fixed(*a.shape) for a in ins],
            out_specs=fixed(*out),
            scratch_shapes=[pltpu.VMEM((width, 2 * shard), F32)],
        ),
        out_shape=jax.ShapeDtypeStruct(out, F32),
        compiler_params=compiler(60),
        name="gram_wires",
    )(core, *ins)


def extra_rows_of(parts, extra, shard):
    pieces = []
    for i, at in enumerate(range(0, shard, 128)):
        top, left = i // 2 * extra, i % 2 * 128
        pieces.append(parts[..., top : top + extra, left : left + min(128, shard - at)])
    return jnp.concatenate(pieces, axis=-1)


def moments_kernel(core, main, other, old_in, old_out, w_in, grad_in, new_in, grad_out, new_out, terms, kept, flat):
    width, _, shard = old_in.shape
    half = width // 2
    rows = (
        pl.ds(pl.multiple_of(core[0] * half, half), half),
        pl.ds(pl.multiple_of((1 - core[0]) * half, half), half),
    )
    for here, part in ((rows[0], main), (rows[1], other)):
        for i in range(3):
            flat[i, here, :] = part[:half, i * shard : (i + 1) * shard].astype(F32)
    for i in range(2):
        grad = flat[i]
        grad_in[:, i, :] = grad
        moment = MOMENTUM * old_in[:, i, :] + grad
        new_in[:, i, :] = moment
        terms[0, i], terms[1, i] = split_two(moment)
        kept[i] = w_in[:, i, :] * (1.0 - MUON_RATE * DECAY_RATE)
    grad = flat[2].T
    grad_out[...] = grad
    moment = MOMENTUM * old_out[...] + grad
    new_out[...] = moment
    terms[0, 2], terms[1, 2] = split_two(moment.T)


def moments(core, main, other, old_in, old_out, w_in):
    width, _, shard = old_in.shape
    ins = (main, other, old_in, old_out, w_in)
    shapes = (
        [(width, 2, shard)] * 2 + [(shard, width)] * 2 + [(2, 3, width, shard), (2, width, shard)]
    )
    fixed = lambda f: pl.BlockSpec(f, lambda i, c, n=len(f): (0,) * n)
    return pl.pallas_call(
        moments_kernel,
        grid_spec=pltpu.PrefetchScalarGridSpec(
            num_scalar_prefetch=1,
            grid=(1,),
            in_specs=[fixed(a.shape) for a in ins],
            out_specs=[fixed(f) for f in shapes],
            scratch_shapes=[pltpu.VMEM((3, width, shard), F32)],
        ),
        out_shape=[jax.ShapeDtypeStruct(f, LOW if len(f) == 4 else F32) for f in shapes],
        compiler_params=compiler(60),
        name="moments",
    )(core, *ins)


def prep_kernel(patches, pad, core, tokens, cot, model, normed, unit, scale, cot_pad, normed_t, cot_t, keep):
    step = pl.program_id(0)
    group = tokens.shape[1] // patches
    rows = group * pad
    width = tokens.shape[2]

    def padded(block):
        block = block[0].astype(F32)
        gap = jnp.zeros((pad - patches, width), F32)
        parts = []
        for image in range(group):
            parts += [block[image * patches : (image + 1) * patches], gap]
        return jnp.concatenate(parts, axis=0)

    here = pl.ds(pl.multiple_of(step * rows, rows), rows)

    @pl.when(step == 0)
    def _():
        keep[...] = jnp.zeros_like(keep)

    cot_here = padded(cot)
    cot_pad[...] = cot_here.astype(LOW)
    keep[1, here, :] = cot_here
    x = padded(tokens)
    centred = x - jnp.sum(x, axis=1, keepdims=True) * (1.0 / width)
    inv = lax.rsqrt(jnp.sum(centred * centred, axis=1, keepdims=True) * (1.0 / width) + EPSILON)
    unit_here = centred * inv
    scale[...] = jnp.broadcast_to(inv, scale.shape)
    unit[...] = unit_here.astype(LOW)
    low = (unit_here * model[0:1, :] + model[1:2, :]).astype(LOW)
    normed[...] = low
    keep[0, here, :] = low.astype(F32)

    @pl.when(step == pl.num_programs(0) - 1)
    def _():
        half = width // 2
        for i, place in enumerate((core[0], 1 - core[0])):
            features = pl.ds(pl.multiple_of(place * half, half), half)
            rows_out = slice(i * half, (i + 1) * half)
            for at in range(0, normed_t.shape[1], 128):
                cols = slice(at, at + 128)
                normed_t[rows_out, cols] = keep[0, cols, features].T.astype(LOW)
                cot_t[rows_out, cols] = keep[1, cols, features].T.astype(LOW)


def prep(core, tokens, cot, model, patches, pad):
    here, width = tokens.shape
    images = here // patches
    group = 2 if images % 2 == 0 else images
    steps = images // group
    total = images * pad
    deep = -(-total // 128) * 128
    block = pl.BlockSpec((1, group * patches, width), lambda i, c: (i, 0, 0))
    rows = lambda n: pl.BlockSpec((group * pad, n), lambda i, c: (i, 0))
    fixed = lambda *f: pl.BlockSpec(f, lambda i, c: (0, 0))
    shape = jax.ShapeDtypeStruct
    return pl.pallas_call(
        functools.partial(prep_kernel, patches, pad),
        grid_spec=pltpu.PrefetchScalarGridSpec(
            num_scalar_prefetch=1,
            grid=(steps,),
            in_specs=[block, block, fixed(3, width)],
            out_specs=[rows(width), rows(width), rows(128), rows(width), fixed(width, deep), fixed(width, deep)],
            scratch_shapes=[pltpu.VMEM((2, deep, width), F32)],
        ),
        out_shape=[
            shape((total, width), LOW),
            shape((total, width), LOW),
            shape((total, 128), F32),
            shape((total, width), LOW),
            shape((width, deep), LOW),
            shape((width, deep), LOW),
        ],
        compiler_params=compiler(60),
        cost_estimate=pl.CostEstimate(flops=20 * total * width, bytes_accessed=20 * total * width, transcendentals=total),
        name="prep",
    )(core, tokens.reshape(steps, group * patches, width), cot.reshape(steps, group * patches, width), model)


def token_kernel(
    patches,
    pad,
    core,
    tokens,
    cot,
    unit,
    scale,
    gated,
    low_value,
    low_gate,
    w_mine,
    w_theirs,
    w_gate,
    model,
    output,
    grad_tokens,
    sums,
    w_value,
    w_back,
    branch,
    grad,
):
    group = tokens.shape[1] // patches
    width = tokens.shape[2]
    rows = group * pad

    @pl.when(pl.program_id(0) == 0)
    def _():
        sums[...] = jnp.zeros_like(sums)
        offset = w_mine.shape[2] - w_value.shape[1] // w_mine.shape[0]
        spread_pieces(core, w_mine, w_theirs, w_value, 0)
        spread_pieces(core, w_mine, w_theirs, w_back, offset)

    def packed(v):
        return jnp.concatenate([v[i * pad : i * pad + patches] for i in range(group)], axis=0)

    branch[...] = dot_nt(gated[...], w_back[...])
    output[0] = (tokens[0].astype(F32) + packed(branch) + model[2:3, :]).astype(LOW)
    grad[...] = dot_nt(low_value[...], w_value[...]) + dot_nt(low_gate[...], w_gate[...])

    def back(i, kept):
        here = pl.ds(pl.multiple_of(i * ROW_TILE, ROW_TILE), ROW_TILE)
        grad_here = grad[here, :]
        unit_here = unit[here, :].astype(F32)
        both = grad_here * unit_here
        du = grad_here * model[0:1, :]
        first = jnp.sum(du, axis=1, keepdims=True) * (1.0 / width)
        second = jnp.sum(both * model[0:1, :], axis=1, keepdims=True) * (1.0 / width)
        branch[here, :] = wide(scale[here, :], width) * (du - first - unit_here * second)
        return kept[0] + eights(both), kept[1] + eights(grad_here)

    zero = jnp.zeros((8, width), F32)
    gain, shift = lax.fori_loop(0, rows // ROW_TILE, back, (zero, zero), unroll=2)
    cot_here = cot[0].astype(F32)
    grad_tokens[0] = (cot_here + packed(branch)).astype(LOW)
    sums[0:1, :] += jnp.sum(gain, axis=0, keepdims=True)
    sums[1:2, :] += jnp.sum(shift, axis=0, keepdims=True)
    sums[2:3, :] += jnp.sum(eights(cot_here), axis=0, keepdims=True)


def token_back(core, tokens, cot, unit, scale, gated, low_value, low_gate, w_mine, w_theirs, w_gate, model, patches, pad):
    here, width = tokens.shape
    full = w_gate.shape[1]
    images = here // patches
    group = 2 if images % 2 == 0 else images
    steps = images // group
    total = images * pad
    block = pl.BlockSpec((1, group * patches, width), lambda i, c: (i, 0, 0))
    rows = lambda n: pl.BlockSpec((group * pad, n), lambda i, c: (i, 0))
    whole = lambda a: pl.BlockSpec(a.shape, lambda i, c: (0,) * a.ndim, pipeline_mode=pl.Buffered(1))
    shape = jax.ShapeDtypeStruct
    output, grad_tokens, sums = pl.pallas_call(
        functools.partial(token_kernel, patches, pad),
        grid_spec=pltpu.PrefetchScalarGridSpec(
            num_scalar_prefetch=1,
            grid=(steps,),
            in_specs=[block, block, rows(width), rows(128), rows(full), rows(full), rows(full)]
            + [whole(w_mine), whole(w_theirs), whole(w_gate), whole(model)],
            out_specs=[block, block, pl.BlockSpec((8, width), lambda i, c: (0, 0))],
            scratch_shapes=[pltpu.VMEM((width, full), LOW)] * 2 + [pltpu.VMEM((group * pad, width), F32)] * 2,
        ),
        out_shape=[shape((steps, group * patches, width), LOW)] * 2 + [shape((8, width), F32)],
        compiler_params=compiler(60),
        cost_estimate=pl.CostEstimate(
            flops=6 * total * width * full, bytes_accessed=8 * total * full, transcendentals=0
        ),
        name="token_back",
    )(
        core,
        tokens.reshape(steps, group * patches, width),
        cot.reshape(steps, group * patches, width),
        unit, scale, gated, low_value, low_gate, w_mine, w_theirs, w_gate, model,
    )
    return output.reshape(here, width), grad_tokens.reshape(here, width), sums


def split_two(v):
    high = v.astype(LOW)
    return high, (v - high.astype(F32)).astype(LOW)


def dot3(a, b):
    return dot_nn(a[0], b[0]) + (dot_nn(a[0], b[1]) + dot_nn(a[1], b[0]))


def symmetric3(a, b):
    half = a[0].shape[0] // 2
    top = dot3([v[:half] for v in a], b)
    corner = dot3([v[half:] for v in a], [v[:, half:] for v in b])
    bottom = jnp.concatenate([top[:, half:].T, corner], axis=1)
    return jnp.concatenate([top, bottom], axis=0)


def square_kernel(moment, ortho, now):
    few = moment.shape[0]
    now[...] = jnp.zeros_like(now)
    start = moment[...]
    now[:few, :few] = start / (jnp.sqrt(jnp.sum(start * start, keepdims=True)) + 1e-07)
    for sweep in range(5):
        x = now[...]
        x_two = split_two(x)
        gram = dot_nt(x_two[0], x_two[0]) + (dot_nt(x_two[0], x_two[1]) + dot_nt(x_two[1], x_two[0]))
        gram_two = split_two(gram)
        extra = COEF_SECOND * gram + COEF_THIRD * dot3(gram_two, gram_two)
        now[...] = COEF_FIRST * x + dot3(split_two(extra), x_two)
    ortho[...] = now[:few, :few]


def square_orthogonal(moment):
    edge = -(-moment.shape[0] // 128) * 128
    return pl.pallas_call(
        square_kernel,
        out_shape=jax.ShapeDtypeStruct(moment.shape, F32),
        scratch_shapes=[pltpu.VMEM((edge, edge), F32)],
        compiler_params=compiler(60),
        name="square_orthogonal",
    )(moment)


def polynomial_kernel(rates, core, pieces, poly, blocks, gram_now, total):
    size = gram_now.shape[0]
    half = size // 2
    count = pieces.shape[1]
    for piece in range(pieces.shape[0]):
        blocks[piece * count : (piece + 1) * count, :] = pieces[piece]
    gram_now[:half, :half] = blocks[:half]
    gram_now[:half, half:] = blocks[half:size]
    gram_now[half:, :half] = blocks[half:size].T
    gram_now[half:, half:] = blocks[size:]
    gram = gram_now[...]
    row = lax.broadcasted_iota(jnp.int32, (size, size), 0)
    col = lax.broadcasted_iota(jnp.int32, (size, size), 1)
    same = row == col
    norm = jnp.sqrt(jnp.sum(jnp.where(same, gram, 0.0), keepdims=True)) + 1e-07
    inv = 1.0 / norm
    gram_now[...] = gram * (inv * inv)
    for sweep in range(5):
        matrix = gram_now[...]
        matrix_two = split_two(matrix)
        extra = COEF_SECOND * matrix + COEF_THIRD * symmetric3(matrix_two, matrix_two)
        extra_two = split_two(extra)
        if sweep == 0:
            total[...] = jnp.where(same, COEF_FIRST + extra, extra)
        else:
            total[...] = COEF_FIRST * total[...] + symmetric3(extra_two, split_two(total[...]))
        if sweep < 4:
            partial = COEF_FIRST * matrix + symmetric3(extra_two, matrix_two)
            gram_now[...] = COEF_FIRST * partial + symmetric3(extra_two, split_two(partial))
    rate = jnp.where(core[0] == 0, rates[0], rates[1])
    poly[...] = total[...] * (inv * rate)


def polynomials(core, pieces, full):
    half = pieces.shape[2]
    size = 2 * half
    rates = [MUON_RATE * 0.2 * math.sqrt(max(size, n)) for n in (full, 2 * full)]
    fixed = lambda *f: pl.BlockSpec(f, lambda i, c: (0,) * len(f))
    return pl.pallas_call(
        functools.partial(polynomial_kernel, rates),
        grid_spec=pltpu.PrefetchScalarGridSpec(
            num_scalar_prefetch=1,
            grid=(1,),
            in_specs=[fixed(*pieces.shape)],
            out_specs=fixed(size, size),
            scratch_shapes=[pltpu.VMEM((3 * half, half), F32)] + [pltpu.VMEM((size, size), F32)] * 2,
        ),
        out_shape=jax.ShapeDtypeStruct((size, size), F32),
        compiler_params=compiler(60),
        cost_estimate=pl.CostEstimate(
            flops=2 * size * size * 51 * size, bytes_accessed=16 * size * size, transcendentals=0
        ),
        name="polynomials",
    )(core, pieces)


def update_kernel(core, mine, theirs, terms, kept, w_out, new_in, new_out):
    zero = core[0] == 0
    shrink_by = 1.0 - MUON_RATE * DECAY_RATE
    poly_out = split_two(jnp.where(zero, mine[...], theirs[...]))
    new_out[...] = w_out[...] * shrink_by - dot3(poly_out, (terms[0, 2], terms[1, 2])).T
    poly_in = split_two(jnp.where(zero, theirs[...], mine[...]))
    for i in range(2):
        new_in[:, i, :] = kept[i] - dot3(poly_in, (terms[0, i], terms[1, i]))


def update(core, mine, theirs, terms, kept, w_out):
    _, width, shard = kept.shape
    rows = 256 if width % 256 == 0 else width
    tall = pl.BlockSpec((rows, width), lambda i, c: (i, 0))
    fixed = pl.BlockSpec(terms.shape, lambda i, c: (0, 0, 0, 0), pipeline_mode=pl.Buffered(1))
    outer = pl.BlockSpec((shard, rows), lambda i, c: (0, i))
    return pl.pallas_call(
        update_kernel,
        grid_spec=pltpu.PrefetchScalarGridSpec(
            num_scalar_prefetch=1,
            grid=(width // rows,),
            in_specs=[tall, tall, fixed, pl.BlockSpec((2, rows, shard), lambda i, c: (0, i, 0)), outer],
            out_specs=[pl.BlockSpec((rows, 2, shard), lambda i, c: (i, 0, 0)), outer],
        ),
        out_shape=[jax.ShapeDtypeStruct((width, 2, shard), F32), jax.ShapeDtypeStruct(w_out.shape, F32)],
        compiler_params=compiler(60),
        name="update",
    )(core, mine, theirs, terms, kept, w_out)


def adam_update(param_now, grad_now, first_old, second_old):
    first_new = BETA_FIRST * first_old + (1.0 - BETA_FIRST) * grad_now
    second_new = BETA_SECOND * second_old + (1.0 - BETA_SECOND) * grad_now * grad_now
    first_hat = first_new / (1.0 - BETA_FIRST**STEP)
    second_hat = second_new / (1.0 - BETA_SECOND**STEP)
    updated = param_now * (1.0 - ADAM_RATE * DECAY_RATE) - ADAM_RATE * first_hat / (
        jnp.sqrt(second_hat) + 1e-08
    )
    return (second_new, updated)


def core_index():
    return lax.axis_index("dp") % 2


def swap_core(part):
    return lax.ppermute(part, "dp", [(i, i ^ 1) for i in range(lax.axis_size("dp"))])


def exchange_mp(parts):
    return lax.all_to_all(parts, "mp", 0, 0)


def send_z(part, step):
    size = lax.axis_size("dp")
    return lax.ppermute(part, "dp", [(i, i ^ (2 * step)) for i in range(size)])


def after(value, *others):
    return lax.optimization_barrier((value, *others))[0]


def copies(part, count):
    return jnp.broadcast_to(part[None], (count,) + part.shape)


def gather_quick(part):
    ways = lax.axis_size("mp")
    if ways != 4:
        return gather_mp(part), 0
    sent = [lax.ppermute(part, "mp", [(i, i ^ j) for i in range(ways)]) for j in range(1, ways)]
    return jnp.stack([part, *sent]), lax.axis_index("mp")


def gather_mp(part):
    return exchange_mp(copies(part, lax.axis_size("mp")))


def core_rows(rows, core):
    half = rows.shape[0] // 2
    return lax.dynamic_slice_in_dim(rows, core * half, half, 0)


def regroup(pieces, parts):
    ways, rows, columns = pieces.shape
    shard = columns // parts
    if shard % 128 == 0:
        return [(pieces, i * shard) for i in range(parts)]
    split = pieces.reshape(ways, rows, parts, shard).transpose(2, 1, 0, 3)
    return [(split[i].reshape(1, rows, ways * shard), 0) for i in range(parts)]


def plane_sum(parts):
    return jnp.sum(parts.astype(F32), axis=0)


def split_again(half, shard, main, first_row):
    row = lax.broadcasted_iota(jnp.int32, main.shape, 0) + first_row
    column = lax.broadcasted_iota(jnp.int32, main.shape, 1)
    here = (row >= half) & (column < 2 * shard)
    value = main + jnp.concatenate([main[:, shard : 2 * shard], main[:, :shard], main[:, 2 * shard :]], axis=1)
    high = lax.reduce_precision(value, 8, 7)
    return jnp.where(here, jnp.where(column < shard, high, value - high), main)


def depth_sum(main, again):
    depth = lax.axis_size("dp") // 2
    place = lax.axis_index("dp") // 2
    rows, columns = main.shape
    each = rows // depth
    main = again(main, 0)
    low = main.astype(LOW)
    parts = [
        send_z(lax.dynamic_slice_in_dim(low, jnp.bitwise_xor(place, step) * each, each, 0), step)
        for step in range(1, depth)
    ]
    mine = lax.dynamic_slice_in_dim(main, place * each, each, 0)
    mine = mine + sum(p.astype(F32) for p in parts)
    mine = again(mine, place * each)
    mine = mine.astype(LOW)
    parts = [mine] + [send_z(mine, step) for step in range(1, depth)]
    pieces = []
    for piece in range(depth):
        here = parts[piece]
        for other in range(1, depth):
            here = jnp.where(place == other, parts[piece ^ other], here)
        pieces.append(here)
    return jnp.concatenate(pieces, axis=0)


def whole_images(rows, patches, count):
    here, width = rows.shape
    spare = count * patches - here
    if spare:
        odd = lax.axis_index("mp") % 2 == 1
        size = lax.axis_size("mp")
        got = lax.ppermute(rows[:spare], "mp", [(i, i - 1) for i in range(1, size, 2)])
        kept = jnp.concatenate([rows[spare:], jnp.zeros((2 * spare, width), rows.dtype)], axis=0)
        rows = jnp.where(odd, kept, jnp.concatenate([rows, got], axis=0))
    return rows


def held_rows(rows, here):
    spare = rows.shape[0] - here
    if spare:
        odd = lax.axis_index("mp") % 2 == 1
        size = lax.axis_size("mp")
        got = lax.ppermute(rows[here:], "mp", [(i, i + 1) for i in range(0, size, 2)])
        kept = jnp.concatenate([got, rows[: here - spare]], axis=0)
        rows = jnp.where(odd, kept, rows[:here])
    return rows


def per_device(
    tokens,
    cotangent,
    w_in,
    w_out,
    spatial,
    model_vectors,
    gate_vectors,
    patch_bias,
    moment_in,
    moment_out,
    moment_mix,
    first_model,
    second_model,
    first_gate,
    second_gate,
    first_patch,
    second_patch,
):
    here, width = tokens.shape
    shard = w_in.shape[2]
    ways = lax.axis_size("mp")
    full = shard * ways
    patches = spatial.shape[0]
    images = -(-here // patches)
    pad = -(-patches // 16) * 16
    core = core_index()
    core_arg = core.astype(jnp.int32).reshape(1)

    half = width // 2

    gate_wire, rest_wire = weight_wires(core_arg, w_in, w_out, gate_vectors)
    gate_mine, base = gather_quick(gate_wire)
    tokens_rows = whole_images(tokens, patches, images)
    cot_rows = whole_images(cotangent, patches, images)
    normed, unit_in, inv_in, cot_pad, normed_t, cot_t = prep(core_arg, tokens_rows, cot_rows, model_vectors, patches, pad)
    mix = jnp.pad(spatial.astype(LOW), ((0, pad - patches), (0, pad - patches)))
    mix_t = mix.T
    bias = jnp.broadcast_to(jnp.pad(patch_bias, (0, pad - patches))[:, None], (pad, 128))
    rest_mine = exchange_mp(rest_wire)
    gate_mine, mix, mix_t, bias = lax.optimization_barrier((gate_mine, mix, mix_t, bias, normed, rest_wire))[:4]
    gate_theirs = swap_core(gate_mine)
    gate_arg = jnp.stack([core, base]).astype(jnp.int32)

    [(gate_mine, _)], [(gate_theirs, _)] = regroup(gate_mine, 1), regroup(gate_theirs, 1)
    normal, unit, slope, scale, w_gate, vec_all = gate_forward(gate_arg, normed, gate_mine, gate_theirs, images, pad)
    rest_mine = after(rest_mine, normal)
    rest_theirs = swap_core(rest_mine)
    rest_mine, rest_theirs = (
        (parts[0][0] if parts[0][0] is parts[1][0] else jnp.concatenate([p[0] for p in parts], axis=2))
        for parts in (regroup(rest_mine, 2), regroup(rest_theirs, 2))
    )
    gated, low_value, low_gate, mine_one, theirs_one, mine_two, theirs_two, grad_mix, vec_sums = channels_both(
        core_arg, normed, cot_pad, normed_t, cot_t, normal, unit, slope, scale, rest_mine, rest_theirs,
        mix, mix_t, bias, vec_all, images, pad, ways if pad % ways == 0 else 1,
    )
    rides = mix_rides(shard, grad_mix)
    extra = EXTRA if shard % 128 == 0 else 2 * EXTRA
    mix_rows = (grad_mix, swap_core(grad_mix)) if rides else ()
    wire = merge(
        core_arg, mine_one, swap_core(theirs_one), mine_two, swap_core(theirs_two), vec_sums, swap_core(vec_sums), ways, extra, mix_rows
    )
    again = functools.partial(split_again, half, shard)
    output, grad_tokens, model_sums = token_back(
        core_arg, tokens_rows, cot_rows, unit_in, inv_in, gated, low_value, after(low_gate, wire),
        rest_mine, rest_theirs, w_gate, model_vectors, patches, pad,
    )

    parts = after(exchange_mp(wire), model_sums)
    model_at, model_width = (grad_mix.shape[2], 128) if rides else (0, shard)
    model_rows = 3 * width // model_width
    tail = model_sums[:3].reshape(model_rows, model_width)
    below = (half + MIX_ROW, extra - MIX_ROW - model_rows)
    plane = plane_sum(parts) + jnp.pad(tail, (below, (model_at, 3 * shard - model_at - model_width)))
    main = depth_sum(plane, again)
    main_other, count, wire = gram_wires(core_arg, main, moment_in, moment_out)
    parts = exchange_mp(wire)
    grad_w_in, new_moment_in, grad_w_out, new_moment_out, terms, kept = moments(
        core_arg, main, main_other, moment_in, moment_out, w_in
    )
    parts = after(parts, kept)
    grams = gather_mp(jnp.sum(parts[:, :count], axis=0))
    extra_rows = extra_rows_of(parts[:, count:], extra, shard)
    extra_rows = jnp.stack([extra_rows, swap_core(extra_rows)])

    vec = main[half : half + MIX_ROW, : 2 * shard].astype(F32)
    grad_vec = vec[:, :shard] + vec[:, shard:]
    tails = extra_rows[:, :, MIX_ROW : MIX_ROW + model_rows, model_at : model_at + model_width]
    tails = jnp.sum(tails, axis=1)
    grad_model = (tails[0] + tails[1]).reshape(3, width)
    if rides:
        each = grad_mix.shape[1] // 2
        rows = extra_rows[:, :, MIX_ROW : MIX_ROW + each, : grad_mix.shape[2]]
        rows = jnp.where(core == 0, rows, rows[::-1])
        grad_mix = jnp.concatenate([rows[0], rows[1]], axis=1)
    else:
        grad_mix = lax.psum(grad_mix, ("dp", "mp"))
    grad_mix = grad_mix.reshape(pad, -1)
    grad_spatial = grad_mix[:patches, :patches]
    grad_patch = grad_mix[:patches, pad]

    new_moment_mix = MOMENTUM * moment_mix + grad_spatial
    ortho_mix = square_orthogonal(new_moment_mix)
    poly = polynomials(core_arg, after(grams, ortho_mix), full)
    new_w_in, new_w_out = update(core_arg, poly, swap_core(poly), terms, kept, w_out)
    shrink_by = 1.0 - MUON_RATE * DECAY_RATE
    new_spatial = spatial * shrink_by - MUON_RATE * 0.2 * math.sqrt(patches) * ortho_mix
    new_second_model, new_model = adam_update(model_vectors, grad_model, first_model, second_model)
    new_second_gate, new_gate = adam_update(gate_vectors, grad_vec, first_gate, second_gate)
    new_second_patch, new_patch = adam_update(patch_bias, grad_patch, first_patch, second_patch)
    return (
        held_rows(output, here),
        held_rows(grad_tokens, here),
        grad_w_in,
        grad_w_out,
        grad_spatial,
        grad_model,
        grad_vec,
        grad_patch,
        new_moment_in,
        new_moment_out,
        new_moment_mix,
        new_second_model,
        new_second_gate,
        new_second_patch,
        new_w_in,
        new_w_out,
        new_spatial,
        new_model,
        new_gate,
        new_patch,
    )


def solution(mesh):
    rows = P(("dp", "mp"), None)
    wide = P(None, None, "mp")
    tall = P("mp", None)
    columns = P(None, "mp")
    return jax.shard_map(
        per_device,
        mesh=mesh,
        in_specs=(
            (rows, rows, wide, tall, P(), P(), columns, P())
            + (wide, tall, P(), P(), P(), columns, columns, P(), P())
        ),
        out_specs=(
            (rows, rows, wide, tall, P(), P(), columns, P())
            + (wide, tall, P(), P(), columns, P())
            + (wide, tall, P(), P(), columns, P())
        ),
        check_vma=False,
    )
```

```python
import functools
import math

import jax
import jax.numpy as jnp
from jax import lax
from jax.experimental import pallas as pl
from jax.experimental.pallas import tpu as pltpu
from jax.sharding import PartitionSpec as P

STEP = 10
EPSILON = 1e-05
COEF_FIRST = 3.4445
COEF_SECOND = -4.775
COEF_THIRD = 2.0315
MOMENTUM = 0.95
MUON_RATE = 0.2
ADAM_RATE = 0.3
DECAY_RATE = 0.01
BETA_FIRST = 0.9
BETA_SECOND = 0.95
LOW = jnp.bfloat16
F32 = jnp.float32


ROW_TILE = 16
UNROLL = 3
EXTRA = 32
MIX_ROW = 4
CHUNK = 512
CUBIC = 0.044715
SLOPE = math.sqrt(2.0 / math.pi)


def compiler(megabytes):
    return pltpu.CompilerParams(vmem_limit_bytes=megabytes << 20)


def dot_nn(a, b):
    return jnp.dot(a, b, preferred_element_type=F32)


def dot_nt(a, b):
    return lax.dot_general(a, b, (((1,), (1,)), ((), ())), preferred_element_type=F32)


def gelu_pair(hidden):
    square = hidden * hidden
    half = 0.5 + 0.5 * jnp.tanh(hidden * (SLOPE + (SLOPE * CUBIC) * square))
    active = hidden * half
    slope = half + (active - active * half) * (2.0 * SLOPE + (6.0 * SLOPE * CUBIC) * square)
    return active, slope


def lanes(v):
    total = v[:, :128]
    for at in range(128, v.shape[1], 128):
        total = total + v[:, at : at + 128]
    return total


def eights(v):
    total = v[:8]
    for at in range(8, v.shape[0], 8):
        total = total + v[at : at + 8]
    return total


def wide(v, width):
    return jnp.concatenate([v] * (width // 128), axis=1) if width % 128 == 0 else v[:, :1]


def tiles(count, body, carry=None):
    for at in range(0, count, ROW_TILE):
        carry = body(slice(at, at + ROW_TILE), carry)
    return carry


def spread_pieces(core, mine, theirs, out, offset):
    half = out.shape[0] // 2
    count = mine.shape[0]
    shard = out.shape[1] // count
    first = pl.ds(pl.multiple_of(core[0] * half, half), half)
    other = pl.ds(pl.multiple_of((1 - core[0]) * half, half), half)
    for piece in range(count):
        cols = slice(piece * shard, (piece + 1) * shard)
        out[first, cols] = mine[piece, :half, offset : offset + shard]
        out[other, cols] = theirs[piece, :half, offset : offset + shard]


def gate_kernel(chunk, core, normed, mine, theirs, normal, unit, slope, scale, weight, vec, active):
    rows, full = active.shape
    half = weight.shape[0] // 2

    @pl.when(pl.program_id(0) == 0)
    def _():
        count, _, shard = mine.shape
        first = pl.ds(pl.multiple_of(core[0] * half, half), half)
        other = pl.ds(pl.multiple_of((1 - core[0]) * half, half), half)
        for piece in range(count):
            owner = jnp.bitwise_xor(core[1], piece) if count > 1 else 0
            cols = pl.ds(pl.multiple_of(owner * shard, shard), shard) if count > 1 else slice(0, shard)
            weight[first, cols] = mine[piece, :half, :]
            weight[other, cols] = theirs[piece, :half, :]
            terms = mine[piece, half:, :].astype(F32)
            vec[:, cols] = (terms[0:8] + terms[8:16]) + terms[16:24]

    starts = range(0, full, chunk)
    for at in starts:
        active[:, at : at + chunk] = dot_nn(normed[...], weight[:, at : at + chunk])

    def act(here, _):
        total = jnp.zeros((ROW_TILE, 128), F32)
        for at in starts:
            cols = slice(at, at + chunk)
            value, grad = gelu_pair(active[here, cols] + vec[1:2, cols])
            active[here, cols] = value
            slope[here, cols] = grad.astype(LOW)
            total = total + lanes(value)
        scale[here, :] = total

    tiles(rows, act)
    mean = jnp.sum(scale[...], axis=1, keepdims=True) * (1.0 / full)
    scale[...] = jnp.broadcast_to(mean, scale.shape)

    def spread(here, _):
        total = jnp.zeros((ROW_TILE, 128), F32)
        mean_here = wide(scale[here, :], chunk)
        for at in starts:
            cols = slice(at, at + chunk)
            centred = active[here, cols] - mean_here
            active[here, cols] = centred
            total = total + lanes(centred * centred)
        scale[here, :] = total

    tiles(rows, spread)
    var = jnp.sum(scale[...], axis=1, keepdims=True) * (1.0 / full)
    scale[...] = jnp.broadcast_to(lax.rsqrt(var + EPSILON), scale.shape)

    def finish(here, _):
        inv = wide(scale[here, :], chunk)
        for at in starts:
            cols = slice(at, at + chunk)
            unit_here = active[here, cols] * inv
            unit[here, cols] = unit_here.astype(LOW)
            normal[here, cols] = (unit_here * vec[2:3, cols] + vec[3:4, cols]).astype(LOW)

    tiles(rows, finish)


def gate_forward(core, normed, mine, theirs, images, pad):
    count, _, shard = mine.shape
    full = count * shard
    width = normed.shape[1]
    chunk = 512 if full % 512 == 0 else full
    total = images * pad
    whole = lambda a: pl.BlockSpec(a.shape, lambda i, c: (0,) * a.ndim, pipeline_mode=pl.Buffered(1))
    rows = lambda n: pl.BlockSpec((pad, n), lambda i, c: (i, 0))
    fixed = lambda *f: pl.BlockSpec(f, lambda i, c: (0, 0))
    shape = jax.ShapeDtypeStruct
    return pl.pallas_call(
        functools.partial(gate_kernel, chunk),
        grid_spec=pltpu.PrefetchScalarGridSpec(
            num_scalar_prefetch=1,
            grid=(images,),
            in_specs=[rows(width), whole(mine), whole(theirs)],
            out_specs=[rows(full), rows(full), rows(full), rows(128), fixed(width, full), fixed(8, full)],
            scratch_shapes=[pltpu.VMEM((pad, full), F32)],
        ),
        out_shape=[shape((total, full), LOW)] * 3
        + [shape((total, 128), F32), shape((width, full), LOW), shape((8, full), F32)],
        compiler_params=compiler(60),
        cost_estimate=pl.CostEstimate(
            flops=2 * total * width * full, bytes_accessed=8 * total * full, transcendentals=total * full
        ),
        name="gate_forward",
    )(core, normed, mine, theirs)


def value_kernel(
    pad,
    images,
    core,
    normed,
    cot,
    normed_t_far,
    cot_t_far,
    normal,
    unit,
    slope_far,
    scale_far,
    w_mine,
    w_theirs,
    mix,
    mix_t,
    bias,
    vec,
    gated,
    low_value,
    low_gate,
    mine,
    theirs,
    mine_gate,
    theirs_gate,
    mix_pieces,
    vec_sums,
    w_value,
    w_back,
    sums,
    grad_mix,
    grad_bias,
    grad_unit,
    hidden,
    back,
    mixed,
    turned,
    low_mixed,
    low_pad,
    gated_pad,
    normed_t,
    cot_t,
    slope_gate,
    scale,
    arrived,
):
    total, chunk = gated.shape
    half = w_value.shape[0] // 2
    step = pl.program_id(0)
    count = pl.num_programs(0) // 2
    cols = pl.ds(pl.multiple_of(lax.rem(step, count) * chunk, chunk), chunk)

    late = (
        pltpu.make_async_copy(normed_t_far, normed_t, arrived.at[0]),
        pltpu.make_async_copy(cot_t_far, cot_t, arrived.at[1]),
        pltpu.make_async_copy(slope_far, slope_gate, arrived.at[2]),
        pltpu.make_async_copy(scale_far, scale, arrived.at[3]),
    )

    @pl.when(step == 0)
    def _():
        for copy in late:
            copy.start()
        offset = w_mine.shape[2] - w_value.shape[1] // w_mine.shape[0]
        spread_pieces(core, w_mine, w_theirs, w_value, 0)
        spread_pieces(core, w_mine, w_theirs, w_back, offset)
        sums[...] = jnp.zeros_like(sums)
        vec_sums[...] = jnp.zeros_like(vec_sums)
        grad_mix[...] = jnp.zeros_like(grad_mix)
        grad_bias[...] = jnp.zeros_like(grad_bias)
        low_pad[total:, :] = jnp.zeros_like(low_pad[total:, :])
        gated_pad[total:, :] = jnp.zeros_like(gated_pad[total:, :])

    pairs = ((hidden.at[0], back.at[0], mixed.at[0]), (hidden.at[1], back.at[1], mixed.at[1]))

    def products(image):
        here = slice(image * pad, (image + 1) * pad)
        hid, bck, mxd = pairs[image % 2]
        hid[...] = dot_nn(normed[here, :], w_value[:, cols])
        bck[...] = dot_nn(cot[here, :], w_back[:, cols])
        mxd[...] = dot_nn(mix[...], normal[here, :])

    def forward(image, sums):
        hid, bck, mxd = pairs[image % 2]
        for row in range(0, pad, ROW_TILE):
            at = slice(row, row + ROW_TILE)
            here = slice(image * pad + row, image * pad + row + ROW_TILE)
            value, slope = gelu_pair(hid[at, :] + vec[0:1, :])
            mixed_here = mxd[at, :] + wide(bias[at, :], chunk)
            back_here = bck[at, :]
            gated_here = (value * mixed_here).astype(LOW)
            gated[here, :] = gated_here
            gated_pad[here, :] = gated_here
            grad_here = (back_here * value).astype(LOW)
            low_mixed[image % 2, at, :] = grad_here
            grad_bias[at, :] += lanes(grad_here.astype(F32))
            low_here = (back_here * mixed_here * slope).astype(LOW)
            low_value[here, :] = low_here
            low_pad[here, :] = low_here
            sums = sums + eights(low_here.astype(F32))
        return sums

    def turn(image):
        here = slice(image * pad, (image + 1) * pad)
        turned[image % 2] = dot_nn(mix_t[...], low_mixed[image % 2])
        grad_mix[:, :pad] += dot_nt(low_mixed[image % 2], normal[here, :])

    def backward(image, kept):
        for row in range(0, pad, ROW_TILE):
            at = slice(row, row + ROW_TILE)
            here = slice(image * pad + row, image * pad + row + ROW_TILE)
            grad = turned[image % 2, at, :]
            unit_here = unit[here, :].astype(F32)
            gain = vec[2:3, :]
            both = grad * unit_here
            du = grad * gain
            grad_unit[here, cols] = du.astype(LOW)
            sums[0, here, :] += lanes(du)
            sums[1, here, :] += lanes(both * gain)
            kept = kept[0] + eights(both), kept[1] + eights(grad)
        return kept

    @pl.when(step < count)
    def _():
        zero = jnp.zeros((8, chunk), F32)
        bias_sum, norm_sums = zero, (zero, zero)
        products(0)
        for image in range(images):
            if image + 1 < images:
                products(image + 1)
            bias_sum = forward(image, bias_sum)
            turn(image)
            if image:
                norm_sums = backward(image - 1, norm_sums)
        norm_sums = backward(images - 1, norm_sums)
        gain_sum, shift_sum = norm_sums


        @pl.when(step == 0)
        def _():
            late[0].wait()
            late[1].wait()

        for i, product in enumerate((dot_nn(normed_t[...], low_pad[...]), dot_nn(cot_t[...], gated_pad[...]))):
            mine[i, :half, :] = product[:half].astype(LOW)
            theirs[i, :half, :] = product[half:].astype(LOW)

        total_of = lambda v: jnp.sum(v, axis=0, keepdims=True)
        vec_sums[0:1, cols] = total_of(bias_sum)
        vec_sums[2:3, cols] = total_of(gain_sum)
        vec_sums[3:4, cols] = total_of(shift_sum)

    @pl.when(step == count - 1)
    def _():
        patch = jnp.sum(grad_bias[...], axis=1, keepdims=True)
        grad_mix[:, pad:] = jnp.broadcast_to(patch, (pad, grad_mix.shape[1] - pad))
        each = mix_pieces.shape[1]
        for piece in range(mix_pieces.shape[0]):
            mix_pieces[piece] = grad_mix[piece * each : (piece + 1) * each, :]


    def gate_tile(i, total_here):
        here = slice(i * ROW_TILE, (i + 1) * ROW_TILE)
        one = wide(sums[0, here, :], chunk)
        two = wide(sums[1, here, :], chunk)
        inv = wide(scale[here, :], chunk)
        grad = inv * (grad_unit[here, cols].astype(F32) - one - unit[here, :].astype(F32) * two)
        low = (grad * slope_gate[here, cols].astype(F32)).astype(LOW)
        low_gate[here, :] = low
        low_pad[here, :] = low
        return total_here + eights(low.astype(F32))

    @pl.when(step == count)
    def _():
        late[2].wait()
        late[3].wait()
        for i in range(2):
            mean = jnp.sum(sums[i], axis=1, keepdims=True) * (1.0 / w_value.shape[1])
            sums[i] = jnp.broadcast_to(mean, (total, 128))

    @pl.when(step >= count)
    def _():
        kept = jnp.zeros((8, chunk), F32)
        for at in range(total // ROW_TILE):
            kept = gate_tile(at, kept)
        vec_sums[1:2, cols] = jnp.sum(kept, axis=0, keepdims=True)
        product = dot_nn(normed_t[...], low_pad[...])
        mine_gate[:half, :] = product[:half].astype(LOW)
        theirs_gate[:half, :] = product[half:].astype(LOW)


def channels_both(
    core, normed, cot, normed_t, cot_t, normal, unit, slope, scale, w_mine, w_theirs, mix, mix_t, bias, vec, images, pad, ways
):
    width = normed.shape[1]
    full = normal.shape[1]
    total = images * pad
    deep = normed_t.shape[1]
    chunk = CHUNK if full % CHUNK == 0 else full
    count = full // chunk
    half = width // 2
    wide_mix = -(-(pad + 1) // 128) * 128
    mix_shape = (ways, pad // ways, wide_mix)
    whole = lambda a: pl.BlockSpec(a.shape, lambda i, c: (0,) * a.ndim, pipeline_mode=pl.Buffered(1))
    early = lambda n: pl.BlockSpec((n, chunk), lambda i, c: (0, jnp.minimum(i, count - 1)))
    late = lambda n: pl.BlockSpec((n, chunk), lambda i, c: (0, jnp.maximum(i - count, 0)))
    twice = lambda n: pl.BlockSpec((n, chunk), lambda i, c: (0, lax.rem(i, count)))
    pair = pl.BlockSpec((2, half, chunk), lambda i, c: (0, 0, jnp.minimum(i, count - 1)))
    shape = jax.ShapeDtypeStruct
    far = pl.BlockSpec(memory_space=pl.ANY)
    return pl.pallas_call(
        functools.partial(value_kernel, pad, images),
        grid_spec=pltpu.PrefetchScalarGridSpec(
            num_scalar_prefetch=1,
            grid=(2 * count,),
            in_specs=[whole(normed), whole(cot), far, far]
            + [early(total), twice(total), far, far, whole(w_mine), whole(w_theirs)]
            + [whole(mix), whole(mix_t), whole(bias), early(8)],
            out_specs=[early(total), early(total), late(total), pair, pair, late(half), late(half)]
            + [pl.BlockSpec(mix_shape, lambda i, c: (0, 0, 0)), pl.BlockSpec((8, full), lambda i, c: (0, 0))],
            scratch_shapes=[pltpu.VMEM((width, full), LOW)] * 2
            + [pltpu.VMEM((2, total, 128), F32), pltpu.VMEM((pad, wide_mix), F32), pltpu.VMEM((pad, 128), F32)]
            + [pltpu.VMEM((total, full), LOW)]
            + [pltpu.VMEM((2, pad, chunk), F32)] * 4
            + [pltpu.VMEM((2, pad, chunk), LOW)]
            + [pltpu.VMEM((deep, chunk), LOW)] * 2
            + [pltpu.VMEM((width, deep), LOW)] * 2
            + [pltpu.VMEM((total, full), LOW), pltpu.VMEM((total, 128), F32), pltpu.SemaphoreType.DMA((4,))],
        ),
        out_shape=[shape((total, full), LOW)] * 3
        + [shape((2, half, full), LOW)] * 2
        + [shape((half, full), LOW)] * 2 + [shape(mix_shape, F32), shape((8, full), F32)],
        compiler_params=compiler(60),
        cost_estimate=pl.CostEstimate(
            flops=14 * total * width * full, bytes_accessed=24 * total * full, transcendentals=total * full
        ),
        name="channels_both",
    )(core, normed, cot, normed_t, cot_t, normal, unit, slope, scale, w_mine, w_theirs, mix, mix_t, bias, vec)


def gate_wire_kernel(core, w_in, vectors, wire):
    half, _, shard = w_in.shape
    low = w_in[:, 1, :].astype(LOW)
    value = jnp.concatenate([vectors[...], jnp.zeros((4, shard), F32)], axis=0)
    high = value.astype(LOW).astype(F32)
    middle = (value - high).astype(LOW).astype(F32)
    last = value - high - middle
    terms = jnp.concatenate([high, middle, last, jnp.zeros((8, shard), F32)], axis=0).astype(LOW)
    wire[:half, :] = low
    wire[half:, :] = terms


def rest_wire_kernel(core, w_in, w_out, wire):
    shard = w_in.shape[2]
    value = w_in[:, 0, :].astype(LOW)
    back = w_out[...].T.astype(LOW)
    for receiver in range(wire.shape[0]):
        wire[receiver, :, :shard] = value
        wire[receiver, :, shard:] = back


def weight_wires(core, w_in, w_out, vectors):
    width, _, shard = w_in.shape
    half = width // 2
    ways = lax.axis_size("mp")
    rows = pl.BlockSpec((half, 2, shard), lambda i, c: (c[0], 0, 0))
    fixed = lambda *f: pl.BlockSpec(f, lambda i, c: (0,) * len(f))
    spec = lambda ins, out: pltpu.PrefetchScalarGridSpec(
        num_scalar_prefetch=1, grid=(1,), in_specs=ins, out_specs=fixed(*out)
    )
    out = (half + 32, shard)
    gate = pl.pallas_call(
        gate_wire_kernel,
        grid_spec=spec([rows, fixed(4, shard)], out),
        out_shape=jax.ShapeDtypeStruct(out, LOW),
        compiler_params=compiler(60),
        name="gate_wire",
    )(core, w_in, vectors)
    out = (ways, half, 2 * shard)
    if shard % 128:
        back = lax.dynamic_slice_in_dim(w_out, core[0] * half, half, 1)
        rest = jnp.concatenate([core_rows(w_in[:, 0], core[0]), back.T], axis=1).astype(LOW)
        return gate, copies(rest, ways)
    rest = pl.pallas_call(
        rest_wire_kernel,
        grid_spec=spec([rows, pl.BlockSpec((shard, half), lambda i, c: (0, c[0]))], out),
        out_shape=jax.ShapeDtypeStruct(out, LOW),
        compiler_params=compiler(60),
        name="rest_wire",
    )(core, w_in, w_out)
    return gate, rest


def merge_kernel(core, mine, theirs, mine_gate, theirs_gate, vec, vec_other, *refs):
    wire = refs[-1]
    _, half, shard = mine.shape
    parts = ((mine.at[0], theirs.at[0]), (mine_gate, theirs_gate), (mine.at[1], theirs.at[1]))
    for i, (own, other) in enumerate(parts):
        wire[0, :half, i * shard : (i + 1) * shard] = (own[...].astype(F32) + other[...].astype(F32)).astype(LOW)
    extra = wire.shape[1] - half
    rows = [(vec[...] + vec_other[...])[:MIX_ROW]]
    if len(refs) > 1:
        mix = refs[0][0] + refs[1][0]
        each = mix.shape[0] // 2
        mix = jnp.where(core[0] == 0, mix[:each], mix[each:])
        rows.append(jnp.concatenate([mix, jnp.zeros((mix.shape[0], shard - mix.shape[1]), F32)], axis=1))
    rows.append(jnp.zeros((extra - sum(r.shape[0] for r in rows), shard), F32))
    rows = jnp.concatenate(rows, axis=0)
    high = rows.astype(LOW).astype(F32)
    for i, part in enumerate((high, rows - high, jnp.zeros_like(rows))):
        wire[0, half:, i * shard : (i + 1) * shard] = part.astype(LOW)


def merge(core, mine, theirs, mine_gate, theirs_gate, vec, vec_other, ways, extra, mix):
    _, rows, full = mine.shape
    shard = full // ways
    if shard % 128:
        both = mine.astype(F32) + theirs.astype(F32)
        both = jnp.stack([both[0], mine_gate.astype(F32) + theirs_gate.astype(F32), both[1]])
        more = jnp.pad((vec + vec_other)[:MIX_ROW], ((0, extra - MIX_ROW), (0, 0)))
        high = lax.reduce_precision(more, 8, 7)
        both = jnp.concatenate([both, jnp.stack([high, more - high, jnp.zeros_like(more)])], axis=1)
        blocks = both.reshape(3, rows + extra, ways, shard).transpose(2, 1, 0, 3)
        return blocks.reshape(ways, rows + extra, 3 * shard).astype(LOW)
    pair = pl.BlockSpec((2, rows, shard), lambda i, c: (0, 0, i))
    block = lambda n: pl.BlockSpec((n, shard), lambda i, c: (0, i))
    return pl.pallas_call(
        merge_kernel,
        grid_spec=pltpu.PrefetchScalarGridSpec(
            num_scalar_prefetch=1,
            grid=(ways,),
            in_specs=[pair, pair, block(rows), block(rows), block(8), block(8)]
            + [pl.BlockSpec((1,) + m.shape[1:], lambda i, c: (i, 0, 0)) for m in mix],
            out_specs=pl.BlockSpec((1, rows + extra, 3 * shard), lambda i, c: (i, 0, 0)),
        ),
        out_shape=jax.ShapeDtypeStruct((ways, rows + extra, 3 * shard), LOW),
        compiler_params=compiler(60),
        name="merge",
    )(core, mine, theirs, mine_gate, theirs_gate, vec, vec_other, *mix)


def mix_rides(shard, mix):
    return shard % 128 == 0 and mix.shape[2] + 128 <= shard and mix.shape[0] > 1 and mix.shape[1] % 2 == 0 and (
        mix.shape[1] // 2 + MIX_ROW <= EXTRA
    )


def decayed_kernel(core, old_in, old_out, kept):
    width, _, shard = old_in.shape

    @pl.when(core[0] == 0)
    def _():
        kept[:, :shard] = MOMENTUM * old_out[...].T
        kept[:, shard:] = jnp.zeros((width, shard), F32)

    @pl.when(core[0] == 1)
    def _():
        for i in range(2):
            kept[:, i * shard : (i + 1) * shard] = MOMENTUM * old_in[:, i, :]


def decayed(core, old_in, old_out):
    width, _, shard = old_in.shape
    fixed = lambda *f: pl.BlockSpec(f, lambda i, c: (0,) * len(f))
    return pl.pallas_call(
        decayed_kernel,
        grid_spec=pltpu.PrefetchScalarGridSpec(
            num_scalar_prefetch=1,
            grid=(1,),
            in_specs=[fixed(*old_in.shape), fixed(*old_out.shape)],
            out_specs=fixed(width, 2 * shard),
        ),
        out_shape=jax.ShapeDtypeStruct((width, 2 * shard), F32),
        compiler_params=compiler(60),
        name="decayed",
    )(core, old_in, old_out)


def gram_kernel(count, core, main, other, kept, wire, moment):
    width, shard = kept.shape[0], kept.shape[1] // 2
    half = width // 2
    halves = (
        (pl.ds(pl.multiple_of(core[0] * half, half), half), main),
        (pl.ds(pl.multiple_of((1 - core[0]) * half, half), half), other),
    )

    @pl.when(core[0] == 0)
    def _():
        for rows, part in halves:
            moment[rows, :shard] = kept[rows, :shard] + part[:half, 2 * shard :].astype(F32)
        moment[:, shard:] = jnp.zeros((width, shard), F32)

    @pl.when(core[0] == 1)
    def _():
        for rows, part in halves:
            moment[rows, :] = kept[rows, :] + part[:half, : 2 * shard].astype(F32)

    high, low = split_two(moment[...])
    rows = (slice(0, half), slice(half, width))
    blocks = []
    for i, j in ((0, 0), (0, 1), (1, 1)):
        i, j = rows[i], rows[j]
        cross = dot_nt(high[i], low[j]) + dot_nt(low[i], high[j])
        blocks.append(dot_nt(high[i], high[j]) + cross)
    blocks = jnp.concatenate(blocks, axis=0)
    terms = main[half:, :].astype(F32)
    terms = terms[:, :shard] + terms[:, shard : 2 * shard]
    extra = terms.shape[0]
    for receiver in range(wire.shape[0]):
        wire[receiver, :count, :] = blocks[receiver * count : (receiver + 1) * count]
        for i, at in enumerate(range(0, shard, 128)):
            part = terms[:, at : at + 128]
            top, left = count + i // 2 * extra, i % 2 * 128
            wire[receiver, top : top + extra, left : left + part.shape[1]] = part


def gram_wires(core, main, kept):
    width, shard = kept.shape[0], kept.shape[1] // 2
    half = width // 2
    ways = lax.axis_size("mp")
    count = 3 * half // ways
    extra = main.shape[0] - half
    rows = count + extra * -(-shard // 256)
    fixed = lambda *f: pl.BlockSpec(f, lambda i, c: (0,) * len(f))
    ins = (main, swap_core(main), kept)
    out = (ways, rows, half)
    return ins[1], count, pl.pallas_call(
        functools.partial(gram_kernel, count),
        grid_spec=pltpu.PrefetchScalarGridSpec(
            num_scalar_prefetch=1,
            grid=(1,),
            in_specs=[fixed(*a.shape) for a in ins],
            out_specs=fixed(*out),
            scratch_shapes=[pltpu.VMEM((width, 2 * shard), F32)],
        ),
        out_shape=jax.ShapeDtypeStruct(out, F32),
        compiler_params=compiler(60),
        name="gram_wires",
    )(core, *ins)


def extra_rows_of(parts, extra, shard):
    pieces = []
    for i, at in enumerate(range(0, shard, 128)):
        top, left = i // 2 * extra, i % 2 * 128
        pieces.append(parts[..., top : top + extra, left : left + min(128, shard - at)])
    return jnp.concatenate(pieces, axis=-1)


def moments_kernel(core, main, other, old_in, old_out, w_in, grad_in, new_in, grad_out, new_out, terms, kept, flat):
    width, _, shard = old_in.shape
    half = width // 2
    rows = (
        pl.ds(pl.multiple_of(core[0] * half, half), half),
        pl.ds(pl.multiple_of((1 - core[0]) * half, half), half),
    )
    for here, part in ((rows[0], main), (rows[1], other)):
        for i in range(3):
            flat[i, here, :] = part[:half, i * shard : (i + 1) * shard].astype(F32)
    for i in range(2):
        grad = flat[i]
        grad_in[:, i, :] = grad
        moment = MOMENTUM * old_in[:, i, :] + grad
        new_in[:, i, :] = moment
        terms[0, i], terms[1, i] = split_two(moment)
        kept[i] = w_in[:, i, :] * (1.0 - MUON_RATE * DECAY_RATE)
    grad = flat[2].T
    grad_out[...] = grad
    moment = MOMENTUM * old_out[...] + grad
    new_out[...] = moment
    terms[0, 2], terms[1, 2] = split_two(moment.T)


def moments(core, main, other, old_in, old_out, w_in):
    width, _, shard = old_in.shape
    ins = (main, other, old_in, old_out, w_in)
    shapes = (
        [(width, 2, shard)] * 2 + [(shard, width)] * 2 + [(2, 3, width, shard), (2, width, shard)]
    )
    fixed = lambda f: pl.BlockSpec(f, lambda i, c, n=len(f): (0,) * n)
    return pl.pallas_call(
        moments_kernel,
        grid_spec=pltpu.PrefetchScalarGridSpec(
            num_scalar_prefetch=1,
            grid=(1,),
            in_specs=[fixed(a.shape) for a in ins],
            out_specs=[fixed(f) for f in shapes],
            scratch_shapes=[pltpu.VMEM((3, width, shard), F32)],
        ),
        out_shape=[jax.ShapeDtypeStruct(f, LOW if len(f) == 4 else F32) for f in shapes],
        compiler_params=compiler(60),
        name="moments",
    )(core, *ins)


def prep_kernel(patches, pad, core, tokens, cot, model, normed, unit, scale, cot_pad, normed_t, cot_t, keep):
    step = pl.program_id(0)
    group = tokens.shape[1] // patches
    rows = group * pad
    width = tokens.shape[2]

    def padded(block):
        block = block[0].astype(F32)
        gap = jnp.zeros((pad - patches, width), F32)
        parts = []
        for image in range(group):
            parts += [block[image * patches : (image + 1) * patches], gap]
        return jnp.concatenate(parts, axis=0)

    here = pl.ds(pl.multiple_of(step * rows, rows), rows)

    @pl.when(step == 0)
    def _():
        keep[...] = jnp.zeros_like(keep)

    cot_here = padded(cot)
    cot_pad[...] = cot_here.astype(LOW)
    keep[1, here, :] = cot_here
    x = padded(tokens)
    centred = x - jnp.sum(x, axis=1, keepdims=True) * (1.0 / width)
    inv = lax.rsqrt(jnp.sum(centred * centred, axis=1, keepdims=True) * (1.0 / width) + EPSILON)
    unit_here = centred * inv
    scale[...] = jnp.broadcast_to(inv, scale.shape)
    unit[...] = unit_here.astype(LOW)
    low = (unit_here * model[0:1, :] + model[1:2, :]).astype(LOW)
    normed[...] = low
    keep[0, here, :] = low.astype(F32)

    @pl.when(step == pl.num_programs(0) - 1)
    def _():
        half = width // 2
        for i, place in enumerate((core[0], 1 - core[0])):
            features = pl.ds(pl.multiple_of(place * half, half), half)
            rows_out = slice(i * half, (i + 1) * half)
            for at in range(0, normed_t.shape[1], 128):
                cols = slice(at, at + 128)
                normed_t[rows_out, cols] = keep[0, cols, features].T.astype(LOW)
                cot_t[rows_out, cols] = keep[1, cols, features].T.astype(LOW)


def prep(core, tokens, cot, model, patches, pad):
    here, width = tokens.shape
    images = here // patches
    group = 2 if images % 2 == 0 else images
    steps = images // group
    total = images * pad
    deep = -(-total // 128) * 128
    block = pl.BlockSpec((1, group * patches, width), lambda i, c: (i, 0, 0))
    rows = lambda n: pl.BlockSpec((group * pad, n), lambda i, c: (i, 0))
    fixed = lambda *f: pl.BlockSpec(f, lambda i, c: (0, 0))
    shape = jax.ShapeDtypeStruct
    return pl.pallas_call(
        functools.partial(prep_kernel, patches, pad),
        grid_spec=pltpu.PrefetchScalarGridSpec(
            num_scalar_prefetch=1,
            grid=(steps,),
            in_specs=[block, block, fixed(3, width)],
            out_specs=[rows(width), rows(width), rows(128), rows(width), fixed(width, deep), fixed(width, deep)],
            scratch_shapes=[pltpu.VMEM((2, deep, width), F32)],
        ),
        out_shape=[
            shape((total, width), LOW),
            shape((total, width), LOW),
            shape((total, 128), F32),
            shape((total, width), LOW),
            shape((width, deep), LOW),
            shape((width, deep), LOW),
        ],
        compiler_params=compiler(60),
        cost_estimate=pl.CostEstimate(flops=20 * total * width, bytes_accessed=20 * total * width, transcendentals=total),
        name="prep",
    )(core, tokens.reshape(steps, group * patches, width), cot.reshape(steps, group * patches, width), model)


def token_kernel(
    patches,
    pad,
    core,
    tokens,
    cot,
    unit,
    scale,
    gated,
    low_value,
    low_gate,
    w_mine,
    w_theirs,
    w_gate,
    model,
    output,
    grad_tokens,
    sums,
    w_value,
    w_back,
    branch,
    grad,
):
    group = tokens.shape[1] // patches
    width = tokens.shape[2]
    rows = group * pad

    @pl.when(pl.program_id(0) == 0)
    def _():
        sums[...] = jnp.zeros_like(sums)
        offset = w_mine.shape[2] - w_value.shape[1] // w_mine.shape[0]
        spread_pieces(core, w_mine, w_theirs, w_value, 0)
        spread_pieces(core, w_mine, w_theirs, w_back, offset)

    def packed(v):
        return jnp.concatenate([v[i * pad : i * pad + patches] for i in range(group)], axis=0)

    branch[...] = dot_nt(gated[...], w_back[...])
    output[0] = (tokens[0].astype(F32) + packed(branch) + model[2:3, :]).astype(LOW)
    grad[...] = dot_nt(low_value[...], w_value[...]) + dot_nt(low_gate[...], w_gate[...])

    def back(i, kept):
        here = pl.ds(pl.multiple_of(i * ROW_TILE, ROW_TILE), ROW_TILE)
        grad_here = grad[here, :]
        unit_here = unit[here, :].astype(F32)
        both = grad_here * unit_here
        du = grad_here * model[0:1, :]
        first = jnp.sum(du, axis=1, keepdims=True) * (1.0 / width)
        second = jnp.sum(both * model[0:1, :], axis=1, keepdims=True) * (1.0 / width)
        branch[here, :] = wide(scale[here, :], width) * (du - first - unit_here * second)
        return kept[0] + eights(both), kept[1] + eights(grad_here)

    zero = jnp.zeros((8, width), F32)
    gain, shift = lax.fori_loop(0, rows // ROW_TILE, back, (zero, zero), unroll=2)
    cot_here = cot[0].astype(F32)
    grad_tokens[0] = (cot_here + packed(branch)).astype(LOW)
    sums[0:1, :] += jnp.sum(gain, axis=0, keepdims=True)
    sums[1:2, :] += jnp.sum(shift, axis=0, keepdims=True)
    sums[2:3, :] += jnp.sum(eights(cot_here), axis=0, keepdims=True)


def token_back(core, tokens, cot, unit, scale, gated, low_value, low_gate, w_mine, w_theirs, w_gate, model, patches, pad):
    here, width = tokens.shape
    full = w_gate.shape[1]
    images = here // patches
    group = 2 if images % 2 == 0 else images
    steps = images // group
    total = images * pad
    block = pl.BlockSpec((1, group * patches, width), lambda i, c: (i, 0, 0))
    rows = lambda n: pl.BlockSpec((group * pad, n), lambda i, c: (i, 0))
    whole = lambda a: pl.BlockSpec(a.shape, lambda i, c: (0,) * a.ndim, pipeline_mode=pl.Buffered(1))
    shape = jax.ShapeDtypeStruct
    output, grad_tokens, sums = pl.pallas_call(
        functools.partial(token_kernel, patches, pad),
        grid_spec=pltpu.PrefetchScalarGridSpec(
            num_scalar_prefetch=1,
            grid=(steps,),
            in_specs=[block, block, rows(width), rows(128), rows(full), rows(full), rows(full)]
            + [whole(w_mine), whole(w_theirs), whole(w_gate), whole(model)],
            out_specs=[block, block, pl.BlockSpec((8, width), lambda i, c: (0, 0))],
            scratch_shapes=[pltpu.VMEM((width, full), LOW)] * 2 + [pltpu.VMEM((group * pad, width), F32)] * 2,
        ),
        out_shape=[shape((steps, group * patches, width), LOW)] * 2 + [shape((8, width), F32)],
        compiler_params=compiler(60),
        cost_estimate=pl.CostEstimate(
            flops=6 * total * width * full, bytes_accessed=8 * total * full, transcendentals=0
        ),
        name="token_back",
    )(
        core,
        tokens.reshape(steps, group * patches, width),
        cot.reshape(steps, group * patches, width),
        unit, scale, gated, low_value, low_gate, w_mine, w_theirs, w_gate, model,
    )
    return output.reshape(here, width), grad_tokens.reshape(here, width), sums


def split_two(v):
    high = v.astype(LOW)
    return high, (v - high.astype(F32)).astype(LOW)


def dot3(a, b):
    return dot_nn(a[0], b[0]) + (dot_nn(a[0], b[1]) + dot_nn(a[1], b[0]))


def symmetric3(a, b):
    half = a[0].shape[0] // 2
    top = dot3([v[:half] for v in a], b)
    corner = dot3([v[half:] for v in a], [v[:, half:] for v in b])
    bottom = jnp.concatenate([top[:, half:].T, corner], axis=1)
    return jnp.concatenate([top, bottom], axis=0)


def square_kernel(moment, ortho, now):
    few = moment.shape[0]
    now[...] = jnp.zeros_like(now)
    start = moment[...]
    now[:few, :few] = start / (jnp.sqrt(jnp.sum(start * start, keepdims=True)) + 1e-07)
    for sweep in range(5):
        x = now[...]
        x_two = split_two(x)
        gram = dot_nt(x_two[0], x_two[0]) + (dot_nt(x_two[0], x_two[1]) + dot_nt(x_two[1], x_two[0]))
        gram_two = split_two(gram)
        extra = COEF_SECOND * gram + COEF_THIRD * dot3(gram_two, gram_two)
        now[...] = COEF_FIRST * x + dot3(split_two(extra), x_two)
    ortho[...] = now[:few, :few]


def square_orthogonal(moment):
    edge = -(-moment.shape[0] // 128) * 128
    return pl.pallas_call(
        square_kernel,
        out_shape=jax.ShapeDtypeStruct(moment.shape, F32),
        scratch_shapes=[pltpu.VMEM((edge, edge), F32)],
        compiler_params=compiler(60),
        name="square_orthogonal",
    )(moment)


def polynomial_kernel(rates, core, pieces, poly, blocks, gram_now, total):
    size = gram_now.shape[0]
    half = size // 2
    count = pieces.shape[1]
    for piece in range(pieces.shape[0]):
        blocks[piece * count : (piece + 1) * count, :] = pieces[piece]
    gram_now[:half, :half] = blocks[:half]
    gram_now[:half, half:] = blocks[half:size]
    gram_now[half:, :half] = blocks[half:size].T
    gram_now[half:, half:] = blocks[size:]
    gram = gram_now[...]
    row = lax.broadcasted_iota(jnp.int32, (size, size), 0)
    col = lax.broadcasted_iota(jnp.int32, (size, size), 1)
    same = row == col
    norm = jnp.sqrt(jnp.sum(jnp.where(same, gram, 0.0), keepdims=True)) + 1e-07
    inv = 1.0 / norm
    gram_now[...] = gram * (inv * inv)
    for sweep in range(5):
        matrix = gram_now[...]
        matrix_two = split_two(matrix)
        extra = COEF_SECOND * matrix + COEF_THIRD * symmetric3(matrix_two, matrix_two)
        extra_two = split_two(extra)
        if sweep == 0:
            total[...] = jnp.where(same, COEF_FIRST + extra, extra)
        else:
            total[...] = COEF_FIRST * total[...] + symmetric3(extra_two, split_two(total[...]))
        if sweep < 4:
            partial = COEF_FIRST * matrix + symmetric3(extra_two, matrix_two)
            gram_now[...] = COEF_FIRST * partial + symmetric3(extra_two, split_two(partial))
    rate = jnp.where(core[0] == 0, rates[0], rates[1])
    poly[...] = total[...] * (inv * rate)


def polynomials(core, pieces, full):
    half = pieces.shape[2]
    size = 2 * half
    rates = [MUON_RATE * 0.2 * math.sqrt(max(size, n)) for n in (full, 2 * full)]
    fixed = lambda *f: pl.BlockSpec(f, lambda i, c: (0,) * len(f))
    return pl.pallas_call(
        functools.partial(polynomial_kernel, rates),
        grid_spec=pltpu.PrefetchScalarGridSpec(
            num_scalar_prefetch=1,
            grid=(1,),
            in_specs=[fixed(*pieces.shape)],
            out_specs=fixed(size, size),
            scratch_shapes=[pltpu.VMEM((3 * half, half), F32)] + [pltpu.VMEM((size, size), F32)] * 2,
        ),
        out_shape=jax.ShapeDtypeStruct((size, size), F32),
        compiler_params=compiler(60),
        cost_estimate=pl.CostEstimate(
            flops=2 * size * size * 51 * size, bytes_accessed=16 * size * size, transcendentals=0
        ),
        name="polynomials",
    )(core, pieces)


def update_kernel(core, mine, theirs, terms, kept, w_out, new_in, new_out):
    zero = core[0] == 0
    shrink_by = 1.0 - MUON_RATE * DECAY_RATE
    poly_out = split_two(jnp.where(zero, mine[...], theirs[...]))
    new_out[...] = w_out[...] * shrink_by - dot3(poly_out, (terms[0, 2], terms[1, 2])).T
    poly_in = split_two(jnp.where(zero, theirs[...], mine[...]))
    for i in range(2):
        new_in[:, i, :] = kept[i] - dot3(poly_in, (terms[0, i], terms[1, i]))


def update(core, mine, theirs, terms, kept, w_out):
    _, width, shard = kept.shape
    rows = 256 if width % 256 == 0 else width
    tall = pl.BlockSpec((rows, width), lambda i, c: (i, 0))
    fixed = pl.BlockSpec(terms.shape, lambda i, c: (0, 0, 0, 0), pipeline_mode=pl.Buffered(1))
    outer = pl.BlockSpec((shard, rows), lambda i, c: (0, i))
    return pl.pallas_call(
        update_kernel,
        grid_spec=pltpu.PrefetchScalarGridSpec(
            num_scalar_prefetch=1,
            grid=(width // rows,),
            in_specs=[tall, tall, fixed, pl.BlockSpec((2, rows, shard), lambda i, c: (0, i, 0)), outer],
            out_specs=[pl.BlockSpec((rows, 2, shard), lambda i, c: (i, 0, 0)), outer],
        ),
        out_shape=[jax.ShapeDtypeStruct((width, 2, shard), F32), jax.ShapeDtypeStruct(w_out.shape, F32)],
        compiler_params=compiler(60),
        name="update",
    )(core, mine, theirs, terms, kept, w_out)


def adam_update(param_now, grad_now, first_old, second_old):
    first_new = BETA_FIRST * first_old + (1.0 - BETA_FIRST) * grad_now
    second_new = BETA_SECOND * second_old + (1.0 - BETA_SECOND) * grad_now * grad_now
    first_hat = first_new / (1.0 - BETA_FIRST**STEP)
    second_hat = second_new / (1.0 - BETA_SECOND**STEP)
    updated = param_now * (1.0 - ADAM_RATE * DECAY_RATE) - ADAM_RATE * first_hat / (
        jnp.sqrt(second_hat) + 1e-08
    )
    return (second_new, updated)


def core_index():
    return lax.axis_index("dp") % 2


def swap_core(part):
    return lax.ppermute(part, "dp", [(i, i ^ 1) for i in range(lax.axis_size("dp"))])


def exchange_mp(parts):
    return lax.all_to_all(parts, "mp", 0, 0)


def send_z(part, step):
    size = lax.axis_size("dp")
    return lax.ppermute(part, "dp", [(i, i ^ (2 * step)) for i in range(size)])


def after(value, *others):
    return lax.optimization_barrier((value, *others))[0]


def copies(part, count):
    return jnp.broadcast_to(part[None], (count,) + part.shape)


def gather_quick(part):
    ways = lax.axis_size("mp")
    if ways != 4:
        return gather_mp(part), 0
    sent = [lax.ppermute(part, "mp", [(i, i ^ j) for i in range(ways)]) for j in range(1, ways)]
    return jnp.stack([part, *sent]), lax.axis_index("mp")


def gather_mp(part):
    return exchange_mp(copies(part, lax.axis_size("mp")))


def core_rows(rows, core):
    half = rows.shape[0] // 2
    return lax.dynamic_slice_in_dim(rows, core * half, half, 0)


def regroup(pieces, parts):
    ways, rows, columns = pieces.shape
    shard = columns // parts
    if shard % 128 == 0:
        return [(pieces, i * shard) for i in range(parts)]
    split = pieces.reshape(ways, rows, parts, shard).transpose(2, 1, 0, 3)
    return [(split[i].reshape(1, rows, ways * shard), 0) for i in range(parts)]


def plane_sum(parts):
    return jnp.sum(parts.astype(F32), axis=0)


def split_again(half, shard, main, first_row):
    row = lax.broadcasted_iota(jnp.int32, main.shape, 0) + first_row
    column = lax.broadcasted_iota(jnp.int32, main.shape, 1)
    here = (row >= half) & (column < 2 * shard)
    value = main + jnp.concatenate([main[:, shard : 2 * shard], main[:, :shard], main[:, 2 * shard :]], axis=1)
    high = lax.reduce_precision(value, 8, 7)
    return jnp.where(here, jnp.where(column < shard, high, value - high), main)


def depth_sum(main, again):
    depth = lax.axis_size("dp") // 2
    place = lax.axis_index("dp") // 2
    rows, columns = main.shape
    each = rows // depth
    main = again(main, 0)
    low = main.astype(LOW)
    parts = [
        send_z(lax.dynamic_slice_in_dim(low, jnp.bitwise_xor(place, step) * each, each, 0), step)
        for step in range(1, depth)
    ]
    mine = lax.dynamic_slice_in_dim(main, place * each, each, 0)
    mine = mine + sum(p.astype(F32) for p in parts)
    mine = again(mine, place * each)
    mine = mine.astype(LOW)
    parts = [mine] + [send_z(mine, step) for step in range(1, depth)]
    pieces = []
    for piece in range(depth):
        here = parts[piece]
        for other in range(1, depth):
            here = jnp.where(place == other, parts[piece ^ other], here)
        pieces.append(here)
    return jnp.concatenate(pieces, axis=0)


def whole_images(rows, patches, count):
    here, width = rows.shape
    spare = count * patches - here
    if spare:
        odd = lax.axis_index("mp") % 2 == 1
        size = lax.axis_size("mp")
        got = lax.ppermute(rows[:spare], "mp", [(i, i - 1) for i in range(1, size, 2)])
        kept = jnp.concatenate([rows[spare:], jnp.zeros((2 * spare, width), rows.dtype)], axis=0)
        rows = jnp.where(odd, kept, jnp.concatenate([rows, got], axis=0))
    return rows


def held_rows(rows, here):
    spare = rows.shape[0] - here
    if spare:
        odd = lax.axis_index("mp") % 2 == 1
        size = lax.axis_size("mp")
        got = lax.ppermute(rows[here:], "mp", [(i, i + 1) for i in range(0, size, 2)])
        kept = jnp.concatenate([got, rows[: here - spare]], axis=0)
        rows = jnp.where(odd, kept, rows[:here])
    return rows


def per_device(
    tokens,
    cotangent,
    w_in,
    w_out,
    spatial,
    model_vectors,
    gate_vectors,
    patch_bias,
    moment_in,
    moment_out,
    moment_mix,
    first_model,
    second_model,
    first_gate,
    second_gate,
    first_patch,
    second_patch,
):
    here, width = tokens.shape
    shard = w_in.shape[2]
    ways = lax.axis_size("mp")
    full = shard * ways
    patches = spatial.shape[0]
    images = -(-here // patches)
    pad = -(-patches // 16) * 16
    core = core_index()
    core_arg = core.astype(jnp.int32).reshape(1)

    half = width // 2

    gate_wire, rest_wire = weight_wires(core_arg, w_in, w_out, gate_vectors)
    gate_mine, base = gather_quick(gate_wire)
    tokens_rows = whole_images(tokens, patches, images)
    cot_rows = whole_images(cotangent, patches, images)
    normed, unit_in, inv_in, cot_pad, normed_t, cot_t = prep(core_arg, tokens_rows, cot_rows, model_vectors, patches, pad)
    mix = jnp.pad(spatial.astype(LOW), ((0, pad - patches), (0, pad - patches)))
    mix_t = mix.T
    bias = jnp.broadcast_to(jnp.pad(patch_bias, (0, pad - patches))[:, None], (pad, 128))
    rest_mine = exchange_mp(rest_wire)
    gate_mine, mix, mix_t, bias = lax.optimization_barrier((gate_mine, mix, mix_t, bias, normed, rest_wire))[:4]
    gate_theirs = swap_core(gate_mine)
    gate_arg = jnp.stack([core, base]).astype(jnp.int32)

    [(gate_mine, _)], [(gate_theirs, _)] = regroup(gate_mine, 1), regroup(gate_theirs, 1)
    normal, unit, slope, scale, w_gate, vec_all = gate_forward(gate_arg, normed, gate_mine, gate_theirs, images, pad)
    rest_mine = after(rest_mine, normal)
    rest_theirs = swap_core(rest_mine)
    rest_mine, rest_theirs = (
        (parts[0][0] if parts[0][0] is parts[1][0] else jnp.concatenate([p[0] for p in parts], axis=2))
        for parts in (regroup(rest_mine, 2), regroup(rest_theirs, 2))
    )
    gated, low_value, low_gate, mine_one, theirs_one, mine_two, theirs_two, grad_mix, vec_sums = channels_both(
        core_arg, normed, cot_pad, normed_t, cot_t, normal, unit, slope, scale, rest_mine, rest_theirs,
        mix, mix_t, bias, vec_all, images, pad, ways if pad % ways == 0 else 1,
    )
    rides = mix_rides(shard, grad_mix)
    extra = EXTRA if shard % 128 == 0 else 2 * EXTRA
    mix_rows = (grad_mix, swap_core(grad_mix)) if rides else ()
    wire = merge(
        core_arg, mine_one, swap_core(theirs_one), mine_two, swap_core(theirs_two), vec_sums, swap_core(vec_sums), ways, extra, mix_rows
    )
    again = functools.partial(split_again, half, shard)
    output, grad_tokens, model_sums = token_back(
        core_arg, tokens_rows, cot_rows, unit_in, inv_in, gated, low_value, after(low_gate, wire),
        rest_mine, rest_theirs, w_gate, model_vectors, patches, pad,
    )

    old_kept = decayed(core_arg, moment_in, moment_out)
    parts = after(exchange_mp(wire), model_sums, old_kept)
    model_at, model_width = (grad_mix.shape[2], 128) if rides else (0, shard)
    model_rows = 3 * width // model_width
    tail = model_sums[:3].reshape(model_rows, model_width)
    below = (half + MIX_ROW, extra - MIX_ROW - model_rows)
    plane = plane_sum(parts) + jnp.pad(tail, (below, (model_at, 3 * shard - model_at - model_width)))
    main = depth_sum(plane, again)
    main_other, count, wire = gram_wires(core_arg, main, old_kept)
    parts = exchange_mp(wire)
    grad_w_in, new_moment_in, grad_w_out, new_moment_out, terms, kept = moments(
        core_arg, main, main_other, moment_in, moment_out, w_in
    )
    parts = after(parts, kept)
    grams = gather_mp(jnp.sum(parts[:, :count], axis=0))
    extra_rows = extra_rows_of(parts[:, count:], extra, shard)
    extra_rows = jnp.stack([extra_rows, swap_core(extra_rows)])

    vec = main[half : half + MIX_ROW, : 2 * shard].astype(F32)
    grad_vec = vec[:, :shard] + vec[:, shard:]
    tails = extra_rows[:, :, MIX_ROW : MIX_ROW + model_rows, model_at : model_at + model_width]
    tails = jnp.sum(tails, axis=1)
    grad_model = (tails[0] + tails[1]).reshape(3, width)
    if rides:
        each = grad_mix.shape[1] // 2
        rows = extra_rows[:, :, MIX_ROW : MIX_ROW + each, : grad_mix.shape[2]]
        rows = jnp.where(core == 0, rows, rows[::-1])
        grad_mix = jnp.concatenate([rows[0], rows[1]], axis=1)
    else:
        grad_mix = lax.psum(grad_mix, ("dp", "mp"))
    grad_mix = grad_mix.reshape(pad, -1)
    grad_spatial = grad_mix[:patches, :patches]
    grad_patch = grad_mix[:patches, pad]

    new_moment_mix = MOMENTUM * moment_mix + grad_spatial
    new_second_model, new_model = adam_update(model_vectors, grad_model, first_model, second_model)
    new_second_gate, new_gate = adam_update(gate_vectors, grad_vec, first_gate, second_gate)
    new_second_patch, new_patch = adam_update(patch_bias, grad_patch, first_patch, second_patch)
    ortho_mix = square_orthogonal(new_moment_mix)
    poly = polynomials(core_arg, after(grams, ortho_mix, new_model, new_gate, new_patch), full)
    new_w_in, new_w_out = update(core_arg, poly, swap_core(poly), terms, kept, w_out)
    shrink_by = 1.0 - MUON_RATE * DECAY_RATE
    new_spatial = spatial * shrink_by - MUON_RATE * 0.2 * math.sqrt(patches) * ortho_mix
    return (
        held_rows(output, here),
        held_rows(grad_tokens, here),
        grad_w_in,
        grad_w_out,
        grad_spatial,
        grad_model,
        grad_vec,
        grad_patch,
        new_moment_in,
        new_moment_out,
        new_moment_mix,
        new_second_model,
        new_second_gate,
        new_second_patch,
        new_w_in,
        new_w_out,
        new_spatial,
        new_model,
        new_gate,
        new_patch,
    )


def solution(mesh):
    rows = P(("dp", "mp"), None)
    wide = P(None, None, "mp")
    tall = P("mp", None)
    columns = P(None, "mp")
    return jax.shard_map(
        per_device,
        mesh=mesh,
        in_specs=(
            (rows, rows, wide, tall, P(), P(), columns, P())
            + (wide, tall, P(), P(), P(), columns, columns, P(), P())
        ),
        out_specs=(
            (rows, rows, wide, tall, P(), P(), columns, P())
            + (wide, tall, P(), P(), columns, P())
            + (wide, tall, P(), P(), columns, P())
        ),
        check_vma=False,
    )
```
